32 devices in a mesh: snap: 4 (over z), py: 4 (over y, core), pz: 2 (over x).
Axes of the slice: x: 2, y: 2, z: 4, core: 2. Of those that a mesh axis runs over, the one named last changes fastest.
Arguments:
- velocity: bfloat16 [4, 3, 48, 384, 1024], P('snap', None, 'pz', 'py'), may hold values from -6 to 6
- metric_x: float32 [1024], replicated, may hold values from 0.5 to 2
- metric_y: float32 [384], replicated, may hold values from 0.3 to 3
- metric_z: float32 [48], replicated, may hold values from 0.5 to 2
- sketch_matrix: float32 [4, 4], replicated, may hold values from -3 to 3
Outputs:
- sketch: float32 [4, 3, 48, 384, 1024], P(None, None, None, ('snap', 'pz'), 'py')
The draws below stay inside these ranges and needn't reach their ends.
All inputs are finite; a program needn't handle non-finite values.
Results may differ from the reference program's by a relative error of at most 0.0065.
Values may be sent and summed in bfloat16 or wider, within the bound.
No kernel may reach another device: no remote copies, remote signals or barrier semaphores. Data moves between devices by JAX's collectives and lax.ppermute only.
A program may use at most 192 MiB of HBM per device.

```python
import math
import jax
import jax.numpy as jnp
from jax import lax

NX = 1024
NY = 384
NZ = 48
RANK = 4
SNAPS = 4
ZBLOCK = 24
YBLOCK = 96


def draw_velocity(key, part):
    phase_key = jax.random.fold_in(key, 11)
    jitter_key = jax.random.fold_in(key, 12)
    value_key = jax.random.fold_in(key, 13)
    zblocks = NZ // ZBLOCK
    yblocks = NY // YBLOCK
    phase = jax.random.randint(phase_key, (), 0, 2)
    zindex = jnp.arange(NZ, dtype=jnp.int32) // ZBLOCK
    yindex = jnp.arange(NY, dtype=jnp.int32) // YBLOCK
    parity = (zindex[:, None] + yindex[None, :] + phase) % 2
    jitter = jax.random.uniform(jitter_key, (zblocks, yblocks), jnp.float32, -0.3, 0.0)
    jitter = jnp.repeat(jnp.repeat(jitter, ZBLOCK, axis=0), YBLOCK, axis=1)
    quiet_level = -3.9
    values = jax.random.truncated_normal(value_key, -6.0, 6.0, (SNAPS, 3, NZ, NY, NX), jnp.float32)
    log_level = jnp.where(parity == 1, 0.0, quiet_level) + jitter
    loudness = jnp.exp(log_level)[None, None, :, :, None]
    return (values * loudness).astype(jnp.bfloat16)


def centred(stream_key, shape, spread, bound, kind=jnp.bfloat16):
    return jnp.clip(spread * jax.random.normal(stream_key, shape, jnp.float32), -bound, bound).astype(kind)


def setup_inputs(seed: int = 0) -> dict:
    splits = jax.random.split(jax.random.key(seed), 6)
    velocity = draw_velocity(jax.random.fold_in(splits[5], 71), 0)
    metric_x = jnp.clip(jnp.exp(jax.random.uniform(splits[1], (NX,), jnp.float32, math.log(0.5), math.log(2.0))), 0.5, 2.0)
    metric_y = jnp.clip(jnp.exp(jax.random.uniform(splits[2], (NY,), jnp.float32, math.log(0.3), math.log(3.0))), 0.3, 3.0)
    metric_z = jnp.clip(jnp.exp(jax.random.uniform(splits[3], (NZ,), jnp.float32, math.log(0.5), math.log(2.0))), 0.5, 2.0)
    sketch_matrix = centred(splits[4], (SNAPS, RANK), SNAPS ** -0.5, 3.0, jnp.float32)
    return dict(velocity=velocity, metric_x=metric_x, metric_y=metric_y, metric_z=metric_z, sketch_matrix=sketch_matrix)


def line_derivative(field, axis):
    moved = jnp.moveaxis(field, axis, 0)
    points = moved.shape[0]
    flattened = moved.reshape(points, -1)
    padded = jnp.pad(flattened, ((2, 2), (0, 0)))
    right_side = 7.0 / 9.0 * (padded[3:points + 3] - padded[1:points + 1]) + 1.0 / 36.0 * (padded[4:points + 4] - padded[0:points])
    lower_band = jnp.full((points,), 1.0 / 3.0, right_side.dtype).at[0].set(0.0)
    upper_band = jnp.full((points,), 1.0 / 3.0, right_side.dtype).at[points - 1].set(0.0)
    main_band = jnp.ones((points,), right_side.dtype)
    solved = lax.linalg.tridiagonal_solve(lower_band, main_band, upper_band, right_side)
    return jnp.moveaxis(solved.reshape(moved.shape), 0, axis)

def reference(velocity, metric_x, metric_y, metric_z, sketch_matrix):
    scale_x = metric_x[None, None, :]
    scale_y = metric_y[None, :, None]
    scale_z = metric_z[:, None, None]

    def one_snapshot(total, inputs):
        snapshot, weights = inputs
        vel_u = snapshot[0].astype(jnp.float32)
        vel_v = snapshot[1].astype(jnp.float32)
        vel_w = snapshot[2].astype(jnp.float32)
        slope_vx = (scale_x * line_derivative(vel_v, 2)).astype(jnp.bfloat16)
        slope_wx = (scale_x * line_derivative(vel_w, 2)).astype(jnp.bfloat16)
        slope_uy = scale_y * line_derivative(vel_u, 1)
        slope_wy = (scale_y * line_derivative(vel_w, 1)).astype(jnp.bfloat16)
        spin_z = (slope_vx.astype(jnp.float32) - slope_uy).astype(jnp.bfloat16)
        slope_uz = scale_z * line_derivative(vel_u, 0)
        slope_vz = scale_z * line_derivative(vel_v, 0)
        spin_x = (slope_wy.astype(jnp.float32) - slope_vz).astype(jnp.bfloat16)
        spin_y = (slope_uz - slope_wx.astype(jnp.float32)).astype(jnp.bfloat16)
        vorticity = jnp.stack([spin_x, spin_y, spin_z], axis=0).astype(jnp.float32)
        term = weights.astype(jnp.float32)[:, None, None, None, None] * vorticity[None]
        return (total + term, None)
    start = jnp.zeros((RANK, 3, NZ, NY, NX), jnp.float32)
    total, unused = lax.scan(one_snapshot, start, (velocity, sketch_matrix))
    return total
```

```python
import functools

import jax
import jax.numpy as jnp
import ml_dtypes
import numpy as np
from jax import lax
from jax.experimental import pallas as pl
from jax.experimental.pallas import tpu as pltpu
from jax.sharding import PartitionSpec as P

ratio = (3.0 - 5.0**0.5) / 2.0
VMEM_LIMIT = 52 * 1024 * 1024
f32 = jnp.float32
bf16 = jnp.bfloat16


def lead(i):
    return 1.0 - ratio ** (2.0 * (np.asarray(i, np.float64) + 1.0))


def trail(i, n):
    return 1.0 - ratio ** (2.0 * (n - np.asarray(i, np.float64)))


def denom(n):
    return 5.0**0.5 / 3.0 * (1.0 - ratio ** (2.0 * (n + 1.0)))


def inverse_entry(row, col, n):
    inside = (col >= 0) & (col < n)
    col = np.clip(col, 0, n - 1)
    near, far = np.minimum(row, col), np.maximum(row, col)
    sign = 1.0 - 2.0 * ((far - near) % 2)
    value = sign * ratio ** (far - near).astype(np.float64) * lead(near) * trail(far, n) / denom(n)
    return np.where(inside, value, 0.0)


def line_table(n, start, size):
    row = start + np.arange(size)[:, None]
    col = start + np.arange(size)[None, :]
    entry = functools.partial(inverse_entry, row, n=n)
    first = entry(col - 1) - entry(col + 1)
    second = entry(col - 2) - entry(col + 2)
    return 7.0 / 9.0 * first + 1.0 / 36.0 * second


def split_table(table):
    high = table.astype(ml_dtypes.bfloat16)
    low = (table - high.astype(np.float64)).astype(ml_dtypes.bfloat16)
    return high, low


def edge_weights(n, start, size):
    last = start + size - 1
    j = start + np.arange(size)

    def forward(k):
        return np.where(k >= 0, (-ratio) ** (last - k).astype(np.float64) * lead(k), 0.0)

    def backward(k):
        return np.where(k <= n - 1, (-ratio) ** (k - start).astype(np.float64) * trail(k, n), 0.0)

    def weights(c):
        return 7.0 / 9.0 * (c(j - 1) - c(j + 1)) + 1.0 / 36.0 * (c(j - 2) - c(j + 2))

    return weights(forward), weights(backward)


def edge_columns(n, start, size):
    i = start + np.arange(size)
    left = (-ratio) ** (i - start + 1.0) * trail(i, n) / denom(n)
    right = (-ratio) ** (start + size - i).astype(np.float64) * lead(i) / denom(n)
    corner_left, corner_right = np.zeros(size), np.zeros(size)
    corner_left[0], corner_right[-1] = -1.0 / 12.0, 1.0 / 12.0
    return np.stack([left, right, corner_left, corner_right], axis=1)


def sweep_scalars(n, start, size):
    i = start + np.arange(size)
    after = start + size
    own_left = [0.0, 0.0]
    own_right = [0.0, 0.0]
    if start > 0:
        own_left = [7.0 / 9.0 * lead(start - 1) - ratio / 36.0 * lead(start - 2), lead(start - 1) / 36.0]
    if after < n:
        own_right = [
            -7.0 / 9.0 * trail(after, n) + ratio / 36.0 * trail(after + 1, n),
            -trail(after, n) / 36.0,
        ]
    rows = [lead(i), trail(i, n), lead(i) / denom(n), trail(i, n) / denom(n)]
    return np.concatenate(rows + [np.array(own_left + own_right)])


def per_block(make, n, count):
    size = n // count
    return np.stack([make(n, block * size, size) for block in range(count)])


def largest_divisor(size, most):
    return max(d for d in range(1, most + 1) if size % d == 0)


def edge_y_kernel(info, weights, u_ref, w_ref, right_ref, left_ref):
    for field, ref in enumerate((u_ref, w_ref)):
        for z in range(ref.shape[1]):
            values = ref[0, z].astype(f32)
            right_ref[field, 0, z, :] = jnp.sum(values * weights[0, :, 0:1], axis=0)
            left_ref[field, 0, z, :] = jnp.sum(values * weights[0, :, 1:2], axis=0)
            right_ref[field, 1, z, :] = values[-1]
            left_ref[field, 1, z, :] = values[0]


def edge_y(info, velocity, weights, chunk):
    _, zb, yb, nx = velocity.shape
    chunk = largest_divisor(zb, 8) if zb % 8 == 0 else zb
    piece = lambda f: pl.BlockSpec((1, chunk, yb, nx), lambda i, info: (f, i, 0, 0))
    out = pl.BlockSpec((2, 2, chunk, nx), lambda i, info: (0, 0, i, 0))
    shape = jax.ShapeDtypeStruct((2, 2, zb, nx), f32)
    return pl.pallas_call(
        edge_y_kernel,
        grid_spec=pltpu.PrefetchScalarGridSpec(
            num_scalar_prefetch=1,
            grid=(zb // chunk,),
            in_specs=[pl.BlockSpec((1, yb, 2), lambda i, info: (info[0], 0, 0)), piece(0), piece(2)],
            out_specs=[out, out],
        ),
        out_shape=[shape, shape],
        compiler_params=pltpu.CompilerParams(vmem_limit_bytes=VMEM_LIMIT),
        cost_estimate=pl.CostEstimate(
            flops=8 * zb * yb * nx, bytes_accessed=4 * zb * yb * nx, transcendentals=0
        ),
        name="edge_y",
    )(info, weights, velocity, velocity)


def edge_z_kernel(info, weights, u_ref, v_ref, right_ref, left_ref):
    zb = u_ref.shape[1]
    for field, ref in enumerate((u_ref, v_ref)):
        values = ref[0, 0].astype(f32)
        right = values * weights[info[1], 0]
        left = values * weights[info[1], zb]
        left_ref[field, 1] = values
        for z in range(1, zb):
            values = ref[0, z].astype(f32)
            right = right + values * weights[info[1], z]
            left = left + values * weights[info[1], zb + z]
        right_ref[field, 1] = values
        right_ref[field, 0] = right
        left_ref[field, 0] = left


def edge_z(info, velocity, weights):
    _, zb, yb, nx = velocity.shape
    rows = 16
    piece = lambda f: pl.BlockSpec((1, zb, rows, nx), lambda i, info: (f, 0, i, 0))
    out = pl.BlockSpec((2, 2, rows, nx), lambda i, info: (0, 0, i, 0))
    shape = jax.ShapeDtypeStruct((2, 2, yb, nx), f32)
    return pl.pallas_call(
        edge_z_kernel,
        grid_spec=pltpu.PrefetchScalarGridSpec(
            num_scalar_prefetch=1,
            grid=(yb // rows,),
            in_specs=[pl.BlockSpec(memory_space=pltpu.SMEM), piece(0), piece(1)],
            out_specs=[out, out],
        ),
        out_shape=[shape, shape],
        compiler_params=pltpu.CompilerParams(vmem_limit_bytes=VMEM_LIMIT),
        cost_estimate=pl.CostEstimate(
            flops=8 * zb * yb * nx, bytes_accessed=4 * zb * yb * nx, transcendentals=0
        ),
        name="edge_z",
    )(info, weights, velocity, velocity)


def from_neighbours(right, left, axis, size):
    count = lax.axis_size(axis)

    def shifted(x, step):
        pairs = [(i, i + step) for i in range(count) if 0 <= i + step < count]
        return lax.ppermute(x, axis, pairs)

    out = []
    for sent, way in ((right, 1), (left, -1)):
        got = shifted(sent, way)
        total = got[:, 0]
        for far in range(2, count):
            more = shifted(sent[:, 0].astype(bf16), way * far).astype(f32)
            total = total + more * f32((-ratio) ** (size * (far - 1)))
        out.append(got if count <= 2 else jnp.stack([total, got[:, 1]], axis=1))
    return out


def slope_along_x(ref, tables, metric):
    chunk, yb, nx = ref.shape[1:]
    field = ref[0].reshape(chunk * yb, nx)
    high, low = tables
    slope = jnp.dot(field, high[...], preferred_element_type=f32)
    slope = slope + jnp.dot(field, low[...], preferred_element_type=f32)
    return (slope * metric[...]).reshape(chunk, yb, nx)


def slope_along_y(ref, z, table, columns, left, right, metric):
    yb = ref.shape[2]
    both = jnp.dot(table[0], ref[0, z], preferred_element_type=f32)
    slope = both[:yb] + both[yb:]
    slope = slope + columns[0, :, 0:1] * left[0, 0, z : z + 1, :]
    slope = slope + columns[0, :, 1:2] * right[0, 0, z : z + 1, :]
    slope = slope + columns[0, :, 2:3] * left[0, 1, z : z + 1, :]
    slope = slope + columns[0, :, 3:4] * right[0, 1, z : z + 1, :]
    return slope * metric[...]


def slopes_along_z(info, ref, scalars, left, right, metric, out):
    _, zb, yb, nx = ref.shape
    rows, lanes = 16, 128
    across = nx // lanes
    block = info[1]

    def tile(t, carry):
        ys = pl.ds(pl.multiple_of((t // across) * rows, rows), rows)
        xs = pl.ds(pl.multiple_of((t % across) * lanes, lanes), lanes)
        f = [ref[0, z, ys, xs].astype(f32) for z in range(zb)]
        scalar = lambda k: scalars[block, k]

        def rhs(z):
            total = None
            for step, weight in ((1, 7.0 / 9.0), (2, 1.0 / 36.0)):
                if z + step < zb and z - step >= 0:
                    term = (f[z + step] - f[z - step]) * weight
                elif z + step < zb:
                    term = f[z + step] * weight
                else:
                    term = f[z - step] * -weight
                total = term if total is None else total + term
            return total

        run = left[0, 0, ys, xs] + f[0] * scalar(4 * zb) + f[1] * scalar(4 * zb + 1)
        forward = []
        for z in range(zb):
            run = run * -ratio + rhs(z) * scalar(z)
            forward.append(run)
        run = right[0, 0, ys, xs] + f[zb - 1] * scalar(4 * zb + 2) + f[zb - 2] * scalar(4 * zb + 3)
        for z in reversed(range(zb)):
            run = run * -ratio
            slope = forward[z] * scalar(3 * zb + z) + run * scalar(2 * zb + z)
            run = run + rhs(z) * scalar(zb + z)
            if z == 0:
                slope = slope - left[0, 1, ys, xs] * (1.0 / 12.0)
            if z == zb - 1:
                slope = slope + right[0, 1, ys, xs] * (1.0 / 12.0)
            out[z, ys, xs] = slope * metric[block * zb + z]
        return carry

    lax.fori_loop(0, (yb // rows) * across, tile, 0)


def hand_out(info, spin, outs):
    if len(outs) == 1:
        outs[0][...] = spin[...]
        return
    count = len(outs)
    rows, lanes = outs[0].shape[1:]
    for q, out in enumerate(outs):
        ys = pl.ds(pl.multiple_of(info[2 + q] * rows, rows), rows)
        xs = pl.ds(pl.multiple_of(info[2 + count + q] * lanes, lanes), lanes)
        out[...] = spin[:, ys, xs]


def spin_z_kernel(info, v_ref, high, low, metric_x, u_ref, table, columns, left, right, metric_y, *rest):
    outs, spin = rest[:-1], rest[-1]
    slope_vx = slope_along_x(v_ref, (high, low), metric_x).astype(bf16)
    for z in range(u_ref.shape[1]):
        slope_uy = slope_along_y(u_ref, z, table, columns, left, right, metric_y)
        spin[z] = (slope_vx[z].astype(f32) - slope_uy).astype(bf16)
    hand_out(info, spin, outs)


def spin_y_kernel(info, w_ref, high, low, metric_x, u_ref, scalars, left, right, metric_z, *rest):
    outs, spin, slopes = rest[:-2], rest[-2], rest[-1]
    step = pl.program_id(0)
    chunk = w_ref.shape[1]

    @pl.when(step == 0)
    def _():
        slopes_along_z(info, u_ref, scalars, left, right, metric_z, slopes)

    slope_wx = slope_along_x(w_ref, (high, low), metric_x).astype(bf16)
    for z in range(chunk):
        spin[z] = (slopes[step * chunk + z] - slope_wx[z].astype(f32)).astype(bf16)
    hand_out(info, spin, outs)


def spin_x_kernel(
    info, w_ref, table, columns, y_left, y_right, metric_y, v_ref, scalars, left, right, metric_z, *rest
):
    outs, spin, slopes = rest[:-2], rest[-2], rest[-1]
    step = pl.program_id(0)
    chunk = w_ref.shape[1]

    @pl.when(step == 0)
    def _():
        slopes_along_z(info, v_ref, scalars, left, right, metric_z, slopes)

    for z in range(chunk):
        slope_wy = slope_along_y(w_ref, z, table, columns, y_left, y_right, metric_y).astype(bf16)
        spin[z] = (slope_wy.astype(f32) - slopes[step * chunk + z]).astype(bf16)
    hand_out(info, spin, outs)


def spin_call(kernel, info, velocity, groups, splits, flops, name):
    _, zb, yb, nx = velocity.shape
    row_parts, col_parts = splits
    chunk = largest_divisor(zb, 4)
    specs, args, scratch = [], [], [pltpu.VMEM((chunk, yb, nx), bf16)]
    whole = lambda a: pl.BlockSpec(a.shape, lambda i, info: (0,) * a.ndim)
    mine = lambda a: pl.BlockSpec((1,) + a.shape[1:], lambda i, info: (info[0],) + (0,) * (a.ndim - 1))
    smem = pl.BlockSpec(memory_space=pltpu.SMEM)

    def add(spec, arg):
        specs.append(spec)
        args.append(arg)

    for kind, field, *more in groups:
        if kind == "z":
            scalars, (place, left, right), metric = more
            edge = pl.BlockSpec((1, 2, yb, nx), lambda i, info, place=place: (place, 0, 0, 0))
            add(pl.BlockSpec((1, zb, yb, nx), lambda i, info, field=field: (field, 0, 0, 0)), velocity)
            add(smem, scalars)
            add(edge, left)
            add(edge, right)
            add(smem, metric)
            scratch.append(pltpu.VMEM((zb, yb, nx), f32))
            continue
        add(pl.BlockSpec((1, chunk, yb, nx), lambda i, info, field=field: (field, i, 0, 0)), velocity)
        if kind == "x":
            (high, low), metric = more
            add(whole(high), high)
            add(whole(low), low)
            add(whole(metric), metric)
        else:
            table, columns, (place, left, right), metric = more
            edge = pl.BlockSpec(
                (1, 2, None, chunk, nx), lambda i, info, place=place: (place, 0, i, 0, 0)
            )
            cut = lambda a: a.reshape(a.shape[0], 2, zb // chunk, chunk, nx)
            add(mine(table), table)
            add(mine(columns), columns)
            add(edge, cut(left))
            add(edge, cut(right))
            add(pl.BlockSpec((yb, 1), lambda i, info: (info[0], 0)), metric)

    count = row_parts * col_parts
    block = (yb // row_parts, nx // col_parts)
    return pl.pallas_call(
        kernel,
        grid_spec=pltpu.PrefetchScalarGridSpec(
            num_scalar_prefetch=1,
            grid=(zb // chunk,),
            in_specs=specs,
            out_specs=[pl.BlockSpec((chunk,) + block, lambda i, info: (i, 0, 0))] * count,
            scratch_shapes=scratch,
        ),
        out_shape=[jax.ShapeDtypeStruct((zb,) + block, bf16)] * count,
        compiler_params=pltpu.CompilerParams(vmem_limit_bytes=VMEM_LIMIT),
        cost_estimate=pl.CostEstimate(
            flops=flops, bytes_accessed=8 * zb * yb * nx, transcendentals=0
        ),
        name=name,
    )(info, *args)


def sketch_kernel(info, weights, *rest, aliased):
    count = weights.shape[0]
    fields = rest[:count]
    out = rest[-1]
    values = [field[...].astype(f32) for field in fields]
    for k in range(out.shape[0]):
        total = values[0] * weights[info[1], k]
        for r in range(1, count):
            total = total + values[r] * weights[info[1 + r], k]
        out[k, 0] = total


def sketch_part(info, sketch_matrix, fields, total, component, shape):
    zb, rows, lanes = fields[0].shape
    rank = sketch_matrix.shape[1]
    chunk = largest_divisor(zb, 8)
    steps = zb // chunk
    piece = pl.BlockSpec((chunk, rows, lanes), lambda i, info: (i, 0, 0))
    specs = [pl.BlockSpec(memory_space=pltpu.SMEM)] + [piece] * len(fields)
    args = [sketch_matrix, *fields]
    aliases = {}
    if total is not None:
        specs.append(pl.BlockSpec(memory_space=pl.ANY))
        args.append(total)
        aliases = {len(args): 0}
    return pl.pallas_call(
        functools.partial(sketch_kernel, aliased=total is not None),
        grid_spec=pltpu.PrefetchScalarGridSpec(
            num_scalar_prefetch=1,
            grid=(steps,),
            in_specs=specs,
            out_specs=pl.BlockSpec(
                (rank, 1, chunk, rows, lanes),
                lambda i, info: (0, component, info[0] * steps + i, 0, 0),
            ),
        ),
        out_shape=jax.ShapeDtypeStruct(shape, f32),
        input_output_aliases=aliases,
        compiler_params=pltpu.CompilerParams(vmem_limit_bytes=VMEM_LIMIT),
        cost_estimate=pl.CostEstimate(
            flops=2 * rank * len(fields) * zb * rows * lanes,
            bytes_accessed=(2 * len(fields) + 4 * rank) * zb * rows * lanes,
            transcendentals=0,
        ),
        name="sketch_part",
    )(info, *args)


def col_rank(c, count):
    return (c % 2) * (count // 2) + c // 2 if count % 2 == 0 else c


def col_of_rank(t, count):
    return (t % (count // 2)) * 2 + t // (count // 2) if count % 2 == 0 else t


def routes(snaps, cols, depth):
    out = []
    for shift in range(depth):
        for turn in range(cols):
            pairs = []
            for s in range(snaps):
                for p in range(cols):
                    for z in range(depth):
                        c = col_of_rank((p - turn - s) % cols, cols)
                        to = (p * cols + c) * depth + (z + shift) % depth
                        pairs.append(((s * cols + p) * depth + z, to))
            out.append(pairs)
    return out


def general_way(vorticity, sketch_matrix):
    lines = lax.all_to_all(vorticity, "py", split_axis=4, concat_axis=3, tiled=True)
    snap_count = lax.axis_size("snap")
    pz_count = lax.axis_size("pz")
    shape_now = lines.shape
    block_rows = shape_now[3] // (snap_count * pz_count)
    split_rows = lines.reshape(shape_now[:3] + (snap_count, pz_count, block_rows, shape_now[4]))
    reordered = jnp.swapaxes(split_rows, 3, 4).reshape(shape_now)
    lines = lax.all_to_all(reordered, "pz", split_axis=3, concat_axis=2, tiled=True)
    lines = lax.all_to_all(lines, "snap", split_axis=3, concat_axis=0, tiled=True)
    return jnp.einsum(
        "sk,sczyx->kczyx", sketch_matrix, lines.astype(f32), precision=lax.Precision.HIGHEST
    )


def on_device(velocity, metric_x, metric_y, metric_z, sketch_matrix):
    snaps, cols, depth = (lax.axis_size(name) for name in ("snap", "py", "pz"))
    s, p, z = (lax.axis_index(name) for name in ("snap", "py", "pz"))
    _, _, zb, yb, nx = velocity.shape
    ny, nz = yb * cols, zb * depth
    velocity = velocity[0]
    direct = snaps == cols
    messages = [(shift, turn) for shift in range(depth) for turn in range(cols)]

    tables_x = [jnp.asarray(t) for t in split_table(line_table(nx, 0, nx).T)]
    tables_y = per_block(line_table, ny, cols)
    tables_y = jnp.asarray(np.concatenate(split_table(tables_y), axis=1))
    columns_y = jnp.asarray(per_block(edge_columns, ny, cols), f32)
    weights_y = per_block(lambda *a: np.stack(edge_weights(*a), axis=1), ny, cols)
    weights_z = per_block(lambda *a: np.concatenate(edge_weights(*a)), nz, depth)
    scalars_z = jnp.asarray(per_block(sweep_scalars, nz, depth), f32)
    metric_x = metric_x.reshape(1, nx)
    metric_y = metric_y.reshape(ny, 1)

    where = [p, z]
    if direct:
        where += [(z + shift) % depth for shift, turn in messages]
        where += [col_of_rank((p - turn - s) % cols, cols) for shift, turn in messages]
    info = jnp.stack(where).astype(jnp.int32)
    splits = (depth, cols) if direct else (1, 1)

    y_edges = edge_y(info, velocity, jnp.asarray(weights_y, f32), 4)
    y_left, y_right = from_neighbours(*y_edges, "py", yb)
    z_edges = edge_z(info, velocity, jnp.asarray(weights_z, f32))
    z_left, z_right = from_neighbours(*z_edges, "pz", zb)

    points = zb * yb * nx
    along_x = lambda field: ("x", field, tables_x, metric_x)
    along_y = lambda field, place: (
        "y", field, tables_y, columns_y, (place, y_left, y_right), metric_y
    )
    along_z = lambda field: ("z", field, scalars_z, (field, z_left, z_right), metric_z)
    spins = {}
    spins[2] = spin_call(
        spin_z_kernel, info, velocity, [along_x(1), along_y(0, 0)], splits,
        points * 4 * (nx + yb), "spin_z",
    )
    spins[1] = spin_call(
        spin_y_kernel, info, velocity, [along_x(2), along_z(0)], splits,
        points * (4 * nx + 20), "spin_y",
    )
    spins[0] = spin_call(
        spin_x_kernel, info, velocity, [along_y(2, 1), along_z(1)], splits,
        points * (4 * yb + 20), "spin_x",
    )
    if not direct:
        vorticity = jnp.stack([spins[c][0] for c in range(3)])[None]
        return general_way(vorticity, sketch_matrix)

    all_routes = routes(snaps, cols, depth)
    shape = (sketch_matrix.shape[1], 3, nz, yb // depth, nx // cols)
    my_rank = col_rank(p, cols)
    total = None
    for component in (2, 1, 0):
        got = [
            lax.ppermute(part, ("snap", "py", "pz"), pairs)
            for part, pairs in zip(spins[component], all_routes)
        ]
        for shift in range(depth):
            whence = [(z - shift) % depth]
            whence += [(s - turn - my_rank) % snaps for turn in range(cols)]
            total = sketch_part(
                jnp.stack(whence).astype(jnp.int32),
                sketch_matrix,
                got[shift * cols : (shift + 1) * cols],
                total,
                component,
                shape,
            )
    return total


def solution(mesh):
    placed = (P("snap", None, "pz", "py", None), P(), P(), P(), P())
    return jax.shard_map(
        on_device,
        mesh=mesh,
        in_specs=placed,
        out_specs=P(None, None, None, ("snap", "pz"), "py"),
        check_vma=False,
    )
```

```python
import functools

import jax
import jax.numpy as jnp
import ml_dtypes
import numpy as np
from jax import lax
from jax.experimental import pallas as pl
from jax.experimental.pallas import tpu as pltpu
from jax.sharding import PartitionSpec as P

ratio = (3.0 - 5.0**0.5) / 2.0
VMEM_LIMIT = 52 * 1024 * 1024
f32 = jnp.float32
bf16 = jnp.bfloat16


def lead(i):
    return 1.0 - ratio ** (2.0 * (np.asarray(i, np.float64) + 1.0))


def trail(i, n):
    return 1.0 - ratio ** (2.0 * (n - np.asarray(i, np.float64)))


def denom(n):
    return 5.0**0.5 / 3.0 * (1.0 - ratio ** (2.0 * (n + 1.0)))


def inverse_entry(row, col, n):
    inside = (col >= 0) & (col < n)
    col = np.clip(col, 0, n - 1)
    near, far = np.minimum(row, col), np.maximum(row, col)
    sign = 1.0 - 2.0 * ((far - near) % 2)
    value = sign * ratio ** (far - near).astype(np.float64) * lead(near) * trail(far, n) / denom(n)
    return np.where(inside, value, 0.0)


def line_table(n, start, size):
    row = start + np.arange(size)[:, None]
    col = start + np.arange(size)[None, :]
    entry = functools.partial(inverse_entry, row, n=n)
    first = entry(col - 1) - entry(col + 1)
    second = entry(col - 2) - entry(col + 2)
    return 7.0 / 9.0 * first + 1.0 / 36.0 * second


def split_table(table):
    high = table.astype(ml_dtypes.bfloat16)
    low = (table - high.astype(np.float64)).astype(ml_dtypes.bfloat16)
    return high, low


def edge_weights(n, start, size):
    last = start + size - 1
    j = start + np.arange(size)

    def forward(k):
        return np.where(k >= 0, (-ratio) ** (last - k).astype(np.float64) * lead(k), 0.0)

    def backward(k):
        return np.where(k <= n - 1, (-ratio) ** (k - start).astype(np.float64) * trail(k, n), 0.0)

    def weights(c):
        return 7.0 / 9.0 * (c(j - 1) - c(j + 1)) + 1.0 / 36.0 * (c(j - 2) - c(j + 2))

    return weights(forward), weights(backward)


def edge_columns(n, start, size):
    i = start + np.arange(size)
    left = (-ratio) ** (i - start + 1.0) * trail(i, n) / denom(n)
    right = (-ratio) ** (start + size - i).astype(np.float64) * lead(i) / denom(n)
    return left, right


def message_weights(n, start, size):
    count, block = n // size, start // size
    right, left = edge_weights(n, start, size)
    return np.stack([right if block < count - k else left for k in range(1, count)])


def message_shares(n, start, size):
    count, block = n // size, start // size
    decay = (-ratio) ** size
    left = [decay ** (k - 1) if block >= k else 0.0 for k in range(1, count)]
    right = [decay ** (count - k - 1) if block < k else 0.0 for k in range(1, count)]
    corner = [-1.0 / 12.0 if block > 0 else 0.0, 1.0 / 12.0 if block < count - 1 else 0.0]
    return np.array(left), np.array(right), np.array(corner)


def message_columns(n, start, size):
    left, right = edge_columns(n, start, size)
    share_left, share_right, corner = message_shares(n, start, size)
    corners = np.zeros((size, 2))
    corners[0, 0], corners[-1, 1] = corner
    return np.concatenate([np.outer(left, share_left) + np.outer(right, share_right), corners], axis=1)


def sweep_scalars(n, start, size):
    i = start + np.arange(size)
    after = start + size
    own_left = [0.0, 0.0]
    own_right = [0.0, 0.0]
    if start > 0:
        own_left = [7.0 / 9.0 * lead(start - 1) - ratio / 36.0 * lead(start - 2), lead(start - 1) / 36.0]
    if after < n:
        own_right = [
            -7.0 / 9.0 * trail(after, n) + ratio / 36.0 * trail(after + 1, n),
            -trail(after, n) / 36.0,
        ]
    rows = [lead(i), trail(i, n), lead(i) / denom(n), trail(i, n) / denom(n)]
    share_left, share_right, corner = message_shares(n, start, size)
    return np.concatenate(rows + [np.array(own_left + own_right), corner, share_left, share_right])


def per_block(make, n, count):
    size = n // count
    return np.stack([make(n, block * size, size) for block in range(count)])


def largest_divisor(size, most):
    return max(d for d in range(1, most + 1) if size % d == 0)


def message_forms(count):
    return [k in (1, count - 1) for k in range(1, count)]


def edge_y_kernel(info, weights, ref, *outs):
    count = len(outs) + 1
    for z in range(ref.shape[1]):
        values = ref[0, z].astype(f32)
        for k, out in enumerate(outs, 1):
            out[0, z, :] = jnp.sum(values * weights[0, :, k - 1 : k], axis=0).astype(out.dtype)
            if out.shape[0] == 2:
                out[1, z, :] = jnp.where(info[0] < count - k, values[-1], values[0])


def edge_y(info, velocity, field, weights):
    _, zb, yb, nx = velocity.shape
    count = weights.shape[0]
    chunk = 8 if zb % 8 == 0 else zb
    forms = message_forms(count)
    return pl.pallas_call(
        edge_y_kernel,
        grid_spec=pltpu.PrefetchScalarGridSpec(
            num_scalar_prefetch=1,
            grid=(zb // chunk,),
            in_specs=[
                pl.BlockSpec((1, yb, count - 1), lambda i, info: (info[0], 0, 0)),
                pl.BlockSpec((1, chunk, yb, nx), lambda i, info: (field, i, 0, 0)),
            ],
            out_specs=[pl.BlockSpec((1 + near, chunk, nx), lambda i, info: (0, i, 0)) for near in forms],
        ),
        out_shape=[jax.ShapeDtypeStruct((1 + near, zb, nx), f32) for near in forms],
        compiler_params=pltpu.CompilerParams(vmem_limit_bytes=VMEM_LIMIT),
        cost_estimate=pl.CostEstimate(
            flops=6 * zb * yb * nx, bytes_accessed=2 * zb * yb * nx, transcendentals=0
        ),
        name="edge_y",
    )(info, weights, velocity)


def edge_z_kernel(info, weights, u_ref, v_ref, *outs):
    zb = u_ref.shape[1]
    count = len(outs) + 1
    for field, ref in enumerate((u_ref, v_ref)):
        for k, out in enumerate(outs, 1):
            first = ref[0, 0].astype(f32)
            total = first * weights[info[1], (k - 1) * zb]
            for z in range(1, zb):
                values = ref[0, z].astype(f32)
                total = total + values * weights[info[1], (k - 1) * zb + z]
            out[field, 0] = total
            if out.shape[1] == 2:
                out[field, 1] = jnp.where(info[1] < count - k, values, first)


def edge_z(info, velocity, weights):
    _, zb, yb, nx = velocity.shape
    rows = 16
    forms = message_forms(weights.shape[0])
    piece = lambda f: pl.BlockSpec((1, zb, rows, nx), lambda i, info: (f, 0, i, 0))
    return pl.pallas_call(
        edge_z_kernel,
        grid_spec=pltpu.PrefetchScalarGridSpec(
            num_scalar_prefetch=1,
            grid=(yb // rows,),
            in_specs=[pl.BlockSpec(memory_space=pltpu.SMEM), piece(0), piece(1)],
            out_specs=[
                pl.BlockSpec((2, 1 + near, rows, nx), lambda i, info: (0, 0, i, 0)) for near in forms
            ],
        ),
        out_shape=[jax.ShapeDtypeStruct((2, 1 + near, yb, nx), f32) for near in forms],
        compiler_params=pltpu.CompilerParams(vmem_limit_bytes=VMEM_LIMIT),
        cost_estimate=pl.CostEstimate(
            flops=6 * zb * yb * nx, bytes_accessed=4 * zb * yb * nx, transcendentals=0
        ),
        name="edge_z",
    )(info, weights, velocity, velocity)


def exchange(messages, axis):
    count = lax.axis_size(axis)
    out = []
    for k, message in enumerate(messages, 1):
        pairs = [(i, (i + k) % count) for i in range(count)]
        out.append(lax.ppermute(message, axis, pairs))
    return out


def slope_along_x(ref, tables, metric):
    chunk, yb, nx = ref.shape[1:]
    field = ref[0].reshape(chunk * yb, nx)
    high, low = tables
    slope = jnp.dot(field, high[...], preferred_element_type=f32)
    slope = slope + jnp.dot(field, low[...], preferred_element_type=f32)
    return (slope * metric[...]).reshape(chunk, yb, nx)


def slope_along_y(ref, z, table, columns, messages, metric):
    yb = ref.shape[2]
    both = jnp.dot(table[0], ref[0, z], preferred_element_type=f32)
    slope = both[:yb] + both[yb:]
    for k, message in enumerate(messages):
        slope = slope + columns[0, :, k : k + 1] * message[0, z : z + 1, :]
    last = len(messages)
    slope = slope + columns[0, :, last : last + 1] * messages[0][1, z : z + 1, :]
    slope = slope + columns[0, :, last + 1 : last + 2] * messages[-1][1, z : z + 1, :]
    return slope * metric[...]


def slopes_along_z(info, ref, scalars, messages, metric, out):
    _, zb, yb, nx = ref.shape
    rows, lanes = 16, 128
    across = nx // lanes
    block = info[1]
    last = len(messages)

    def tile(t, carry):
        ys = pl.ds(pl.multiple_of((t // across) * rows, rows), rows)
        xs = pl.ds(pl.multiple_of((t % across) * lanes, lanes), lanes)
        f = [ref[0, z, ys, xs].astype(f32) for z in range(zb)]
        scalar = lambda k: scalars[block, k]

        def rhs(z):
            total = None
            for step, weight in ((1, 7.0 / 9.0), (2, 1.0 / 36.0)):
                if z + step < zb and z - step >= 0:
                    term = (f[z + step] - f[z - step]) * weight
                elif z + step < zb:
                    term = f[z + step] * weight
                else:
                    term = f[z - step] * -weight
                total = term if total is None else total + term
            return total

        own = 4 * zb
        run = f[0] * scalar(own) + f[1] * scalar(own + 1)
        for k, message in enumerate(messages):
            run = run + message[0, 0, ys, xs] * scalar(own + 6 + k)
        forward = []
        for z in range(zb):
            run = run * -ratio + rhs(z) * scalar(z)
            forward.append(run)
        run = f[zb - 1] * scalar(own + 2) + f[zb - 2] * scalar(own + 3)
        for k, message in enumerate(messages):
            run = run + message[0, 0, ys, xs] * scalar(own + 6 + last + k)
        for z in reversed(range(zb)):
            run = run * -ratio
            slope = forward[z] * scalar(3 * zb + z) + run * scalar(2 * zb + z)
            run = run + rhs(z) * scalar(zb + z)
            if z == 0:
                slope = slope + messages[0][0, 1, ys, xs] * scalar(own + 4)
            if z == zb - 1:
                slope = slope + messages[-1][0, 1, ys, xs] * scalar(own + 5)
            out[z, ys, xs] = slope * metric[block * zb + z]
        return carry

    lax.fori_loop(0, (yb // rows) * across, tile, 0)


def hand_out(info, spin, outs):
    if len(outs) == 1:
        outs[0][...] = spin[...]
        return
    count = len(outs)
    rows, lanes = outs[0].shape[1:]
    for q, out in enumerate(outs):
        ys = pl.ds(pl.multiple_of(info[2 + q] * rows, rows), rows)
        xs = pl.ds(pl.multiple_of(info[2 + count + q] * lanes, lanes), lanes)
        out[...] = spin[:, ys, xs]


def spin_z_kernel(info, ways, v_ref, high, low, metric_x, u_ref, table, columns, *rest):
    messages, (metric_y, *outs, spin) = rest[: ways[0]], rest[ways[0] :]
    slope_vx = slope_along_x(v_ref, (high, low), metric_x).astype(bf16)
    for z in range(u_ref.shape[1]):
        slope_uy = slope_along_y(u_ref, z, table, columns, messages, metric_y)
        spin[z] = (slope_vx[z].astype(f32) - slope_uy).astype(bf16)
    hand_out(info, spin, outs)


def spin_y_kernel(info, ways, w_ref, high, low, metric_x, u_ref, scalars, *rest):
    messages, (metric_z, *outs, spin, slopes) = rest[: ways[1]], rest[ways[1] :]
    step = pl.program_id(0)
    chunk = w_ref.shape[1]

    @pl.when(step == 0)
    def _():
        slopes_along_z(info, u_ref, scalars, messages, metric_z, slopes)

    slope_wx = slope_along_x(w_ref, (high, low), metric_x).astype(bf16)
    for z in range(chunk):
        spin[z] = (slopes[step * chunk + z] - slope_wx[z].astype(f32)).astype(bf16)
    hand_out(info, spin, outs)


def spin_x_kernel(info, ways, w_ref, table, columns, *rest):
    y_messages, (metric_y, v_ref, scalars, *rest) = rest[: ways[0]], rest[ways[0] :]
    messages, (metric_z, *outs, spin, slopes) = rest[: ways[1]], rest[ways[1] :]
    step = pl.program_id(0)
    chunk = w_ref.shape[1]

    @pl.when(step == 0)
    def _():
        slopes_along_z(info, v_ref, scalars, messages, metric_z, slopes)

    for z in range(chunk):
        slope_wy = slope_along_y(w_ref, z, table, columns, y_messages, metric_y).astype(bf16)
        spin[z] = (slope_wy.astype(f32) - slopes[step * chunk + z]).astype(bf16)
    hand_out(info, spin, outs)


def spin_call(kernel, info, velocity, groups, splits, flops, ways, name):
    _, zb, yb, nx = velocity.shape
    row_parts, col_parts = splits
    chunk = largest_divisor(zb, 4)
    specs, args, scratch = [], [], [pltpu.VMEM((chunk, yb, nx), bf16)]
    whole = lambda a: pl.BlockSpec(a.shape, lambda i, info: (0,) * a.ndim)
    mine = lambda a: pl.BlockSpec((1,) + a.shape[1:], lambda i, info: (info[0],) + (0,) * (a.ndim - 1))
    smem = pl.BlockSpec(memory_space=pltpu.SMEM)

    def add(spec, arg):
        specs.append(spec)
        args.append(arg)

    for kind, field, *more in groups:
        if kind == "z":
            scalars, place, messages, metric = more
            add(pl.BlockSpec((1, zb, yb, nx), lambda i, info, field=field: (field, 0, 0, 0)), velocity)
            add(smem, scalars)
            for message in messages:
                add(
                    pl.BlockSpec(
                        (1,) + message.shape[1:], lambda i, info, place=place: (place, 0, 0, 0)
                    ),
                    message,
                )
            add(smem, metric)
            scratch.append(pltpu.VMEM((zb, yb, nx), f32))
            continue
        add(pl.BlockSpec((1, chunk, yb, nx), lambda i, info, field=field: (field, i, 0, 0)), velocity)
        if kind == "x":
            (high, low), metric = more
            add(whole(high), high)
            add(whole(low), low)
            add(whole(metric), metric)
        else:
            table, columns, messages, metric = more
            add(mine(table), table)
            add(mine(columns), columns)
            for message in messages:
                parts = message.shape[0]
                add(
                    pl.BlockSpec((parts, None, chunk, nx), lambda i, info: (0, i, 0, 0)),
                    message.reshape(parts, zb // chunk, chunk, nx),
                )
            add(pl.BlockSpec((yb, 1), lambda i, info: (info[0], 0)), metric)

    count = row_parts * col_parts
    block = (yb // row_parts, nx // col_parts)
    return pl.pallas_call(
        lambda info, *refs: kernel(info, ways, *refs),
        grid_spec=pltpu.PrefetchScalarGridSpec(
            num_scalar_prefetch=1,
            grid=(zb // chunk,),
            in_specs=specs,
            out_specs=[pl.BlockSpec((chunk,) + block, lambda i, info: (i, 0, 0))] * count,
            scratch_shapes=scratch,
        ),
        out_shape=[jax.ShapeDtypeStruct((zb,) + block, bf16)] * count,
        compiler_params=pltpu.CompilerParams(vmem_limit_bytes=VMEM_LIMIT),
        cost_estimate=pl.CostEstimate(
            flops=flops, bytes_accessed=8 * zb * yb * nx, transcendentals=0
        ),
        name=name,
    )(info, *args)


def sketch_kernel(info, weights, *rest):
    count = weights.shape[0]
    fields = rest[:count]
    out = rest[-1]
    values = [field[...].astype(f32) for field in fields]
    for k in range(out.shape[0]):
        total = values[0] * weights[info[1], k]
        for r in range(1, count):
            total = total + values[r] * weights[info[1 + r], k]
        out[k, 0] = total


def sketch_part(info, sketch_matrix, fields, total, component, shape):
    zb, rows, lanes = fields[0].shape
    rank = sketch_matrix.shape[1]
    chunk = largest_divisor(zb, 8)
    steps = zb // chunk
    piece = pl.BlockSpec((chunk, rows, lanes), lambda i, info: (i, 0, 0))
    specs = [pl.BlockSpec(memory_space=pltpu.SMEM)] + [piece] * len(fields)
    args = [sketch_matrix, *fields]
    aliases = {}
    if total is not None:
        specs.append(pl.BlockSpec(memory_space=pl.ANY))
        args.append(total)
        aliases = {len(args): 0}
    return pl.pallas_call(
        sketch_kernel,
        grid_spec=pltpu.PrefetchScalarGridSpec(
            num_scalar_prefetch=1,
            grid=(steps,),
            in_specs=specs,
            out_specs=pl.BlockSpec(
                (rank, 1, chunk, rows, lanes),
                lambda i, info: (0, component, info[0] * steps + i, 0, 0),
            ),
        ),
        out_shape=jax.ShapeDtypeStruct(shape, f32),
        input_output_aliases=aliases,
        compiler_params=pltpu.CompilerParams(vmem_limit_bytes=VMEM_LIMIT),
        cost_estimate=pl.CostEstimate(
            flops=2 * rank * len(fields) * zb * rows * lanes,
            bytes_accessed=(2 * len(fields) + 4 * rank) * zb * rows * lanes,
            transcendentals=0,
        ),
        name="sketch_part",
    )(info, *args)


def col_rank(c, count):
    return (c % 2) * (count // 2) + c // 2 if count % 2 == 0 else c


def col_of_rank(t, count):
    return (t % (count // 2)) * 2 + t // (count // 2) if count % 2 == 0 else t


def routes(snaps, cols, depth):
    out = []
    place = lambda s, y, z: (s * cols + y) * depth + z
    for shift in range(depth):
        for turn in range(cols):
            first, second = [], []
            for s in range(snaps):
                for p in range(cols):
                    for z in range(depth):
                        c = col_of_rank((p - turn - s) % cols, cols)
                        first.append((place(s, p, z), place(s, c, z)))
                        second.append((place(s, c, z), place(p, c, (z + shift) % depth)))
            out.append((first, second))
    return out


def general_way(vorticity, sketch_matrix):
    lines = lax.all_to_all(vorticity, "py", split_axis=4, concat_axis=3, tiled=True)
    snap_count = lax.axis_size("snap")
    pz_count = lax.axis_size("pz")
    shape_now = lines.shape
    block_rows = shape_now[3] // (snap_count * pz_count)
    split_rows = lines.reshape(shape_now[:3] + (snap_count, pz_count, block_rows, shape_now[4]))
    reordered = jnp.swapaxes(split_rows, 3, 4).reshape(shape_now)
    lines = lax.all_to_all(reordered, "pz", split_axis=3, concat_axis=2, tiled=True)
    lines = lax.all_to_all(lines, "snap", split_axis=3, concat_axis=0, tiled=True)
    return jnp.einsum(
        "sk,sczyx->kczyx", sketch_matrix, lines.astype(f32), precision=lax.Precision.HIGHEST
    )


def on_device(velocity, metric_x, metric_y, metric_z, sketch_matrix):
    snaps, cols, depth = (lax.axis_size(name) for name in ("snap", "py", "pz"))
    s, p, z = (lax.axis_index(name) for name in ("snap", "py", "pz"))
    _, _, zb, yb, nx = velocity.shape
    ny, nz = yb * cols, zb * depth
    velocity = velocity[0]
    direct = snaps == cols
    messages = [(shift, turn) for shift in range(depth) for turn in range(cols)]

    tables_x = [jnp.asarray(t) for t in split_table(line_table(nx, 0, nx).T)]
    tables_y = per_block(line_table, ny, cols)
    tables_y = jnp.asarray(np.concatenate(split_table(tables_y), axis=1))
    columns_y = jnp.asarray(per_block(message_columns, ny, cols), f32)
    weights_y = jnp.asarray(np.swapaxes(per_block(message_weights, ny, cols), 1, 2), f32)
    weights_z = jnp.asarray(per_block(message_weights, nz, depth).reshape(depth, -1), f32)
    scalars_z = jnp.asarray(per_block(sweep_scalars, nz, depth), f32)
    metric_x = metric_x.reshape(1, nx)
    metric_y = metric_y.reshape(ny, 1)

    where = [p, z]
    if direct:
        where += [(z + shift) % depth for shift, turn in messages]
        where += [col_of_rank((p - turn - s) % cols, cols) for shift, turn in messages]
    info = jnp.stack(where).astype(jnp.int32)
    splits = (depth, cols) if direct else (1, 1)

    u_edges = exchange(edge_y(info, velocity, 0, weights_y), "py")
    w_edges = exchange(edge_y(info, velocity, 2, weights_y), "py")
    z_edges = exchange(edge_z(info, velocity, weights_z), "pz")

    points = zb * yb * nx
    along_x = lambda field: ("x", field, tables_x, metric_x)
    along_y = lambda field, edges: ("y", field, tables_y, columns_y, edges, metric_y)
    along_z = lambda field: ("z", field, scalars_z, field, z_edges, metric_z)
    call = functools.partial(spin_call, splits=splits, ways=(cols - 1, depth - 1))
    spins = {}
    spins[2] = call(
        spin_z_kernel, info, velocity, [along_x(1), along_y(0, u_edges)],
        flops=points * 4 * (nx + yb), name="spin_z",
    )
    spins[1] = call(
        spin_y_kernel, info, velocity, [along_x(2), along_z(0)],
        flops=points * (4 * nx + 20), name="spin_y",
    )
    spins[0] = call(
        spin_x_kernel, info, velocity, [along_y(2, w_edges), along_z(1)],
        flops=points * (4 * yb + 20), name="spin_x",
    )
    if not direct:
        vorticity = jnp.stack([spins[c][0] for c in range(3)])[None]
        return general_way(vorticity, sketch_matrix)

    all_routes = routes(snaps, cols, depth)
    shape = (sketch_matrix.shape[1], 3, nz, yb // depth, nx // cols)
    my_rank = col_rank(p, cols)
    total = None
    for component in (2, 1, 0):
        got = []
        for part, (first, second) in zip(spins[component], all_routes):
            part = lax.ppermute(part, ("snap", "py", "pz"), first)
            got.append(lax.ppermute(part, ("snap", "py", "pz"), second))
        for shift in range(depth):
            whence = [(z - shift) % depth]
            whence += [(s - turn - my_rank) % snaps for turn in range(cols)]
            total = sketch_part(
                jnp.stack(whence).astype(jnp.int32),
                sketch_matrix,
                got[shift * cols : (shift + 1) * cols],
                total,
                component,
                shape,
            )
    return total


def solution(mesh):
    placed = (P("snap", None, "pz", "py", None), P(), P(), P(), P())
    return jax.shard_map(
        on_device,
        mesh=mesh,
        in_specs=placed,
        out_specs=P(None, None, None, ("snap", "pz"), "py"),
        check_vma=False,
    )
```

```python
import functools

import jax
import jax.numpy as jnp
import ml_dtypes
import numpy as np
from jax import lax
from jax.experimental import pallas as pl
from jax.experimental.pallas import tpu as pltpu
from jax.sharding import PartitionSpec as P

ratio = (3.0 - 5.0**0.5) / 2.0
VMEM_LIMIT = 52 * 1024 * 1024
in_flight = 4
f32 = jnp.float32
bf16 = jnp.bfloat16


def lead(i):
    return 1.0 - ratio ** (2.0 * (np.asarray(i, np.float64) + 1.0))


def trail(i, n):
    return 1.0 - ratio ** (2.0 * (n - np.asarray(i, np.float64)))


def denom(n):
    return 5.0**0.5 / 3.0 * (1.0 - ratio ** (2.0 * (n + 1.0)))


def inverse_entry(row, col, n):
    inside = (col >= 0) & (col < n)
    col = np.clip(col, 0, n - 1)
    near, far = np.minimum(row, col), np.maximum(row, col)
    sign = 1.0 - 2.0 * ((far - near) % 2)
    value = sign * ratio ** (far - near).astype(np.float64) * lead(near) * trail(far, n) / denom(n)
    return np.where(inside, value, 0.0)


def line_table(n, start, size):
    row = start + np.arange(size)[:, None]
    col = start + np.arange(size)[None, :]
    entry = functools.partial(inverse_entry, row, n=n)
    first = entry(col - 1) - entry(col + 1)
    second = entry(col - 2) - entry(col + 2)
    return 7.0 / 9.0 * first + 1.0 / 36.0 * second


def split_table(table):
    high = table.astype(ml_dtypes.bfloat16)
    low = (table - high.astype(np.float64)).astype(ml_dtypes.bfloat16)
    return high, low


def edge_weights(n, start, size):
    last = start + size - 1
    j = start + np.arange(size)

    def forward(k):
        return np.where(k >= 0, (-ratio) ** (last - k).astype(np.float64) * lead(k), 0.0)

    def backward(k):
        return np.where(k <= n - 1, (-ratio) ** (k - start).astype(np.float64) * trail(k, n), 0.0)

    def weights(c):
        return 7.0 / 9.0 * (c(j - 1) - c(j + 1)) + 1.0 / 36.0 * (c(j - 2) - c(j + 2))

    return weights(forward), weights(backward)


def edge_columns(n, start, size):
    i = start + np.arange(size)
    left = (-ratio) ** (i - start + 1.0) * trail(i, n) / denom(n)
    right = (-ratio) ** (start + size - i).astype(np.float64) * lead(i) / denom(n)
    return left, right


def message_weights(n, start, size):
    count, block = n // size, start // size
    right, left = edge_weights(n, start, size)
    return np.stack([right if block < count - k else left for k in range(1, count)])


def message_shares(n, start, size):
    count, block = n // size, start // size
    decay = (-ratio) ** size
    left = [decay ** (k - 1) if block >= k else 0.0 for k in range(1, count)]
    right = [decay ** (count - k - 1) if block < k else 0.0 for k in range(1, count)]
    corner = [-1.0 / 12.0 if block > 0 else 0.0, 1.0 / 12.0 if block < count - 1 else 0.0]
    return np.array(left), np.array(right), np.array(corner)


def message_columns(n, start, size):
    left, right = edge_columns(n, start, size)
    share_left, share_right, corner = message_shares(n, start, size)
    corners = np.zeros((size, 2))
    corners[0, 0], corners[-1, 1] = corner
    return np.concatenate([np.outer(left, share_left) + np.outer(right, share_right), corners], axis=1)


def sweep_scalars(n, start, size):
    i = start + np.arange(size)
    after = start + size
    own_left = [0.0, 0.0]
    own_right = [0.0, 0.0]
    if start > 0:
        own_left = [7.0 / 9.0 * lead(start - 1) - ratio / 36.0 * lead(start - 2), lead(start - 1) / 36.0]
    if after < n:
        own_right = [
            -7.0 / 9.0 * trail(after, n) + ratio / 36.0 * trail(after + 1, n),
            -trail(after, n) / 36.0,
        ]
    rows = [lead(i), trail(i, n), lead(i) / denom(n), trail(i, n) / denom(n)]
    share_left, share_right, corner = message_shares(n, start, size)
    return np.concatenate(rows + [np.array(own_left + own_right), corner, share_left, share_right])


def per_block(make, n, count):
    size = n // count
    return np.stack([make(n, block * size, size) for block in range(count)])


def largest_divisor(size, most):
    return max(d for d in range(1, most + 1) if size % d == 0)


def message_forms(count):
    return [k in (1, count - 1) for k in range(1, count)]


def edge_y_kernel(info, weights, ref, *outs):
    count = len(outs) + 1
    for z in range(ref.shape[1]):
        values = ref[0, z].astype(f32)
        for k, out in enumerate(outs, 1):
            out[0, z, :] = jnp.sum(values * weights[0, :, k - 1 : k], axis=0).astype(out.dtype)
            if out.shape[0] == 2:
                out[1, z, :] = jnp.where(info[0] < count - k, values[-1], values[0])


def edge_y(info, velocity, field, weights):
    _, zb, yb, nx = velocity.shape
    count = weights.shape[0]
    chunk = 8 if zb % 8 == 0 else zb
    forms = message_forms(count)
    return pl.pallas_call(
        edge_y_kernel,
        grid_spec=pltpu.PrefetchScalarGridSpec(
            num_scalar_prefetch=1,
            grid=(zb // chunk,),
            in_specs=[
                pl.BlockSpec((1, yb, count - 1), lambda i, info: (info[0], 0, 0)),
                pl.BlockSpec((1, chunk, yb, nx), lambda i, info: (field, i, 0, 0)),
            ],
            out_specs=[pl.BlockSpec((1 + near, chunk, nx), lambda i, info: (0, i, 0)) for near in forms],
        ),
        out_shape=[jax.ShapeDtypeStruct((1 + near, zb, nx), f32) for near in forms],
        compiler_params=pltpu.CompilerParams(vmem_limit_bytes=VMEM_LIMIT),
        cost_estimate=pl.CostEstimate(
            flops=6 * zb * yb * nx, bytes_accessed=2 * zb * yb * nx, transcendentals=0
        ),
        name="edge_y",
    )(info, weights, velocity)


def edge_z_kernel(info, weights, u_ref, v_ref, *outs):
    zb = u_ref.shape[1]
    count = len(outs) + 1
    for field, ref in enumerate((u_ref, v_ref)):
        for k, out in enumerate(outs, 1):
            first = ref[0, 0].astype(f32)
            total = first * weights[info[1], (k - 1) * zb]
            for z in range(1, zb):
                values = ref[0, z].astype(f32)
                total = total + values * weights[info[1], (k - 1) * zb + z]
            out[field, 0] = total
            if out.shape[1] == 2:
                out[field, 1] = jnp.where(info[1] < count - k, values, first)


def edge_z(info, velocity, weights):
    _, zb, yb, nx = velocity.shape
    rows = 16
    forms = message_forms(weights.shape[0])
    piece = lambda f: pl.BlockSpec((1, zb, rows, nx), lambda i, info: (f, 0, i, 0))
    return pl.pallas_call(
        edge_z_kernel,
        grid_spec=pltpu.PrefetchScalarGridSpec(
            num_scalar_prefetch=1,
            grid=(yb // rows,),
            in_specs=[pl.BlockSpec(memory_space=pltpu.SMEM), piece(0), piece(1)],
            out_specs=[
                pl.BlockSpec((2, 1 + near, rows, nx), lambda i, info: (0, 0, i, 0)) for near in forms
            ],
        ),
        out_shape=[jax.ShapeDtypeStruct((2, 1 + near, yb, nx), f32) for near in forms],
        compiler_params=pltpu.CompilerParams(vmem_limit_bytes=VMEM_LIMIT),
        cost_estimate=pl.CostEstimate(
            flops=6 * zb * yb * nx, bytes_accessed=4 * zb * yb * nx, transcendentals=0
        ),
        name="edge_z",
    )(info, weights, velocity, velocity)


def exchange(messages, axis):
    count = lax.axis_size(axis)
    out = []
    for k, message in enumerate(messages, 1):
        pairs = [(i, (i + k) % count) for i in range(count)]
        out.append(lax.ppermute(message, axis, pairs))
    return out


def slope_along_x(ref, tables, metric):
    chunk, yb, nx = ref.shape[1:]
    field = ref[0].reshape(chunk * yb, nx)
    high, low = tables
    slope = jnp.dot(field, high[...], preferred_element_type=f32)
    slope = slope + jnp.dot(field, low[...], preferred_element_type=f32)
    return (slope * metric[...]).reshape(chunk, yb, nx)


def slope_along_y(ref, z, table, columns, messages, metric):
    yb = ref.shape[2]
    both = jnp.dot(table[0], ref[0, z], preferred_element_type=f32)
    slope = both[:yb] + both[yb:]
    for k, message in enumerate(messages):
        slope = slope + columns[0, :, k : k + 1] * message[0, z : z + 1, :]
    last = len(messages)
    slope = slope + columns[0, :, last : last + 1] * messages[0][1, z : z + 1, :]
    slope = slope + columns[0, :, last + 1 : last + 2] * messages[-1][1, z : z + 1, :]
    return slope * metric[...]


def slopes_along_z(info, ref, scalars, messages, metric, out):
    _, zb, yb, nx = ref.shape
    rows, lanes = 16, 128
    across = nx // lanes
    block = info[1]
    last = len(messages)

    def tile(t, carry):
        ys = pl.ds(pl.multiple_of((t // across) * rows, rows), rows)
        xs = pl.ds(pl.multiple_of((t % across) * lanes, lanes), lanes)
        f = [ref[0, z, ys, xs].astype(f32) for z in range(zb)]
        scalar = lambda k: scalars[block, k]

        def rhs(z):
            total = None
            for step, weight in ((1, 7.0 / 9.0), (2, 1.0 / 36.0)):
                if z + step < zb and z - step >= 0:
                    term = (f[z + step] - f[z - step]) * weight
                elif z + step < zb:
                    term = f[z + step] * weight
                else:
                    term = f[z - step] * -weight
                total = term if total is None else total + term
            return total

        own = 4 * zb
        run = f[0] * scalar(own) + f[1] * scalar(own + 1)
        for k, message in enumerate(messages):
            run = run + message[0, 0, ys, xs] * scalar(own + 6 + k)
        forward = []
        for z in range(zb):
            run = run * -ratio + rhs(z) * scalar(z)
            forward.append(run)
        run = f[zb - 1] * scalar(own + 2) + f[zb - 2] * scalar(own + 3)
        for k, message in enumerate(messages):
            run = run + message[0, 0, ys, xs] * scalar(own + 6 + last + k)
        for z in reversed(range(zb)):
            run = run * -ratio
            slope = forward[z] * scalar(3 * zb + z) + run * scalar(2 * zb + z)
            run = run + rhs(z) * scalar(zb + z)
            if z == 0:
                slope = slope + messages[0][0, 1, ys, xs] * scalar(own + 4)
            if z == zb - 1:
                slope = slope + messages[-1][0, 1, ys, xs] * scalar(own + 5)
            out[z, ys, xs] = slope * metric[block * zb + z]
        return carry

    lax.fori_loop(0, (yb // rows) * across, tile, 0)


def hand_out(info, spin, outs):
    if len(outs) == 1:
        outs[0][...] = spin[...]
        return
    count = len(outs)
    rows, lanes = outs[0].shape[1:]
    for q, out in enumerate(outs):
        ys = pl.ds(pl.multiple_of(info[2 + q] * rows, rows), rows)
        xs = pl.ds(pl.multiple_of(info[2 + count + q] * lanes, lanes), lanes)
        out[...] = spin[:, ys, xs]


def spin_z_kernel(info, ways, v_ref, high, low, metric_x, u_ref, table, columns, *rest):
    messages, (metric_y, *outs, spin) = rest[: ways[0]], rest[ways[0] :]
    slope_vx = slope_along_x(v_ref, (high, low), metric_x).astype(bf16)
    for z in range(u_ref.shape[1]):
        slope_uy = slope_along_y(u_ref, z, table, columns, messages, metric_y)
        spin[z] = (slope_vx[z].astype(f32) - slope_uy).astype(bf16)
    hand_out(info, spin, outs)


def spin_y_kernel(info, ways, w_ref, high, low, metric_x, u_ref, scalars, *rest):
    messages, (metric_z, *outs, spin, slopes) = rest[: ways[1]], rest[ways[1] :]
    step = pl.program_id(0)
    chunk = w_ref.shape[1]

    @pl.when(step == 0)
    def _():
        slopes_along_z(info, u_ref, scalars, messages, metric_z, slopes)

    slope_wx = slope_along_x(w_ref, (high, low), metric_x).astype(bf16)
    for z in range(chunk):
        spin[z] = (slopes[step * chunk + z] - slope_wx[z].astype(f32)).astype(bf16)
    hand_out(info, spin, outs)


def spin_x_kernel(info, ways, w_ref, table, columns, *rest):
    y_messages, (metric_y, v_ref, scalars, *rest) = rest[: ways[0]], rest[ways[0] :]
    messages, (metric_z, *outs, spin, slopes) = rest[: ways[1]], rest[ways[1] :]
    step = pl.program_id(0)
    chunk = w_ref.shape[1]

    @pl.when(step == 0)
    def _():
        slopes_along_z(info, v_ref, scalars, messages, metric_z, slopes)

    for z in range(chunk):
        slope_wy = slope_along_y(w_ref, z, table, columns, y_messages, metric_y).astype(bf16)
        spin[z] = (slope_wy.astype(f32) - slopes[step * chunk + z]).astype(bf16)
    hand_out(info, spin, outs)


def spin_call(kernel, info, velocity, groups, splits, flops, ways, name):
    _, zb, yb, nx = velocity.shape
    row_parts, col_parts = splits
    chunk = largest_divisor(zb, 4)
    specs, args, scratch = [], [], [pltpu.VMEM((chunk, yb, nx), bf16)]
    whole = lambda a: pl.BlockSpec(a.shape, lambda i, info: (0,) * a.ndim)
    mine = lambda a: pl.BlockSpec((1,) + a.shape[1:], lambda i, info: (info[0],) + (0,) * (a.ndim - 1))
    smem = pl.BlockSpec(memory_space=pltpu.SMEM)

    def add(spec, arg):
        specs.append(spec)
        args.append(arg)

    for kind, field, *more in groups:
        if kind == "z":
            scalars, place, messages, metric = more
            add(pl.BlockSpec((1, zb, yb, nx), lambda i, info, field=field: (field, 0, 0, 0)), velocity)
            add(smem, scalars)
            for message in messages:
                add(
                    pl.BlockSpec(
                        (1,) + message.shape[1:], lambda i, info, place=place: (place, 0, 0, 0)
                    ),
                    message,
                )
            add(smem, metric)
            scratch.append(pltpu.VMEM((zb, yb, nx), f32))
            continue
        add(pl.BlockSpec((1, chunk, yb, nx), lambda i, info, field=field: (field, i, 0, 0)), velocity)
        if kind == "x":
            (high, low), metric = more
            add(whole(high), high)
            add(whole(low), low)
            add(whole(metric), metric)
        else:
            table, columns, messages, metric = more
            add(mine(table), table)
            add(mine(columns), columns)
            for message in messages:
                parts = message.shape[0]
                add(
                    pl.BlockSpec((parts, None, chunk, nx), lambda i, info: (0, i, 0, 0)),
                    message.reshape(parts, zb // chunk, chunk, nx),
                )
            add(pl.BlockSpec((yb, 1), lambda i, info: (info[0], 0)), metric)

    count = row_parts * col_parts
    block = (yb // row_parts, nx // col_parts)
    return pl.pallas_call(
        lambda info, *refs: kernel(info, ways, *refs),
        grid_spec=pltpu.PrefetchScalarGridSpec(
            num_scalar_prefetch=1,
            grid=(zb // chunk,),
            in_specs=specs,
            out_specs=[pl.BlockSpec((chunk,) + block, lambda i, info: (i, 0, 0))] * count,
            scratch_shapes=scratch,
        ),
        out_shape=[jax.ShapeDtypeStruct((zb,) + block, bf16)] * count,
        compiler_params=pltpu.CompilerParams(vmem_limit_bytes=VMEM_LIMIT),
        cost_estimate=pl.CostEstimate(
            flops=flops, bytes_accessed=8 * zb * yb * nx, transcendentals=0
        ),
        name=name,
    )(info, *args)


def sketch_kernel(info, weights, *rest):
    count = weights.shape[0]
    fields = rest[:count]
    out = rest[-1]
    values = [field[...].astype(f32) for field in fields]
    for k in range(out.shape[0]):
        total = values[0] * weights[info[1], k]
        for r in range(1, count):
            total = total + values[r] * weights[info[1 + r], k]
        out[k, 0] = total


def sketch_part(info, sketch_matrix, fields, total, component, shape):
    zb, rows, lanes = fields[0].shape
    rank = sketch_matrix.shape[1]
    chunk = largest_divisor(zb, 8)
    steps = zb // chunk
    piece = pl.BlockSpec((chunk, rows, lanes), lambda i, info: (i, 0, 0))
    specs = [pl.BlockSpec(memory_space=pltpu.SMEM)] + [piece] * len(fields)
    args = [sketch_matrix, *fields]
    aliases = {}
    if total is not None:
        specs.append(pl.BlockSpec(memory_space=pl.ANY))
        args.append(total)
        aliases = {len(args): 0}
    return pl.pallas_call(
        sketch_kernel,
        grid_spec=pltpu.PrefetchScalarGridSpec(
            num_scalar_prefetch=1,
            grid=(steps,),
            in_specs=specs,
            out_specs=pl.BlockSpec(
                (rank, 1, chunk, rows, lanes),
                lambda i, info: (0, component, info[0] * steps + i, 0, 0),
            ),
        ),
        out_shape=jax.ShapeDtypeStruct(shape, f32),
        input_output_aliases=aliases,
        compiler_params=pltpu.CompilerParams(vmem_limit_bytes=VMEM_LIMIT),
        cost_estimate=pl.CostEstimate(
            flops=2 * rank * len(fields) * zb * rows * lanes,
            bytes_accessed=(2 * len(fields) + 4 * rank) * zb * rows * lanes,
            transcendentals=0,
        ),
        name="sketch_part",
    )(info, *args)


def col_rank(c, count):
    return (c % 2) * (count // 2) + c // 2 if count % 2 == 0 else c


def col_of_rank(t, count):
    return (t % (count // 2)) * 2 + t // (count // 2) if count % 2 == 0 else t


def routes(snaps, cols, depth):
    out = []
    place = lambda s, y, z: (s * cols + y) * depth + z
    for shift in range(depth):
        for turn in range(cols):
            first, second = [], []
            for s in range(snaps):
                for p in range(cols):
                    for z in range(depth):
                        c = col_of_rank((p - turn - s) % cols, cols)
                        first.append((place(s, p, z), place(s, c, z)))
                        second.append((place(s, c, z), place(p, c, (z + shift) % depth)))
            out.append((first, second))
    return out


def travel_order(count, ahead):
    steps = [(0, i) for i in range(min(ahead, count))]
    for i in range(count):
        steps.append((1, i))
        if i + ahead < count:
            steps.append((0, i + ahead))
    return steps


def general_way(vorticity, sketch_matrix):
    lines = lax.all_to_all(vorticity, "py", split_axis=4, concat_axis=3, tiled=True)
    snap_count = lax.axis_size("snap")
    pz_count = lax.axis_size("pz")
    shape_now = lines.shape
    block_rows = shape_now[3] // (snap_count * pz_count)
    split_rows = lines.reshape(shape_now[:3] + (snap_count, pz_count, block_rows, shape_now[4]))
    reordered = jnp.swapaxes(split_rows, 3, 4).reshape(shape_now)
    lines = lax.all_to_all(reordered, "pz", split_axis=3, concat_axis=2, tiled=True)
    lines = lax.all_to_all(lines, "snap", split_axis=3, concat_axis=0, tiled=True)
    return jnp.einsum(
        "sk,sczyx->kczyx", sketch_matrix, lines.astype(f32), precision=lax.Precision.HIGHEST
    )


def on_device(velocity, metric_x, metric_y, metric_z, sketch_matrix):
    snaps, cols, depth = (lax.axis_size(name) for name in ("snap", "py", "pz"))
    s, p, z = (lax.axis_index(name) for name in ("snap", "py", "pz"))
    _, _, zb, yb, nx = velocity.shape
    ny, nz = yb * cols, zb * depth
    velocity = velocity[0]
    direct = snaps == cols
    messages = [(shift, turn) for shift in range(depth) for turn in range(cols)]

    tables_x = [jnp.asarray(t) for t in split_table(line_table(nx, 0, nx).T)]
    tables_y = per_block(line_table, ny, cols)
    tables_y = jnp.asarray(np.concatenate(split_table(tables_y), axis=1))
    columns_y = jnp.asarray(per_block(message_columns, ny, cols), f32)
    weights_y = jnp.asarray(np.swapaxes(per_block(message_weights, ny, cols), 1, 2), f32)
    weights_z = jnp.asarray(per_block(message_weights, nz, depth).reshape(depth, -1), f32)
    scalars_z = jnp.asarray(per_block(sweep_scalars, nz, depth), f32)
    metric_x = metric_x.reshape(1, nx)
    metric_y = metric_y.reshape(ny, 1)

    where = [p, z]
    if direct:
        where += [(z + shift) % depth for shift, turn in messages]
        where += [col_of_rank((p - turn - s) % cols, cols) for shift, turn in messages]
    info = jnp.stack(where).astype(jnp.int32)
    splits = (depth, cols) if direct else (1, 1)

    u_edges = exchange(edge_y(info, velocity, 0, weights_y), "py")
    points = zb * yb * nx
    along_x = lambda field: ("x", field, tables_x, metric_x)
    along_y = lambda field, edges: ("y", field, tables_y, columns_y, edges, metric_y)
    along_z = lambda field: ("z", field, scalars_z, field, z_edges, metric_z)
    call = functools.partial(spin_call, splits=splits, ways=(cols - 1, depth - 1))
    spins = {}
    spins[2] = call(
        spin_z_kernel, info, velocity, [along_x(1), along_y(0, u_edges)],
        flops=points * 4 * (nx + yb), name="spin_z",
    )
    info, _ = lax.optimization_barrier((info, spins[2][0]))
    z_edges = exchange(edge_z(info, velocity, weights_z), "pz")
    w_edges = exchange(edge_y(info, velocity, 2, weights_y), "py")
    spins[1] = call(
        spin_y_kernel, info, velocity, [along_x(2), along_z(0)],
        flops=points * (4 * nx + 20), name="spin_y",
    )
    spins[0] = call(
        spin_x_kernel, info, velocity, [along_y(2, w_edges), along_z(1)],
        flops=points * (4 * yb + 20), name="spin_x",
    )
    if not direct:
        vorticity = jnp.stack([spins[c][0] for c in range(3)])[None]
        return general_way(vorticity, sketch_matrix)

    all_routes = routes(snaps, cols, depth)
    everywhere = ("snap", "py", "pz")
    order = (2, 1, 0)
    parts = [part for component in order for part in spins[component]]
    count = len(all_routes)
    steps = travel_order(len(parts), ahead=4)
    arrived = {}
    for place, (hop, i) in enumerate(steps):
        sent = parts[i] if hop == 0 else arrived[0, i]
        if place >= in_flight:
            sent, _ = lax.optimization_barrier((sent, arrived[steps[place - in_flight]]))
        arrived[hop, i] = lax.ppermute(sent, everywhere, all_routes[i % count][hop])

    shape = (sketch_matrix.shape[1], 3, nz, yb // depth, nx // cols)
    my_rank = col_rank(p, cols)
    total = None
    for place, component in enumerate(order):
        for shift in range(depth):
            whence = [(z - shift) % depth]
            whence += [(s - turn - my_rank) % snaps for turn in range(cols)]
            begin = place * count + shift * cols
            total = sketch_part(
                jnp.stack(whence).astype(jnp.int32),
                sketch_matrix,
                [arrived[1, i] for i in range(begin, begin + cols)],
                total,
                component,
                shape,
            )
    return total


def solution(mesh):
    placed = (P("snap", None, "pz", "py", None), P(), P(), P(), P())
    return jax.shard_map(
        on_device,
        mesh=mesh,
        in_specs=placed,
        out_specs=P(None, None, None, ("snap", "pz"), "py"),
        check_vma=False,
    )
```

```python
import functools

import jax
import jax.numpy as jnp
import ml_dtypes
import numpy as np
from jax import lax
from jax.experimental import pallas as pl
from jax.experimental.pallas import tpu as pltpu
from jax.sharding import PartitionSpec as P

ratio = (3.0 - 5.0**0.5) / 2.0
VMEM_LIMIT = 52 * 1024 * 1024
f32 = jnp.float32
bf16 = jnp.bfloat16


def lead(i):
    return 1.0 - ratio ** (2.0 * (np.asarray(i, np.float64) + 1.0))


def trail(i, n):
    return 1.0 - ratio ** (2.0 * (n - np.asarray(i, np.float64)))


def denom(n):
    return 5.0**0.5 / 3.0 * (1.0 - ratio ** (2.0 * (n + 1.0)))


def inverse_entry(row, col, n):
    inside = (col >= 0) & (col < n)
    col = np.clip(col, 0, n - 1)
    near, far = np.minimum(row, col), np.maximum(row, col)
    sign = 1.0 - 2.0 * ((far - near) % 2)
    value = sign * ratio ** (far - near).astype(np.float64) * lead(near) * trail(far, n) / denom(n)
    return np.where(inside, value, 0.0)


def line_table(n, start, size):
    row = start + np.arange(size)[:, None]
    col = start + np.arange(size)[None, :]
    entry = functools.partial(inverse_entry, row, n=n)
    first = entry(col - 1) - entry(col + 1)
    second = entry(col - 2) - entry(col + 2)
    return 7.0 / 9.0 * first + 1.0 / 36.0 * second


def split_table(table):
    high = table.astype(ml_dtypes.bfloat16)
    low = (table - high.astype(np.float64)).astype(ml_dtypes.bfloat16)
    return high, low


def edge_weights(n, start, size):
    last = start + size - 1
    j = start + np.arange(size)

    def forward(k):
        return np.where(k >= 0, (-ratio) ** (last - k).astype(np.float64) * lead(k), 0.0)

    def backward(k):
        return np.where(k <= n - 1, (-ratio) ** (k - start).astype(np.float64) * trail(k, n), 0.0)

    def weights(c):
        return 7.0 / 9.0 * (c(j - 1) - c(j + 1)) + 1.0 / 36.0 * (c(j - 2) - c(j + 2))

    return weights(forward), weights(backward)


def edge_columns(n, start, size):
    i = start + np.arange(size)
    left = (-ratio) ** (i - start + 1.0) * trail(i, n) / denom(n)
    right = (-ratio) ** (start + size - i).astype(np.float64) * lead(i) / denom(n)
    return left, right


def message_weights(n, start, size):
    count, block = n // size, start // size
    right, left = edge_weights(n, start, size)
    return np.stack([right if block < count - k else left for k in range(1, count)])


def message_shares(n, start, size):
    count, block = n // size, start // size
    decay = (-ratio) ** size
    left = [decay ** (k - 1) if block >= k else 0.0 for k in range(1, count)]
    right = [decay ** (count - k - 1) if block < k else 0.0 for k in range(1, count)]
    corner = [-1.0 / 12.0 if block > 0 else 0.0, 1.0 / 12.0 if block < count - 1 else 0.0]
    return np.array(left), np.array(right), np.array(corner)


def message_columns(n, start, size):
    left, right = edge_columns(n, start, size)
    share_left, share_right, corner = message_shares(n, start, size)
    corners = np.zeros((size, 2))
    corners[0, 0], corners[-1, 1] = corner
    return np.concatenate([np.outer(left, share_left) + np.outer(right, share_right), corners], axis=1)


def sweep_scalars(n, start, size):
    i = start + np.arange(size)
    after = start + size
    own_left = [0.0, 0.0]
    own_right = [0.0, 0.0]
    if start > 0:
        own_left = [7.0 / 9.0 * lead(start - 1) - ratio / 36.0 * lead(start - 2), lead(start - 1) / 36.0]
    if after < n:
        own_right = [
            -7.0 / 9.0 * trail(after, n) + ratio / 36.0 * trail(after + 1, n),
            -trail(after, n) / 36.0,
        ]
    rows = [lead(i), trail(i, n), lead(i) / denom(n), trail(i, n) / denom(n)]
    share_left, share_right, corner = message_shares(n, start, size)
    return np.concatenate(rows + [np.array(own_left + own_right), corner, share_left, share_right])


def per_block(make, n, count):
    size = n // count
    return np.stack([make(n, block * size, size) for block in range(count)])


def largest_divisor(size, most):
    return max(d for d in range(1, most + 1) if size % d == 0)


def message_forms(count):
    return [k in (1, count - 1) for k in range(1, count)]


def edge_kernel(info, y_weights, z_weights, u_ref, v_ref, w_ref, *outs):
    step, steps = pl.program_id(0), pl.num_programs(0)
    chunk, yb, _ = u_ref.shape[1:]
    ways = y_weights.shape[1] // 2
    y_outs, z_outs = outs[:ways], outs[ways:]
    for field, ref in enumerate((u_ref, w_ref)):
        for z in range(chunk):
            sums = jnp.dot(y_weights[0], ref[0, z], preferred_element_type=f32)
            sums = sums[:ways] + sums[ways:]
            for k, out in enumerate(y_outs):
                out[field, 0, z, :] = sums[k]
                if out.shape[1] == 2:
                    edge = jnp.where(info[0] < ways - k, ref[0, z, yb - 1 :, :], ref[0, z, 0:1, :])
                    out[field, 1, z : z + 1, :] = edge.astype(f32)

    zb = z_weights.shape[1] // len(z_outs)
    for field, ref in enumerate((u_ref, v_ref)):
        for k, out in enumerate(z_outs):
            total = None
            for z in range(chunk):
                term = ref[0, z].astype(f32) * z_weights[info[1], k * zb + step * chunk + z]
                total = term if total is None else total + term

            @pl.when(step == 0)
            def _():
                out[field, 0] = total
                if out.shape[1] == 2:
                    out[field, 1] = ref[0, 0].astype(f32)

            @pl.when(step > 0)
            def _():
                out[field, 0] += total

            if out.shape[1] == 2:

                @pl.when((step == steps - 1) & (info[1] < len(z_outs) - k))
                def _():
                    out[field, 1] = ref[0, chunk - 1].astype(f32)


def edge_messages(info, velocity, y_weights, z_weights):
    _, zb, yb, nx = velocity.shape
    y_forms = message_forms(y_weights.shape[0])
    z_forms = message_forms(z_weights.shape[0])
    chunk = 8 if zb % 8 == 0 else zb
    piece = lambda f: pl.BlockSpec((1, chunk, yb, nx), lambda i, info: (f, i, 0, 0))
    y_spec = lambda near: pl.BlockSpec((2, 1 + near, chunk, nx), lambda i, info: (0, 0, i, 0))
    z_spec = lambda near: pl.BlockSpec((2, 1 + near, yb, nx), lambda i, info: (0, 0, 0, 0))
    outs = pl.pallas_call(
        edge_kernel,
        grid_spec=pltpu.PrefetchScalarGridSpec(
            num_scalar_prefetch=1,
            grid=(zb // chunk,),
            in_specs=[
                pl.BlockSpec((1,) + y_weights.shape[1:], lambda i, info: (info[0], 0, 0)),
                pl.BlockSpec(memory_space=pltpu.SMEM),
                piece(0),
                piece(1),
                piece(2),
            ],
            out_specs=[y_spec(near) for near in y_forms] + [z_spec(near) for near in z_forms],
        ),
        out_shape=[jax.ShapeDtypeStruct((2, 1 + near, zb, nx), f32) for near in y_forms]
        + [jax.ShapeDtypeStruct((2, 1 + near, yb, nx), f32) for near in z_forms],
        compiler_params=pltpu.CompilerParams(vmem_limit_bytes=VMEM_LIMIT),
        cost_estimate=pl.CostEstimate(
            flops=20 * zb * yb * nx, bytes_accessed=6 * zb * yb * nx, transcendentals=0
        ),
        name="edge_messages",
    )(info, y_weights, z_weights, velocity, velocity, velocity)
    return outs[: len(y_forms)], outs[len(y_forms) :]


def exchange(messages, axis):
    count = lax.axis_size(axis)
    out = []
    for k, message in enumerate(messages, 1):
        pairs = [(i, (i + k) % count) for i in range(count)]
        out.append(lax.ppermute(message, axis, pairs))
    return out


def slope_along_x(ref, tables, metric):
    chunk, yb, nx = ref.shape[1:]
    field = ref[0].reshape(chunk * yb, nx)
    high, low = tables
    slope = jnp.dot(field, high[...], preferred_element_type=f32)
    slope = slope + jnp.dot(field, low[...], preferred_element_type=f32)
    return (slope * metric[...]).reshape(chunk, yb, nx)


def slope_along_y(ref, z, table, columns, messages, metric):
    yb = ref.shape[2]
    both = jnp.dot(table[0], ref[0, z], preferred_element_type=f32)
    slope = both[:yb] + both[yb:]
    for k, message in enumerate(messages):
        slope = slope + columns[0, :, k : k + 1] * message[0, z : z + 1, :]
    last = len(messages)
    slope = slope + columns[0, :, last : last + 1] * messages[0][1, z : z + 1, :]
    slope = slope + columns[0, :, last + 1 : last + 2] * messages[-1][1, z : z + 1, :]
    return slope * metric[...]


def slopes_along_z(info, ref, scalars, messages, metric, out):
    _, zb, yb, nx = ref.shape
    rows, lanes = 16, 128
    across = nx // lanes
    block = info[1]
    last = len(messages)

    def tile(t, carry):
        ys = pl.ds(pl.multiple_of((t // across) * rows, rows), rows)
        xs = pl.ds(pl.multiple_of((t % across) * lanes, lanes), lanes)
        f = [ref[0, z, ys, xs].astype(f32) for z in range(zb)]
        scalar = lambda k: scalars[block, k]

        def rhs(z):
            total = None
            for step, weight in ((1, 7.0 / 9.0), (2, 1.0 / 36.0)):
                if z + step < zb and z - step >= 0:
                    term = (f[z + step] - f[z - step]) * weight
                elif z + step < zb:
                    term = f[z + step] * weight
                else:
                    term = f[z - step] * -weight
                total = term if total is None else total + term
            return total

        own = 4 * zb
        run = f[0] * scalar(own) + f[1] * scalar(own + 1)
        for k, message in enumerate(messages):
            run = run + message[0, 0, ys, xs] * scalar(own + 6 + k)
        forward = []
        for z in range(zb):
            run = run * -ratio + rhs(z) * scalar(z)
            forward.append(run)
        run = f[zb - 1] * scalar(own + 2) + f[zb - 2] * scalar(own + 3)
        for k, message in enumerate(messages):
            run = run + message[0, 0, ys, xs] * scalar(own + 6 + last + k)
        for z in reversed(range(zb)):
            run = run * -ratio
            slope = forward[z] * scalar(3 * zb + z) + run * scalar(2 * zb + z)
            run = run + rhs(z) * scalar(zb + z)
            if z == 0:
                slope = slope + messages[0][0, 1, ys, xs] * scalar(own + 4)
            if z == zb - 1:
                slope = slope + messages[-1][0, 1, ys, xs] * scalar(own + 5)
            out[z, ys, xs] = slope * metric[block * zb + z]
        return carry

    lax.fori_loop(0, (yb // rows) * across, tile, 0)


def hand_out(info, spin, outs):
    if len(outs) == 1:
        outs[0][...] = spin[...]
        return
    count = len(outs)
    rows, lanes = outs[0].shape[1:]
    for q, out in enumerate(outs):
        ys = pl.ds(pl.multiple_of(info[2 + q] * rows, rows), rows)
        xs = pl.ds(pl.multiple_of(info[2 + count + q] * lanes, lanes), lanes)
        out[...] = spin[:, ys, xs]


def spin_z_kernel(info, ways, v_ref, high, low, metric_x, u_ref, table, columns, *rest):
    messages, (metric_y, *outs, spin) = rest[: ways[0]], rest[ways[0] :]
    slope_vx = slope_along_x(v_ref, (high, low), metric_x).astype(bf16)
    for z in range(u_ref.shape[1]):
        slope_uy = slope_along_y(u_ref, z, table, columns, messages, metric_y)
        spin[z] = (slope_vx[z].astype(f32) - slope_uy).astype(bf16)
    hand_out(info, spin, outs)


def spin_y_kernel(info, ways, w_ref, high, low, metric_x, u_ref, scalars, *rest):
    messages, (metric_z, *outs, spin, slopes) = rest[: ways[1]], rest[ways[1] :]
    step = pl.program_id(0)
    chunk = w_ref.shape[1]

    @pl.when(step == 0)
    def _():
        slopes_along_z(info, u_ref, scalars, messages, metric_z, slopes)

    slope_wx = slope_along_x(w_ref, (high, low), metric_x).astype(bf16)
    for z in range(chunk):
        spin[z] = (slopes[step * chunk + z] - slope_wx[z].astype(f32)).astype(bf16)
    hand_out(info, spin, outs)


def spin_x_kernel(info, ways, w_ref, table, columns, *rest):
    y_messages, (metric_y, v_ref, scalars, *rest) = rest[: ways[0]], rest[ways[0] :]
    messages, (metric_z, *rest, spin, slopes) = rest[: ways[1]], rest[ways[1] :]
    outs = rest[len(rest) // 2 :]
    step = pl.program_id(0)
    chunk = w_ref.shape[1]

    @pl.when(step == 0)
    def _():
        slopes_along_z(info, v_ref, scalars, messages, metric_z, slopes)

    for z in range(chunk):
        slope_wy = slope_along_y(w_ref, z, table, columns, y_messages, metric_y).astype(bf16)
        spin[z] = (slope_wy.astype(f32) - slopes[step * chunk + z]).astype(bf16)
    hand_out(info, spin, outs)


def spin_call(kernel, info, velocity, groups, splits, flops, ways, name, slot=(0, 1), into=()):
    _, zb, yb, nx = velocity.shape
    row_parts, col_parts = splits
    chunk = largest_divisor(zb, 4)
    specs, args, scratch = [], [], [pltpu.VMEM((chunk, yb, nx), bf16)]
    whole = lambda a: pl.BlockSpec(a.shape, lambda i, info: (0,) * a.ndim)
    mine = lambda a: pl.BlockSpec((1,) + a.shape[1:], lambda i, info: (info[0],) + (0,) * (a.ndim - 1))
    smem = pl.BlockSpec(memory_space=pltpu.SMEM)

    def add(spec, arg):
        specs.append(spec)
        args.append(arg)

    for kind, field, *more in groups:
        if kind == "z":
            scalars, place, messages, metric = more
            add(pl.BlockSpec((1, zb, yb, nx), lambda i, info, field=field: (field, 0, 0, 0)), velocity)
            add(smem, scalars)
            for message in messages:
                add(
                    pl.BlockSpec(
                        (1,) + message.shape[1:], lambda i, info, place=place: (place, 0, 0, 0)
                    ),
                    message,
                )
            add(smem, metric)
            scratch.append(pltpu.VMEM((zb, yb, nx), f32))
            continue
        add(pl.BlockSpec((1, chunk, yb, nx), lambda i, info, field=field: (field, i, 0, 0)), velocity)
        if kind == "x":
            (high, low), metric = more
            add(whole(high), high)
            add(whole(low), low)
            add(whole(metric), metric)
        else:
            table, columns, place, messages, metric = more
            add(mine(table), table)
            add(mine(columns), columns)
            for message in messages:
                parts = message.shape[1]
                add(
                    pl.BlockSpec(
                        (None, parts, None, chunk, nx),
                        lambda i, info, place=place: (place, 0, i, 0, 0),
                    ),
                    message.reshape(2, parts, zb // chunk, chunk, nx),
                )
            add(pl.BlockSpec((yb, 1), lambda i, info: (info[0], 0)), metric)

    count = row_parts * col_parts
    block = (yb // row_parts, nx // col_parts)
    at, held = slot
    aliases = {}
    for q, buffer in enumerate(into):
        add(pl.BlockSpec(memory_space=pl.ANY), buffer)
        aliases[len(args)] = q
    return pl.pallas_call(
        lambda info, *refs: kernel(info, ways, *refs),
        grid_spec=pltpu.PrefetchScalarGridSpec(
            num_scalar_prefetch=1,
            grid=(zb // chunk,),
            in_specs=specs,
            out_specs=[pl.BlockSpec((None, chunk) + block, lambda i, info: (at, i, 0, 0))] * count,
            scratch_shapes=scratch,
        ),
        out_shape=[jax.ShapeDtypeStruct((held, zb) + block, bf16)] * count,
        input_output_aliases=aliases,
        compiler_params=pltpu.CompilerParams(vmem_limit_bytes=VMEM_LIMIT),
        cost_estimate=pl.CostEstimate(
            flops=flops, bytes_accessed=8 * zb * yb * nx, transcendentals=0
        ),
        name=name,
    )(info, *args)


def sketch_kernel(info, weights, *rest):
    count = weights.shape[0]
    fields = rest[:count]
    out = rest[-1]
    values = [field[...].astype(f32) for field in fields]
    for k in range(out.shape[0]):
        total = values[0] * weights[info[1], k]
        for r in range(1, count):
            total = total + values[r] * weights[info[1 + r], k]
        out[k] = total


def sketch_part(info, sketch_matrix, fields, total, component, shape):
    held, zb, rows, lanes = fields[0].shape
    rank = sketch_matrix.shape[1]
    chunk = largest_divisor(zb, 4)
    steps = zb // chunk
    piece = pl.BlockSpec((held, chunk, rows, lanes), lambda i, info: (0, i, 0, 0))
    specs = [pl.BlockSpec(memory_space=pltpu.SMEM)] + [piece] * len(fields)
    args = [sketch_matrix, *fields]
    aliases = {}
    if total is not None:
        specs.append(pl.BlockSpec(memory_space=pl.ANY))
        args.append(total)
        aliases = {len(args): 0}
    return pl.pallas_call(
        sketch_kernel,
        grid_spec=pltpu.PrefetchScalarGridSpec(
            num_scalar_prefetch=1,
            grid=(steps,),
            in_specs=specs,
            out_specs=pl.BlockSpec(
                (rank, held, chunk, rows, lanes),
                lambda i, info: (0, component // held, info[0] * steps + i, 0, 0),
            ),
        ),
        out_shape=jax.ShapeDtypeStruct(shape, f32),
        input_output_aliases=aliases,
        compiler_params=pltpu.CompilerParams(vmem_limit_bytes=VMEM_LIMIT),
        cost_estimate=pl.CostEstimate(
            flops=2 * rank * len(fields) * held * zb * rows * lanes,
            bytes_accessed=(2 * len(fields) + 4 * rank) * held * zb * rows * lanes,
            transcendentals=0,
        ),
        name="sketch_part",
    )(info, *args)


def col_rank(c, count):
    return (c % 2) * (count // 2) + c // 2 if count % 2 == 0 else c


def col_of_rank(t, count):
    return (t % (count // 2)) * 2 + t // (count // 2) if count % 2 == 0 else t


def routes(snaps, cols, depth):
    out = []
    place = lambda s, y, z: (s * cols + y) * depth + z
    for shift in range(depth):
        for turn in range(cols):
            first, second = [], []
            for s in range(snaps):
                for p in range(cols):
                    for z in range(depth):
                        c = col_of_rank((p - turn - s) % cols, cols)
                        first.append((place(s, p, z), place(s, c, z)))
                        second.append((place(s, c, z), place(p, c, (z + shift) % depth)))
            out.append((first, second))
    return out


def travel_order(count, ahead):
    steps = [(0, i) for i in range(min(ahead, count))]
    for i in range(count):
        steps.append((1, i))
        if i + ahead < count:
            steps.append((0, i + ahead))
    return steps


def after(x, *others):
    return lax.optimization_barrier((x, *others))[0]


def general_way(vorticity, sketch_matrix):
    lines = lax.all_to_all(vorticity, "py", split_axis=4, concat_axis=3, tiled=True)
    snap_count = lax.axis_size("snap")
    pz_count = lax.axis_size("pz")
    shape_now = lines.shape
    block_rows = shape_now[3] // (snap_count * pz_count)
    split_rows = lines.reshape(shape_now[:3] + (snap_count, pz_count, block_rows, shape_now[4]))
    reordered = jnp.swapaxes(split_rows, 3, 4).reshape(shape_now)
    lines = lax.all_to_all(reordered, "pz", split_axis=3, concat_axis=2, tiled=True)
    lines = lax.all_to_all(lines, "snap", split_axis=3, concat_axis=0, tiled=True)
    return jnp.einsum(
        "sk,sczyx->kczyx", sketch_matrix, lines.astype(f32), precision=lax.Precision.HIGHEST
    )


def on_device(velocity, metric_x, metric_y, metric_z, sketch_matrix):
    snaps, cols, depth = (lax.axis_size(name) for name in ("snap", "py", "pz"))
    s, p, z = (lax.axis_index(name) for name in ("snap", "py", "pz"))
    _, _, zb, yb, nx = velocity.shape
    ny, nz = yb * cols, zb * depth
    velocity = velocity[0]
    direct = snaps == cols
    messages = [(shift, turn) for shift in range(depth) for turn in range(cols)]

    tables_x = [jnp.asarray(t) for t in split_table(line_table(nx, 0, nx).T)]
    tables_y = per_block(line_table, ny, cols)
    tables_y = jnp.asarray(np.concatenate(split_table(tables_y), axis=1))
    columns_y = jnp.asarray(per_block(message_columns, ny, cols), f32)
    weights_y = split_table(per_block(message_weights, ny, cols))
    weights_y = jnp.asarray(np.concatenate(weights_y, axis=1))
    weights_z = jnp.asarray(per_block(message_weights, nz, depth).reshape(depth, -1), f32)
    scalars_z = jnp.asarray(per_block(sweep_scalars, nz, depth), f32)
    metric_x = metric_x.reshape(1, nx)
    metric_y = metric_y.reshape(ny, 1)

    where = [p, z]
    if direct:
        where += [(z + shift) % depth for shift, turn in messages]
        where += [col_of_rank((p - turn - s) % cols, cols) for shift, turn in messages]
    info = jnp.stack(where).astype(jnp.int32)
    splits = (depth, cols) if direct else (1, 1)

    y_edges, z_edges = edge_messages(info, velocity, weights_y, weights_z)
    y_edges, z_edges = exchange(y_edges, "py"), exchange(z_edges, "pz")

    points = zb * yb * nx
    along_x = lambda field: ("x", field, tables_x, metric_x)
    along_y = lambda field, place: ("y", field, tables_y, columns_y, place, y_edges, metric_y)
    along_z = lambda field: ("z", field, scalars_z, field, z_edges, metric_z)
    call = functools.partial(spin_call, splits=splits, ways=(cols - 1, depth - 1))
    spins = {}
    spins[2] = call(
        spin_z_kernel, info, velocity, [along_x(1), along_y(0, 0)],
        flops=points * 4 * (nx + yb), name="spin_z",
    )
    pair = call(
        spin_y_kernel, info, velocity, [along_x(2), along_z(0)],
        flops=points * (4 * nx + 20), name="spin_y", slot=(1, 2),
    )

    def with_spin_x(pair, info):
        return call(
            spin_x_kernel, info, velocity, [along_y(2, 1), along_z(1)],
            flops=points * (4 * yb + 20), name="spin_x", slot=(0, 2), into=pair,
        )

    if not direct:
        pair = with_spin_x(pair, info)
        vorticity = jnp.concatenate([pair[0], spins[2][0]])[None]
        return general_way(vorticity, sketch_matrix)

    all_routes = routes(snaps, cols, depth)
    everywhere = ("snap", "py", "pz")
    count = len(all_routes)
    parts = list(spins[2])
    ahead, first_flight, second_flight = cols, 2, 3
    arrived = {}
    for hop, i in travel_order(2 * count, ahead):
        if (hop, i) == (0, count):
            parts += with_spin_x(pair, after(info, arrived[1, count - ahead - second_flight + 1]))
        sent = parts[i] if hop == 0 else arrived[0, i]
        behind = [(1, i - second_flight)]
        if hop == 0:
            behind = [(0, i - first_flight)] if i >= ahead else []
            behind.append((1, i - ahead - second_flight + 1))
        behind = [arrived[key] for key in behind if key[1] >= 0]
        if (hop, i) == (1, count // 2):
            behind.append(pair[0])
        if behind:
            sent = after(sent, *behind)
        arrived[hop, i] = lax.ppermute(sent, everywhere, all_routes[i % count][hop])

    shape = (sketch_matrix.shape[1], 3, nz, yb // depth, nx // cols)
    my_rank = col_rank(p, cols)
    total = None
    for place, component in enumerate((2, 0)):
        for shift in range(depth):
            whence = [(z - shift) % depth]
            whence += [(s - turn - my_rank) % snaps for turn in range(cols)]
            begin = place * count + shift * cols
            total = sketch_part(
                jnp.stack(whence).astype(jnp.int32),
                sketch_matrix,
                [arrived[1, i] for i in range(begin, begin + cols)],
                total,
                component,
                shape,
            )
    return total


def solution(mesh):
    placed = (P("snap", None, "pz", "py", None), P(), P(), P(), P())
    return jax.shard_map(
        on_device,
        mesh=mesh,
        in_specs=placed,
        out_specs=P(None, None, None, ("snap", "pz"), "py"),
        check_vma=False,
    )
```

```python
import functools

import jax
import jax.numpy as jnp
import ml_dtypes
import numpy as np
from jax import lax
from jax.experimental import pallas as pl
from jax.experimental.pallas import tpu as pltpu
from jax.sharding import PartitionSpec as P

ratio = (3.0 - 5.0**0.5) / 2.0
VMEM_LIMIT = 52 * 1024 * 1024
f32 = jnp.float32
bf16 = jnp.bfloat16


def lead(i):
    return 1.0 - ratio ** (2.0 * (np.asarray(i, np.float64) + 1.0))


def trail(i, n):
    return 1.0 - ratio ** (2.0 * (n - np.asarray(i, np.float64)))


def denom(n):
    return 5.0**0.5 / 3.0 * (1.0 - ratio ** (2.0 * (n + 1.0)))


def inverse_entry(row, col, n):
    inside = (col >= 0) & (col < n)
    col = np.clip(col, 0, n - 1)
    near, far = np.minimum(row, col), np.maximum(row, col)
    sign = 1.0 - 2.0 * ((far - near) % 2)
    value = sign * ratio ** (far - near).astype(np.float64) * lead(near) * trail(far, n) / denom(n)
    return np.where(inside, value, 0.0)


def line_table(n, start, size):
    row = start + np.arange(size)[:, None]
    col = start + np.arange(size)[None, :]
    entry = functools.partial(inverse_entry, row, n=n)
    first = entry(col - 1) - entry(col + 1)
    second = entry(col - 2) - entry(col + 2)
    return 7.0 / 9.0 * first + 1.0 / 36.0 * second


def split_table(table):
    high = table.astype(ml_dtypes.bfloat16)
    low = (table - high.astype(np.float64)).astype(ml_dtypes.bfloat16)
    return high, low


def edge_weights(n, start, size):
    last = start + size - 1
    j = start + np.arange(size)

    def forward(k):
        return np.where(k >= 0, (-ratio) ** (last - k).astype(np.float64) * lead(k), 0.0)

    def backward(k):
        return np.where(k <= n - 1, (-ratio) ** (k - start).astype(np.float64) * trail(k, n), 0.0)

    def weights(c):
        return 7.0 / 9.0 * (c(j - 1) - c(j + 1)) + 1.0 / 36.0 * (c(j - 2) - c(j + 2))

    return weights(forward), weights(backward)


def edge_columns(n, start, size):
    i = start + np.arange(size)
    left = (-ratio) ** (i - start + 1.0) * trail(i, n) / denom(n)
    right = (-ratio) ** (start + size - i).astype(np.float64) * lead(i) / denom(n)
    return left, right


def message_weights(n, start, size):
    count, block = n // size, start // size
    right, left = edge_weights(n, start, size)
    return np.stack([right if block < count - k else left for k in range(1, count)])


def message_shares(n, start, size):
    count, block = n // size, start // size
    decay = (-ratio) ** size
    left = [decay ** (k - 1) if block >= k else 0.0 for k in range(1, count)]
    right = [decay ** (count - k - 1) if block < k else 0.0 for k in range(1, count)]
    corner = [-1.0 / 12.0 if block > 0 else 0.0, 1.0 / 12.0 if block < count - 1 else 0.0]
    return np.array(left), np.array(right), np.array(corner)


def message_columns(n, start, size):
    left, right = edge_columns(n, start, size)
    share_left, share_right, corner = message_shares(n, start, size)
    corners = np.zeros((size, 2))
    corners[0, 0], corners[-1, 1] = corner
    return np.concatenate([np.outer(left, share_left) + np.outer(right, share_right), corners], axis=1)


def sweep_scalars(n, start, size):
    i = start + np.arange(size)
    after = start + size
    own_left = [0.0, 0.0]
    own_right = [0.0, 0.0]
    if start > 0:
        own_left = [7.0 / 9.0 * lead(start - 1) - ratio / 36.0 * lead(start - 2), lead(start - 1) / 36.0]
    if after < n:
        own_right = [
            -7.0 / 9.0 * trail(after, n) + ratio / 36.0 * trail(after + 1, n),
            -trail(after, n) / 36.0,
        ]
    rows = [lead(i), trail(i, n), lead(i) / denom(n), trail(i, n) / denom(n)]
    share_left, share_right, corner = message_shares(n, start, size)
    return np.concatenate(rows + [np.array(own_left + own_right), corner, share_left, share_right])


def per_block(make, n, count):
    size = n // count
    return np.stack([make(n, block * size, size) for block in range(count)])


def largest_divisor(size, most):
    return max(d for d in range(1, most + 1) if size % d == 0)


def message_forms(count):
    return [k in (1, count - 1) for k in range(1, count)]


def edge_kernel(info, y_weights, z_weights, *refs, y_count, z_count):
    step, steps = pl.program_id(0), pl.num_programs(0)
    y_refs, z_refs, outs = refs[:y_count], refs[y_count : y_count + z_count], refs[y_count + z_count :]
    chunk, yb, _ = y_refs[0].shape[1:]
    ways = y_weights.shape[1] // 2
    y_outs, z_outs = outs[:ways], outs[ways:]
    for field, ref in enumerate(y_refs):
        for z in range(chunk):
            sums = jnp.dot(y_weights[0], ref[0, z], preferred_element_type=f32)
            sums = sums[:ways] + sums[ways:]
            for k, out in enumerate(y_outs):
                out[field, 0, z, :] = sums[k]
                if out.shape[1] == 2:
                    edge = jnp.where(info[0] < ways - k, ref[0, z, yb - 1 :, :], ref[0, z, 0:1, :])
                    out[field, 1, z : z + 1, :] = edge.astype(f32)
    if not z_refs:
        return

    zb = z_weights.shape[1] // len(z_outs)
    for field, ref in enumerate(z_refs):
        for k, out in enumerate(z_outs):
            total = None
            for z in range(chunk):
                term = ref[0, z].astype(f32) * z_weights[info[1], k * zb + step * chunk + z]
                total = term if total is None else total + term

            @pl.when(step == 0)
            def _():
                out[field, 0] = total
                if out.shape[1] == 2:
                    out[field, 1] = ref[0, 0].astype(f32)

            @pl.when(step > 0)
            def _():
                out[field, 0] += total

            if out.shape[1] == 2:

                @pl.when((step == steps - 1) & (info[1] < len(z_outs) - k))
                def _():
                    out[field, 1] = ref[0, chunk - 1].astype(f32)


def edge_messages(info, velocity, y_weights, z_weights, y_fields, z_fields):
    _, zb, yb, nx = velocity.shape
    y_forms = message_forms(y_weights.shape[0])
    z_forms = message_forms(z_weights.shape[0]) if z_fields else []
    chunk = 8 if zb % 8 == 0 else zb
    fields = y_fields + z_fields
    in_y, in_z = len(y_fields), len(z_fields)
    piece = lambda f: pl.BlockSpec((1, chunk, yb, nx), lambda i, info: (f, i, 0, 0))
    y_spec = lambda near: pl.BlockSpec((in_y, 1 + near, chunk, nx), lambda i, info: (0, 0, i, 0))
    z_spec = lambda near: pl.BlockSpec((in_z, 1 + near, yb, nx), lambda i, info: (0, 0, 0, 0))
    outs = pl.pallas_call(
        functools.partial(edge_kernel, y_count=in_y, z_count=in_z),
        grid_spec=pltpu.PrefetchScalarGridSpec(
            num_scalar_prefetch=1,
            grid=(zb // chunk,),
            in_specs=[
                pl.BlockSpec((1,) + y_weights.shape[1:], lambda i, info: (info[0], 0, 0)),
                pl.BlockSpec(memory_space=pltpu.SMEM),
                *[piece(f) for f in fields],
            ],
            out_specs=[y_spec(near) for near in y_forms] + [z_spec(near) for near in z_forms],
        ),
        out_shape=[jax.ShapeDtypeStruct((in_y, 1 + near, zb, nx), f32) for near in y_forms]
        + [jax.ShapeDtypeStruct((in_z, 1 + near, yb, nx), f32) for near in z_forms],
        compiler_params=pltpu.CompilerParams(vmem_limit_bytes=VMEM_LIMIT),
        cost_estimate=pl.CostEstimate(
            flops=6 * len(fields) * zb * yb * nx,
            bytes_accessed=2 * len(fields) * zb * yb * nx,
            transcendentals=0,
        ),
        name="edge_messages",
    )(info, y_weights, z_weights, *[velocity] * len(fields))
    return outs[: len(y_forms)], outs[len(y_forms) :]


def exchange(messages, axis):
    count = lax.axis_size(axis)
    out = []
    for k, message in enumerate(messages, 1):
        pairs = [(i, (i + k) % count) for i in range(count)]
        out.append(lax.ppermute(message, axis, pairs))
    return out


def slope_along_x(ref, tables, metric):
    chunk, yb, nx = ref.shape[1:]
    field = ref[0].reshape(chunk * yb, nx)
    high, low = tables
    slope = jnp.dot(field, high[...], preferred_element_type=f32)
    slope = slope + jnp.dot(field, low[...], preferred_element_type=f32)
    return (slope * metric[...]).reshape(chunk, yb, nx)


def slope_along_y(ref, z, table, columns, messages, metric):
    rows = table.shape[1] // 2
    both = jnp.dot(table[0], ref[0, z], preferred_element_type=f32)
    slope = both[:rows] + both[rows:]
    for k, message in enumerate(messages):
        slope = slope + columns[0, :, k : k + 1] * message[0, z : z + 1, :]
    last = len(messages)
    slope = slope + columns[0, :, last : last + 1] * messages[0][1, z : z + 1, :]
    slope = slope + columns[0, :, last + 1 : last + 2] * messages[-1][1, z : z + 1, :]
    return slope * metric[...]


def slopes_along_z(info, ref, scalars, messages, metric, out):
    _, zb, yb, nx = ref.shape
    rows, lanes = 16, 128
    across = nx // lanes
    block = info[1]
    last = len(messages)

    def tile(t, carry):
        ys = pl.ds(pl.multiple_of((t // across) * rows, rows), rows)
        xs = pl.ds(pl.multiple_of((t % across) * lanes, lanes), lanes)
        f = [ref[0, z, ys, xs].astype(f32) for z in range(zb)]
        scalar = lambda k: scalars[block, k]

        def rhs(z):
            total = None
            for step, weight in ((1, 7.0 / 9.0), (2, 1.0 / 36.0)):
                if z + step < zb and z - step >= 0:
                    term = (f[z + step] - f[z - step]) * weight
                elif z + step < zb:
                    term = f[z + step] * weight
                else:
                    term = f[z - step] * -weight
                total = term if total is None else total + term
            return total

        own = 4 * zb
        run = f[0] * scalar(own) + f[1] * scalar(own + 1)
        for k, message in enumerate(messages):
            run = run + message[0, 0, ys, xs] * scalar(own + 6 + k)
        forward = []
        for z in range(zb):
            run = run * -ratio + rhs(z) * scalar(z)
            forward.append(run)
        run = f[zb - 1] * scalar(own + 2) + f[zb - 2] * scalar(own + 3)
        for k, message in enumerate(messages):
            run = run + message[0, 0, ys, xs] * scalar(own + 6 + last + k)
        for z in reversed(range(zb)):
            run = run * -ratio
            slope = forward[z] * scalar(3 * zb + z) + run * scalar(2 * zb + z)
            run = run + rhs(z) * scalar(zb + z)
            if z == 0:
                slope = slope + messages[0][0, 1, ys, xs] * scalar(own + 4)
            if z == zb - 1:
                slope = slope + messages[-1][0, 1, ys, xs] * scalar(own + 5)
            out[z, ys, xs] = slope * metric[block * zb + z]
        return carry

    lax.fori_loop(0, (yb // rows) * across, tile, 0)


def hand_out(info, spin, outs):
    if len(outs) == 1:
        outs[0][...] = spin[...]
        return
    count = len(outs)
    rows, lanes = outs[0].shape[1:]
    for q, out in enumerate(outs):
        ys = pl.ds(pl.multiple_of(info[2 + q] * rows, rows), rows)
        xs = pl.ds(pl.multiple_of(info[2 + count + q] * lanes, lanes), lanes)
        out[...] = spin[:, ys, xs]


def spin_z_kernel(info, ways, v_ref, high, low, metric_x, u_ref, table, columns, *rest):
    messages, (metric_y, *outs, spin) = rest[: ways[0]], rest[ways[0] :]
    slope_vx = slope_along_x(v_ref, (high, low), metric_x).astype(bf16)
    for z in range(u_ref.shape[1]):
        slope_uy = slope_along_y(u_ref, z, table, columns, messages, metric_y)
        spin[z] = (slope_vx[z].astype(f32) - slope_uy).astype(bf16)
    hand_out(info, spin, outs)


def spin_y_kernel(info, ways, w_ref, high, low, metric_x, u_ref, scalars, *rest):
    messages, (metric_z, *outs, spin, slopes) = rest[: ways[1]], rest[ways[1] :]
    step = pl.program_id(0)
    chunk = w_ref.shape[1]

    @pl.when(step == 0)
    def _():
        slopes_along_z(info, u_ref, scalars, messages, metric_z, slopes)

    slope_wx = slope_along_x(w_ref, (high, low), metric_x).astype(bf16)
    for z in range(chunk):
        spin[z] = (slopes[step * chunk + z] - slope_wx[z].astype(f32)).astype(bf16)
    hand_out(info, spin, outs)


def spin_x_kernel(info, ways, w_ref, table, columns, *rest):
    y_messages, (metric_y, v_ref, scalars, *rest) = rest[: ways[0]], rest[ways[0] :]
    messages, (metric_z, *rest, spin, slopes) = rest[: ways[1]], rest[ways[1] :]
    outs = rest[len(rest) // 2 :]
    step = pl.program_id(0)
    chunk = w_ref.shape[1]

    @pl.when(step == 0)
    def _():
        slopes_along_z(info, v_ref, scalars, messages, metric_z, slopes)

    for z in range(chunk):
        slope_wy = slope_along_y(w_ref, z, table, columns, y_messages, metric_y).astype(bf16)
        spin[z] = (slope_wy.astype(f32) - slopes[step * chunk + z]).astype(bf16)
    hand_out(info, spin, outs)


def spin_call(kernel, info, velocity, groups, splits, flops, ways, name, slot=(0, 1), into=(), cut=1):
    _, zb, yb, nx = velocity.shape
    row_parts, col_parts = splits
    rows = yb // cut
    chunk = largest_divisor(zb, 4 if cut == 1 else 8)
    specs, args, scratch = [], [], [pltpu.VMEM((chunk, rows, nx), bf16)]
    at_row = lambda info: info[info.shape[0] - 1] if cut > 1 else 0
    whole = lambda a: pl.BlockSpec(a.shape, lambda i, info: (0,) * a.ndim)
    mine = lambda a: pl.BlockSpec(
        (1,) + a.shape[1:], lambda i, info: (info[0] * cut + at_row(info),) + (0,) * (a.ndim - 1)
    )
    smem = pl.BlockSpec(memory_space=pltpu.SMEM)

    def add(spec, arg):
        specs.append(spec)
        args.append(arg)

    for kind, field, *more in groups:
        if kind == "z":
            scalars, place, messages, metric = more
            add(pl.BlockSpec((1, zb, yb, nx), lambda i, info, field=field: (field, 0, 0, 0)), velocity)
            add(smem, scalars)
            for message in messages:
                add(
                    pl.BlockSpec(
                        (1,) + message.shape[1:], lambda i, info, place=place: (place, 0, 0, 0)
                    ),
                    message,
                )
            add(smem, metric)
            scratch.append(pltpu.VMEM((zb, yb, nx), f32))
            continue
        if kind == "x":
            add(
                pl.BlockSpec(
                    (1, chunk, rows, nx), lambda i, info, field=field: (field, i, at_row(info), 0)
                ),
                velocity,
            )
            (high, low), metric = more
            add(whole(high), high)
            add(whole(low), low)
            add(whole(metric), metric)
        else:
            table, columns, messages, metric = more
            table = table.reshape(table.shape[0], 2, cut, rows, yb).swapaxes(1, 2)
            table = jnp.asarray(table.reshape(-1, 2 * rows, yb))
            columns = jnp.asarray(columns.reshape(-1, rows, columns.shape[2]), f32)
            add(pl.BlockSpec((1, chunk, yb, nx), lambda i, info, field=field: (field, i, 0, 0)), velocity)
            add(mine(table), table)
            add(mine(columns), columns)
            for message in messages:
                parts = message.shape[1]
                add(
                    pl.BlockSpec((None, parts, None, chunk, nx), lambda i, info: (0, 0, i, 0, 0)),
                    message.reshape(1, parts, zb // chunk, chunk, nx),
                )
            add(pl.BlockSpec((rows, 1), lambda i, info: (info[0] * cut + at_row(info), 0)), metric)

    count = row_parts * col_parts
    block = (rows // row_parts, nx // col_parts)
    at, held = slot
    aliases = {}
    for q, buffer in enumerate(into):
        add(pl.BlockSpec(memory_space=pl.ANY), buffer)
        aliases[len(args)] = q
    return pl.pallas_call(
        lambda info, *refs: kernel(info, ways, *refs),
        grid_spec=pltpu.PrefetchScalarGridSpec(
            num_scalar_prefetch=1,
            grid=(zb // chunk,),
            in_specs=specs,
            out_specs=[pl.BlockSpec((None, chunk) + block, lambda i, info: (at, i, 0, 0))] * count,
            scratch_shapes=scratch,
        ),
        out_shape=[jax.ShapeDtypeStruct((held, zb) + block, bf16)] * count,
        input_output_aliases=aliases,
        compiler_params=pltpu.CompilerParams(vmem_limit_bytes=VMEM_LIMIT),
        cost_estimate=pl.CostEstimate(
            flops=flops, bytes_accessed=8 * zb * rows * nx, transcendentals=0
        ),
        name=name,
    )(info, *args)


def sketch_kernel(info, weights, *rest):
    count = weights.shape[0]
    fields = rest[:count]
    out = rest[-1]
    values = [field[...].astype(f32) for field in fields]
    for k in range(out.shape[0]):
        total = values[0] * weights[info[1], k]
        for r in range(1, count):
            total = total + values[r] * weights[info[1 + r], k]
        out[k] = total


def sketch_part(info, sketch_matrix, fields, total, component, shape):
    held, zb, rows, lanes = fields[0].shape
    rank = sketch_matrix.shape[1]
    chunk = largest_divisor(zb, 4)
    steps = zb // chunk
    piece = pl.BlockSpec((held, chunk, rows, lanes), lambda i, info: (0, i, 0, 0))
    specs = [pl.BlockSpec(memory_space=pltpu.SMEM)] + [piece] * len(fields)
    args = [sketch_matrix, *fields]
    aliases = {}
    if total is not None:
        specs.append(pl.BlockSpec(memory_space=pl.ANY))
        args.append(total)
        aliases = {len(args): 0}
    return pl.pallas_call(
        sketch_kernel,
        grid_spec=pltpu.PrefetchScalarGridSpec(
            num_scalar_prefetch=1,
            grid=(steps,),
            in_specs=specs,
            out_specs=pl.BlockSpec(
                (rank, held, chunk, rows, lanes),
                lambda i, info: (0, component // held, info[0] * steps + i, 0, 0),
            ),
        ),
        out_shape=jax.ShapeDtypeStruct(shape, f32),
        input_output_aliases=aliases,
        compiler_params=pltpu.CompilerParams(vmem_limit_bytes=VMEM_LIMIT),
        cost_estimate=pl.CostEstimate(
            flops=2 * rank * len(fields) * held * zb * rows * lanes,
            bytes_accessed=(2 * len(fields) + 4 * rank) * held * zb * rows * lanes,
            transcendentals=0,
        ),
        name="sketch_part",
    )(info, *args)


def col_rank(c, count):
    return (c % 2) * (count // 2) + c // 2 if count % 2 == 0 else c


def col_of_rank(t, count):
    return (t % (count // 2)) * 2 + t // (count // 2) if count % 2 == 0 else t


def routes(snaps, cols, depth):
    out = []
    place = lambda s, y, z: (s * cols + y) * depth + z
    for shift in range(depth):
        for turn in range(cols):
            first, second = [], []
            for s in range(snaps):
                for p in range(cols):
                    for z in range(depth):
                        c = col_of_rank((p - turn - s) % cols, cols)
                        first.append((place(s, p, z), place(s, c, z)))
                        second.append((place(s, c, z), place(p, c, (z + shift) % depth)))
            out.append((first, second))
    return out


def travel_order(count, ahead):
    steps = [(0, i) for i in range(min(ahead, count))]
    for i in range(count):
        steps.append((1, i))
        if i + ahead < count:
            steps.append((0, i + ahead))
    return steps


def after(x, *others):
    return lax.optimization_barrier((x, *others))[0]


def general_way(vorticity, sketch_matrix):
    lines = lax.all_to_all(vorticity, "py", split_axis=4, concat_axis=3, tiled=True)
    snap_count = lax.axis_size("snap")
    pz_count = lax.axis_size("pz")
    shape_now = lines.shape
    block_rows = shape_now[3] // (snap_count * pz_count)
    split_rows = lines.reshape(shape_now[:3] + (snap_count, pz_count, block_rows, shape_now[4]))
    reordered = jnp.swapaxes(split_rows, 3, 4).reshape(shape_now)
    lines = lax.all_to_all(reordered, "pz", split_axis=3, concat_axis=2, tiled=True)
    lines = lax.all_to_all(lines, "snap", split_axis=3, concat_axis=0, tiled=True)
    return jnp.einsum(
        "sk,sczyx->kczyx", sketch_matrix, lines.astype(f32), precision=lax.Precision.HIGHEST
    )


def on_device(velocity, metric_x, metric_y, metric_z, sketch_matrix):
    snaps, cols, depth = (lax.axis_size(name) for name in ("snap", "py", "pz"))
    s, p, z = (lax.axis_index(name) for name in ("snap", "py", "pz"))
    _, _, zb, yb, nx = velocity.shape
    ny, nz = yb * cols, zb * depth
    velocity = velocity[0]
    direct = snaps == cols
    messages = [(shift, turn) for shift in range(depth) for turn in range(cols)]

    tables_x = [jnp.asarray(t) for t in split_table(line_table(nx, 0, nx).T)]
    tables_y = per_block(line_table, ny, cols)
    tables_y = np.concatenate(split_table(tables_y), axis=1)
    columns_y = per_block(message_columns, ny, cols)
    weights_y = split_table(per_block(message_weights, ny, cols))
    weights_y = jnp.asarray(np.concatenate(weights_y, axis=1))
    weights_z = jnp.asarray(per_block(message_weights, nz, depth).reshape(depth, -1), f32)
    scalars_z = jnp.asarray(per_block(sweep_scalars, nz, depth), f32)
    metric_x = metric_x.reshape(1, nx)
    metric_y = metric_y.reshape(ny, 1)

    rows_to = [(z + shift) % depth for shift, turn in messages]
    cols_to = [col_of_rank((p - turn - s) % cols, cols) for shift, turn in messages]
    pack = lambda *items: jnp.stack(items).astype(jnp.int32)
    info = pack(p, z, *rows_to, *cols_to) if direct else pack(p, z)

    weights = (weights_y, weights_z)
    u_edges, _ = edge_messages(info, velocity, *weights, (0,), ())
    u_edges = exchange(u_edges, "py")
    w_edges, z_edges = edge_messages(info, velocity, *weights, (2,), (0, 1))

    points = zb * yb * nx
    along_x = lambda field: ("x", field, tables_x, metric_x)
    along_y = lambda field, edges: ("y", field, tables_y, columns_y, edges, metric_y)
    along_z = lambda field: ("z", field, scalars_z, field, z_edges, metric_z)
    splits = (depth, cols) if direct else (1, 1)
    call = functools.partial(spin_call, ways=(cols - 1, depth - 1))
    spin_z = []
    for shift in range(depth if direct else 1):
        mine = slice(shift * cols, (shift + 1) * cols)
        spin_z += call(
            spin_z_kernel,
            pack(p, z, *[0 * z] * cols, *cols_to[mine], rows_to[mine][0]) if direct else info,
            velocity,
            [along_x(1), along_y(0, u_edges)],
            splits=(1, cols) if direct else (1, 1),
            flops=points * 4 * (nx + yb) // (depth if direct else 1),
            name="spin_z",
            cut=depth if direct else 1,
        )
    w_edges = exchange([after(m, spin_z[0]) for m in w_edges], "py")
    z_edges = exchange([after(m, spin_z[0]) for m in z_edges], "pz")
    pair = call(
        spin_y_kernel, after(info, *w_edges), velocity, [along_x(2), along_z(0)],
        flops=points * (4 * nx + 20), name="spin_y", slot=(1, 2), splits=splits,
    )

    def with_spin_x(pair, info):
        return call(
            spin_x_kernel, info, velocity, [along_y(2, w_edges), along_z(1)],
            flops=points * (4 * yb + 20), name="spin_x", slot=(0, 2), into=pair, splits=splits,
        )

    if not direct:
        pair = with_spin_x(pair, info)
        vorticity = jnp.concatenate([pair[0], spin_z[0]])[None]
        return general_way(vorticity, sketch_matrix)

    all_routes = routes(snaps, cols, depth)
    everywhere = ("snap", "py", "pz")
    count = len(all_routes)
    parts = list(spin_z)
    ahead, first_flight, second_flight = cols, 2, 3
    arrived = {}
    for hop, i in travel_order(2 * count, ahead):
        if (hop, i) == (0, count):
            parts += with_spin_x(pair, after(info, arrived[1, 0]))
        sent = parts[i] if hop == 0 else arrived[0, i]
        behind = [(1, i - second_flight)]
        if hop == 0:
            behind = [(0, i - first_flight)] if i >= ahead else []
            behind.append((1, i - ahead - second_flight + 1))
        behind = [arrived[key] for key in behind if key[1] >= 0]
        if (hop, i) == (1, count // 4):
            behind.append(pair[0])
        if (hop, i) == (1, count // 2 + 1):
            behind.append(parts[count])
        if behind:
            sent = after(sent, *behind)
        arrived[hop, i] = lax.ppermute(sent, everywhere, all_routes[i % count][hop])

    shape = (sketch_matrix.shape[1], 3, nz, yb // depth, nx // cols)
    my_rank = col_rank(p, cols)
    total = None
    for place, component in enumerate((2, 0)):
        for shift in range(depth):
            whence = [(z - shift) % depth]
            whence += [(s - turn - my_rank) % snaps for turn in range(cols)]
            begin = place * count + shift * cols
            total = sketch_part(
                jnp.stack(whence).astype(jnp.int32),
                sketch_matrix,
                [arrived[1, i] for i in range(begin, begin + cols)],
                total,
                component,
                shape,
            )
    return total


def solution(mesh):
    placed = (P("snap", None, "pz", "py", None), P(), P(), P(), P())
    return jax.shard_map(
        on_device,
        mesh=mesh,
        in_specs=placed,
        out_specs=P(None, None, None, ("snap", "pz"), "py"),
        check_vma=False,
    )
```

```python
import functools

import jax
import jax.numpy as jnp
import ml_dtypes
import numpy as np
from jax import lax
from jax.experimental import pallas as pl
from jax.experimental.pallas import tpu as pltpu
from jax.sharding import PartitionSpec as P

ratio = (3.0 - 5.0**0.5) / 2.0
VMEM_LIMIT = 52 * 1024 * 1024
light = pl.CostEstimate(flops=1024, bytes_accessed=1024, transcendentals=0)
f32 = jnp.float32
bf16 = jnp.bfloat16


def lead(i):
    return 1.0 - ratio ** (2.0 * (np.asarray(i, np.float64) + 1.0))


def trail(i, n):
    return 1.0 - ratio ** (2.0 * (n - np.asarray(i, np.float64)))


def denom(n):
    return 5.0**0.5 / 3.0 * (1.0 - ratio ** (2.0 * (n + 1.0)))


def inverse_entry(row, col, n):
    inside = (col >= 0) & (col < n)
    col = np.clip(col, 0, n - 1)
    near, far = np.minimum(row, col), np.maximum(row, col)
    sign = 1.0 - 2.0 * ((far - near) % 2)
    value = sign * ratio ** (far - near).astype(np.float64) * lead(near) * trail(far, n) / denom(n)
    return np.where(inside, value, 0.0)


def line_table(n, start, size):
    row = start + np.arange(size)[:, None]
    col = start + np.arange(size)[None, :]
    entry = functools.partial(inverse_entry, row, n=n)
    first = entry(col - 1) - entry(col + 1)
    second = entry(col - 2) - entry(col + 2)
    return 7.0 / 9.0 * first + 1.0 / 36.0 * second


def split_table(table):
    high = table.astype(ml_dtypes.bfloat16)
    low = (table - high.astype(np.float64)).astype(ml_dtypes.bfloat16)
    return high, low


def edge_weights(n, start, size):
    last = start + size - 1
    j = start + np.arange(size)

    def forward(k):
        return np.where(k >= 0, (-ratio) ** (last - k).astype(np.float64) * lead(k), 0.0)

    def backward(k):
        return np.where(k <= n - 1, (-ratio) ** (k - start).astype(np.float64) * trail(k, n), 0.0)

    def weights(c):
        return 7.0 / 9.0 * (c(j - 1) - c(j + 1)) + 1.0 / 36.0 * (c(j - 2) - c(j + 2))

    return weights(forward), weights(backward)


def edge_columns(n, start, size):
    i = start + np.arange(size)
    left = (-ratio) ** (i - start + 1.0) * trail(i, n) / denom(n)
    right = (-ratio) ** (start + size - i).astype(np.float64) * lead(i) / denom(n)
    return left, right


def message_weights(n, start, size):
    count, block = n // size, start // size
    right, left = edge_weights(n, start, size)
    return np.stack([right if block < count - k else left for k in range(1, count)])


def message_shares(n, start, size):
    count, block = n // size, start // size
    decay = (-ratio) ** size
    left = [decay ** (k - 1) if block >= k else 0.0 for k in range(1, count)]
    right = [decay ** (count - k - 1) if block < k else 0.0 for k in range(1, count)]
    corner = [-1.0 / 12.0 if block > 0 else 0.0, 1.0 / 12.0 if block < count - 1 else 0.0]
    return np.array(left), np.array(right), np.array(corner)


def message_columns(n, start, size):
    left, right = edge_columns(n, start, size)
    share_left, share_right, corner = message_shares(n, start, size)
    corners = np.zeros((size, 2))
    corners[0, 0], corners[-1, 1] = corner
    return np.concatenate([np.outer(left, share_left) + np.outer(right, share_right), corners], axis=1)


def sweep_scalars(n, start, size):
    i = start + np.arange(size)
    after = start + size
    own_left = [0.0, 0.0]
    own_right = [0.0, 0.0]
    if start > 0:
        own_left = [7.0 / 9.0 * lead(start - 1) - ratio / 36.0 * lead(start - 2), lead(start - 1) / 36.0]
    if after < n:
        own_right = [
            -7.0 / 9.0 * trail(after, n) + ratio / 36.0 * trail(after + 1, n),
            -trail(after, n) / 36.0,
        ]
    rows = [lead(i), trail(i, n), lead(i) / denom(n), trail(i, n) / denom(n)]
    share_left, share_right, corner = message_shares(n, start, size)
    return np.concatenate(rows + [np.array(own_left + own_right), corner, share_left, share_right])


def per_block(make, n, count):
    size = n // count
    return np.stack([make(n, block * size, size) for block in range(count)])


def largest_divisor(size, most):
    return max(d for d in range(1, most + 1) if size % d == 0)


def message_forms(count):
    return [k in (1, count - 1) for k in range(1, count)]


def edge_kernel(info, y_weights, z_weights, *refs, y_count, z_count):
    step, steps = pl.program_id(0), pl.num_programs(0)
    y_refs, z_refs, outs = refs[:y_count], refs[y_count : y_count + z_count], refs[y_count + z_count :]
    chunk, yb, _ = y_refs[0].shape[1:]
    ways = y_weights.shape[1] // 2
    y_outs, z_outs = outs[:ways], outs[ways:]
    for field, ref in enumerate(y_refs):
        for z in range(chunk):
            sums = jnp.dot(y_weights[0], ref[0, z], preferred_element_type=f32)
            sums = sums[:ways] + sums[ways:]
            for k, out in enumerate(y_outs):
                out[field, 0, z, :] = sums[k]
                if out.shape[1] == 2:
                    edge = jnp.where(info[0] < ways - k, ref[0, z, yb - 1 :, :], ref[0, z, 0:1, :])
                    out[field, 1, z : z + 1, :] = edge.astype(f32)
    if not z_refs:
        return

    zb = z_weights.shape[1] // len(z_outs)
    for field, ref in enumerate(z_refs):
        for k, out in enumerate(z_outs):
            total = None
            for z in range(chunk):
                term = ref[0, z].astype(f32) * z_weights[info[1], k * zb + step * chunk + z]
                total = term if total is None else total + term

            @pl.when(step == 0)
            def _():
                out[field, 0] = total
                if out.shape[1] == 2:
                    out[field, 1] = ref[0, 0].astype(f32)

            @pl.when(step > 0)
            def _():
                out[field, 0] += total

            if out.shape[1] == 2:

                @pl.when((step == steps - 1) & (info[1] < len(z_outs) - k))
                def _():
                    out[field, 1] = ref[0, chunk - 1].astype(f32)


def edge_messages(info, velocity, y_weights, z_weights, y_fields, z_fields):
    _, zb, yb, nx = velocity.shape
    y_forms = message_forms(y_weights.shape[0])
    z_forms = message_forms(z_weights.shape[0]) if z_fields else []
    chunk = 8 if zb % 8 == 0 else zb
    fields = y_fields + z_fields
    in_y, in_z = len(y_fields), len(z_fields)
    piece = lambda f: pl.BlockSpec((1, chunk, yb, nx), lambda i, info: (f, i, 0, 0))
    y_spec = lambda near: pl.BlockSpec((in_y, 1 + near, chunk, nx), lambda i, info: (0, 0, i, 0))
    z_spec = lambda near: pl.BlockSpec((in_z, 1 + near, yb, nx), lambda i, info: (0, 0, 0, 0))
    outs = pl.pallas_call(
        functools.partial(edge_kernel, y_count=in_y, z_count=in_z),
        grid_spec=pltpu.PrefetchScalarGridSpec(
            num_scalar_prefetch=1,
            grid=(zb // chunk,),
            in_specs=[
                pl.BlockSpec((1,) + y_weights.shape[1:], lambda i, info: (info[0], 0, 0)),
                pl.BlockSpec(memory_space=pltpu.SMEM),
                *[piece(f) for f in fields],
            ],
            out_specs=[y_spec(near) for near in y_forms] + [z_spec(near) for near in z_forms],
        ),
        out_shape=[jax.ShapeDtypeStruct((in_y, 1 + near, zb, nx), f32) for near in y_forms]
        + [jax.ShapeDtypeStruct((in_z, 1 + near, yb, nx), f32) for near in z_forms],
        compiler_params=pltpu.CompilerParams(vmem_limit_bytes=VMEM_LIMIT),
        cost_estimate=light,
        name="edge_messages",
    )(info, y_weights, z_weights, *[velocity] * len(fields))
    return outs[: len(y_forms)], outs[len(y_forms) :]


def exchange(messages, axis):
    count = lax.axis_size(axis)
    out = []
    for k, message in enumerate(messages, 1):
        pairs = [(i, (i + k) % count) for i in range(count)]
        out.append(lax.ppermute(message, axis, pairs))
    return out


def slope_along_x(ref, tables, metric):
    chunk, yb, nx = ref.shape[1:]
    field = ref[0].reshape(chunk * yb, nx)
    high, low = tables
    slope = jnp.dot(field, high[...], preferred_element_type=f32)
    slope = slope + jnp.dot(field, low[...], preferred_element_type=f32)
    return (slope * metric[...]).reshape(chunk, yb, nx)


def slope_along_y(ref, z, table, columns, messages, metric):
    rows = table.shape[1] // 2
    both = jnp.dot(table[0], ref[0, z], preferred_element_type=f32)
    slope = both[:rows] + both[rows:]
    for k, message in enumerate(messages):
        slope = slope + columns[0, :, k : k + 1] * message[0, z : z + 1, :]
    last = len(messages)
    slope = slope + columns[0, :, last : last + 1] * messages[0][1, z : z + 1, :]
    slope = slope + columns[0, :, last + 1 : last + 2] * messages[-1][1, z : z + 1, :]
    return slope * metric[...]


def slopes_along_z(info, ref, scalars, messages, metric, out):
    _, zb, yb, nx = ref.shape
    rows, lanes = 16, 128
    across = nx // lanes
    block = info[1]
    last = len(messages)

    def tile(t, carry):
        ys = pl.ds(pl.multiple_of((t // across) * rows, rows), rows)
        xs = pl.ds(pl.multiple_of((t % across) * lanes, lanes), lanes)
        f = [ref[0, z, ys, xs].astype(f32) for z in range(zb)]
        scalar = lambda k: scalars[block, k]

        def rhs(z):
            total = None
            for step, weight in ((1, 7.0 / 9.0), (2, 1.0 / 36.0)):
                if z + step < zb and z - step >= 0:
                    term = (f[z + step] - f[z - step]) * weight
                elif z + step < zb:
                    term = f[z + step] * weight
                else:
                    term = f[z - step] * -weight
                total = term if total is None else total + term
            return total

        own = 4 * zb
        run = f[0] * scalar(own) + f[1] * scalar(own + 1)
        for k, message in enumerate(messages):
            run = run + message[0, 0, ys, xs] * scalar(own + 6 + k)
        forward = []
        for z in range(zb):
            run = run * -ratio + rhs(z) * scalar(z)
            forward.append(run)
        run = f[zb - 1] * scalar(own + 2) + f[zb - 2] * scalar(own + 3)
        for k, message in enumerate(messages):
            run = run + message[0, 0, ys, xs] * scalar(own + 6 + last + k)
        for z in reversed(range(zb)):
            run = run * -ratio
            slope = forward[z] * scalar(3 * zb + z) + run * scalar(2 * zb + z)
            run = run + rhs(z) * scalar(zb + z)
            if z == 0:
                slope = slope + messages[0][0, 1, ys, xs] * scalar(own + 4)
            if z == zb - 1:
                slope = slope + messages[-1][0, 1, ys, xs] * scalar(own + 5)
            out[z, ys, xs] = slope * metric[block * zb + z]
        return carry

    lax.fori_loop(0, (yb // rows) * across, tile, 0)


def hand_out(info, spin, outs):
    parts, _, rows, lanes = outs[0].shape
    if len(outs) == 1 and parts == 1:
        outs[0][0] = spin[...]
        return
    for q, out in enumerate(outs):
        xs = pl.ds(pl.multiple_of(info[2 + parts + q] * lanes, lanes), lanes)
        for part in range(parts):
            ys = pl.ds(pl.multiple_of(info[2 + part] * rows, rows), rows)
            out[part] = spin[:, ys, xs]


def spin_z_kernel(info, ways, v_ref, high, low, metric_x, u_ref, table, columns, *rest):
    messages, (metric_y, *outs, spin) = rest[: ways[0]], rest[ways[0] :]
    slope_vx = slope_along_x(v_ref, (high, low), metric_x).astype(bf16)
    for z in range(u_ref.shape[1]):
        slope_uy = slope_along_y(u_ref, z, table, columns, messages, metric_y)
        spin[z] = (slope_vx[z].astype(f32) - slope_uy).astype(bf16)
    hand_out(info, spin, outs)


def spin_y_kernel(info, ways, w_ref, high, low, metric_x, u_ref, scalars, *rest):
    messages, (metric_z, *outs, spin, slopes) = rest[: ways[1]], rest[ways[1] :]
    step = pl.program_id(0)
    chunk = w_ref.shape[1]

    @pl.when(step == 0)
    def _():
        slopes_along_z(info, u_ref, scalars, messages, metric_z, slopes)

    slope_wx = slope_along_x(w_ref, (high, low), metric_x).astype(bf16)
    for z in range(chunk):
        spin[z] = (slopes[step * chunk + z] - slope_wx[z].astype(f32)).astype(bf16)
    hand_out(info, spin, outs)


def spin_x_kernel(info, ways, w_ref, table, columns, *rest):
    y_messages, (metric_y, v_ref, scalars, *rest) = rest[: ways[0]], rest[ways[0] :]
    messages, (metric_z, *rest, spin, slopes) = rest[: ways[1]], rest[ways[1] :]
    outs = rest[len(rest) // 2 :]
    step = pl.program_id(0)
    chunk = w_ref.shape[1]

    @pl.when(step == 0)
    def _():
        slopes_along_z(info, v_ref, scalars, messages, metric_z, slopes)

    for z in range(chunk):
        slope_wy = slope_along_y(w_ref, z, table, columns, y_messages, metric_y).astype(bf16)
        spin[z] = (slope_wy.astype(f32) - slopes[step * chunk + z]).astype(bf16)
    hand_out(info, spin, outs)


def spin_call(kernel, info, velocity, groups, splits, flops, ways, name, slot=(0, 1), into=(), cut=1):
    _, zb, yb, nx = velocity.shape
    row_parts, col_parts = splits
    rows = yb // cut
    chunk = largest_divisor(zb, 4 if cut == 1 else 8)
    specs, args, scratch = [], [], [pltpu.VMEM((chunk, rows, nx), bf16)]
    at_row = lambda info: info[info.shape[0] - 1] if cut > 1 else 0
    whole = lambda a: pl.BlockSpec(a.shape, lambda i, info: (0,) * a.ndim)
    mine = lambda a: pl.BlockSpec(
        (1,) + a.shape[1:], lambda i, info: (info[0] * cut + at_row(info),) + (0,) * (a.ndim - 1)
    )
    smem = pl.BlockSpec(memory_space=pltpu.SMEM)

    def add(spec, arg):
        specs.append(spec)
        args.append(arg)

    for kind, field, *more in groups:
        if kind == "z":
            scalars, place, messages, metric = more
            add(pl.BlockSpec((1, zb, yb, nx), lambda i, info, field=field: (field, 0, 0, 0)), velocity)
            add(smem, scalars)
            for message in messages:
                add(
                    pl.BlockSpec(
                        (1,) + message.shape[1:], lambda i, info, place=place: (place, 0, 0, 0)
                    ),
                    message,
                )
            add(smem, metric)
            scratch.append(pltpu.VMEM((zb, yb, nx), f32))
            continue
        if kind == "x":
            add(
                pl.BlockSpec(
                    (1, chunk, rows, nx), lambda i, info, field=field: (field, i, at_row(info), 0)
                ),
                velocity,
            )
            (high, low), metric = more
            add(whole(high), high)
            add(whole(low), low)
            add(whole(metric), metric)
        else:
            table, columns, messages, metric = more
            table = table.reshape(table.shape[0], 2, cut, rows, yb).swapaxes(1, 2)
            table = jnp.asarray(table.reshape(-1, 2 * rows, yb))
            columns = jnp.asarray(columns.reshape(-1, rows, columns.shape[2]), f32)
            add(pl.BlockSpec((1, chunk, yb, nx), lambda i, info, field=field: (field, i, 0, 0)), velocity)
            add(mine(table), table)
            add(mine(columns), columns)
            for message in messages:
                parts = message.shape[1]
                add(
                    pl.BlockSpec((None, parts, None, chunk, nx), lambda i, info: (0, 0, i, 0, 0)),
                    message.reshape(1, parts, zb // chunk, chunk, nx),
                )
            add(pl.BlockSpec((rows, 1), lambda i, info: (info[0] * cut + at_row(info), 0)), metric)

    block = (rows // row_parts, nx // col_parts)
    at, held = slot
    aliases = {}
    for q, buffer in enumerate(into):
        add(pl.BlockSpec(memory_space=pl.ANY), buffer)
        aliases[len(args)] = q
    out_spec = pl.BlockSpec((row_parts, None, chunk) + block, lambda i, info: (0, at, i, 0, 0))
    return pl.pallas_call(
        lambda info, *refs: kernel(info, ways, *refs),
        grid_spec=pltpu.PrefetchScalarGridSpec(
            num_scalar_prefetch=1,
            grid=(zb // chunk,),
            in_specs=specs,
            out_specs=[out_spec] * col_parts,
            scratch_shapes=scratch,
        ),
        out_shape=[jax.ShapeDtypeStruct((row_parts, held, zb) + block, bf16)] * col_parts,
        input_output_aliases=aliases,
        compiler_params=pltpu.CompilerParams(vmem_limit_bytes=VMEM_LIMIT),
        cost_estimate=light,
        name=name,
    )(info, *args)


def sketch_kernel(info, weights, *rest):
    count = weights.shape[0]
    fields = rest[:count]
    out = rest[-1]
    values = [field[...].astype(f32) for field in fields]
    for k in range(out.shape[0]):
        total = values[0] * weights[info[1], k]
        for r in range(1, count):
            total = total + values[r] * weights[info[1 + r], k]
        out[k] = total


def sketch_part(info, sketch_matrix, fields, total, component, shape):
    held, zb, rows, lanes = fields[0].shape
    rank = sketch_matrix.shape[1]
    chunk = largest_divisor(zb, 4)
    steps = zb // chunk
    piece = pl.BlockSpec((held, chunk, rows, lanes), lambda i, info: (0, i, 0, 0))
    specs = [pl.BlockSpec(memory_space=pltpu.SMEM)] + [piece] * len(fields)
    args = [sketch_matrix, *fields]
    aliases = {}
    if total is not None:
        specs.append(pl.BlockSpec(memory_space=pl.ANY))
        args.append(total)
        aliases = {len(args): 0}
    return pl.pallas_call(
        sketch_kernel,
        grid_spec=pltpu.PrefetchScalarGridSpec(
            num_scalar_prefetch=1,
            grid=(steps,),
            in_specs=specs,
            out_specs=pl.BlockSpec(
                (rank, held, chunk, rows, lanes),
                lambda i, info: (0, component // held, info[0] * steps + i, 0, 0),
            ),
        ),
        out_shape=jax.ShapeDtypeStruct(shape, f32),
        input_output_aliases=aliases,
        compiler_params=pltpu.CompilerParams(vmem_limit_bytes=VMEM_LIMIT),
        cost_estimate=light,
        name="sketch_part",
    )(info, *args)


def col_rank(c, count):
    return (c % 2) * (count // 2) + c // 2 if count % 2 == 0 else c


def col_of_rank(t, count):
    return (t % (count // 2)) * 2 + t // (count // 2) if count % 2 == 0 else t


def routes(snaps, cols, depth):
    out = []
    place = lambda s, y, z: (s * cols + y) * depth + z
    for shift in range(depth):
        for turn in range(cols):
            first, second = [], []
            for s in range(snaps):
                for p in range(cols):
                    for z in range(depth):
                        c = col_of_rank((p - turn - s) % cols, cols)
                        first.append((place(s, p, z), place(s, c, z)))
                        second.append((place(s, c, z), place(p, c, (z + shift) % depth)))
            out.append((first, second))
    return out


def after(x, *others):
    return lax.optimization_barrier((x, *others))[0]


def general_way(vorticity, sketch_matrix):
    lines = lax.all_to_all(vorticity, "py", split_axis=4, concat_axis=3, tiled=True)
    snap_count = lax.axis_size("snap")
    pz_count = lax.axis_size("pz")
    shape_now = lines.shape
    block_rows = shape_now[3] // (snap_count * pz_count)
    split_rows = lines.reshape(shape_now[:3] + (snap_count, pz_count, block_rows, shape_now[4]))
    reordered = jnp.swapaxes(split_rows, 3, 4).reshape(shape_now)
    lines = lax.all_to_all(reordered, "pz", split_axis=3, concat_axis=2, tiled=True)
    lines = lax.all_to_all(lines, "snap", split_axis=3, concat_axis=0, tiled=True)
    return jnp.einsum(
        "sk,sczyx->kczyx", sketch_matrix, lines.astype(f32), precision=lax.Precision.HIGHEST
    )


def on_device(velocity, metric_x, metric_y, metric_z, sketch_matrix):
    snaps, cols, depth = (lax.axis_size(name) for name in ("snap", "py", "pz"))
    s, p, z = (lax.axis_index(name) for name in ("snap", "py", "pz"))
    _, _, zb, yb, nx = velocity.shape
    ny, nz = yb * cols, zb * depth
    velocity = velocity[0]
    direct = snaps == cols

    tables_x = [jnp.asarray(t) for t in split_table(line_table(nx, 0, nx).T)]
    tables_y = per_block(line_table, ny, cols)
    tables_y = np.concatenate(split_table(tables_y), axis=1)
    columns_y = per_block(message_columns, ny, cols)
    weights_y = split_table(per_block(message_weights, ny, cols))
    weights_y = jnp.asarray(np.concatenate(weights_y, axis=1))
    weights_z = jnp.asarray(per_block(message_weights, nz, depth).reshape(depth, -1), f32)
    scalars_z = jnp.asarray(per_block(sweep_scalars, nz, depth), f32)
    metric_x = metric_x.reshape(1, nx)
    metric_y = metric_y.reshape(ny, 1)

    rows_to = [(z + shift) % depth for shift in range(depth)]
    cols_to = [col_of_rank((p - turn - s) % cols, cols) for turn in range(cols)]
    pack = lambda *items: jnp.stack(items).astype(jnp.int32)
    info = pack(p, z, *rows_to, *cols_to) if direct else pack(p, z)

    weights = (weights_y, weights_z)
    u_edges, _ = edge_messages(info, velocity, *weights, (0,), ())
    u_edges = exchange(u_edges, "py")
    w_edges, z_edges = edge_messages(info, velocity, *weights, (2,), (0, 1))

    points = zb * yb * nx
    along_x = lambda field: ("x", field, tables_x, metric_x)
    along_y = lambda field, edges: ("y", field, tables_y, columns_y, edges, metric_y)
    along_z = lambda field: ("z", field, scalars_z, field, z_edges, metric_z)
    splits = (depth, cols) if direct else (1, 1)
    call = functools.partial(spin_call, ways=(cols - 1, depth - 1))
    spin_z = []
    ready = w_edges[0]
    for shift in range(depth if direct else 1):
        here = pack(p, z, 0 * z, *cols_to, rows_to[shift]) if direct else info
        spin_z += call(
            spin_z_kernel,
            after(here, ready),
            velocity,
            [along_x(1), along_y(0, u_edges)],
            splits=(1, cols) if direct else (1, 1),
            flops=points * 4 * (nx + yb) // (depth if direct else 1),
            name="spin_z",
            cut=depth if direct else 1,
        )
    w_edges = exchange([after(m, spin_z[0]) for m in w_edges], "py")
    z_edges = exchange([after(m, spin_z[0]) for m in z_edges], "pz")

    def with_spin_y(info):
        return call(
            spin_y_kernel, info, velocity, [along_x(2), along_z(0)],
            flops=points * (4 * nx + 20), name="spin_y", slot=(1, 2), splits=splits,
        )

    def with_spin_x(pair, info):
        return call(
            spin_x_kernel, info, velocity, [along_y(2, w_edges), along_z(1)],
            flops=points * (4 * yb + 20), name="spin_x", slot=(0, 2), into=pair, splits=splits,
        )

    if not direct:
        pair = with_spin_x(with_spin_y(info), info)
        vorticity = jnp.concatenate([pair[0][0], spin_z[0][0]])[None]
        return general_way(vorticity, sketch_matrix)

    all_routes = routes(snaps, cols, depth)
    everywhere = ("snap", "py", "pz")
    count = len(all_routes)
    arrived = {}

    def travel(hop, i, sent, *behind):
        behind = [arrived[b] if isinstance(b, tuple) else b for b in behind]
        if behind:
            sent = after(sent, *behind)
        arrived[hop, i] = lax.ppermute(sent, everywhere, all_routes[i % count][hop])

    line = [(0, i) for i in range(count)] + [(1, i) for i in range(cols)]
    spin_y_at = len(line)
    line += [(1, i) for i in range(cols, count)]
    spin_x_at = spin_y_at + 1
    line += [(0, count + turn) for turn in range(cols)]
    line += [(1, i) for i in range(count, 2 * count)]
    pair = None
    for at, (hop, i) in enumerate(line):
        behind = [line[at - 4]] if at >= 4 else []
        if at == spin_y_at:
            pair = with_spin_y(after(info, *w_edges, *[arrived[0, i] for i in range(count)]))
            behind.append(pair[0])
        if at == spin_x_at:
            pair = with_spin_x(pair, info)
            behind.append(pair[0])
        if hop == 0:
            sent = spin_z[i] if i < count else pair[i - count]
        elif i < count:
            sent = arrived[0, i][0]
        else:
            sent = arrived[0, count + i % cols][(i - count) // cols]
        travel(hop, i, sent, *behind)

    shape = (sketch_matrix.shape[1], 3, nz, yb // depth, nx // cols)
    my_rank = col_rank(p, cols)
    total = None
    for place, component in enumerate((2, 0)):
        for shift in range(depth):
            whence = [(z - shift) % depth]
            whence += [(s - turn - my_rank) % snaps for turn in range(cols)]
            begin = place * count + shift * cols
            total = sketch_part(
                jnp.stack(whence).astype(jnp.int32),
                sketch_matrix,
                [arrived[1, i] for i in range(begin, begin + cols)],
                total,
                component,
                shape,
            )
    return total


def solution(mesh):
    placed = (P("snap", None, "pz", "py", None), P(), P(), P(), P())
    return jax.shard_map(
        on_device,
        mesh=mesh,
        in_specs=placed,
        out_specs=P(None, None, None, ("snap", "pz"), "py"),
        check_vma=False,
    )
```

```python
import functools

import jax
import jax.numpy as jnp
import ml_dtypes
import numpy as np
from jax import lax
from jax.experimental import pallas as pl
from jax.experimental.pallas import tpu as pltpu
from jax.sharding import PartitionSpec as P

ratio = (3.0 - 5.0**0.5) / 2.0
VMEM_LIMIT = 52 * 1024 * 1024
light = pl.CostEstimate(flops=1024, bytes_accessed=1024, transcendentals=0)
f32 = jnp.float32
bf16 = jnp.bfloat16


def lead(i):
    return 1.0 - ratio ** (2.0 * (np.asarray(i, np.float64) + 1.0))


def trail(i, n):
    return 1.0 - ratio ** (2.0 * (n - np.asarray(i, np.float64)))


def denom(n):
    return 5.0**0.5 / 3.0 * (1.0 - ratio ** (2.0 * (n + 1.0)))


def inverse_entry(row, col, n):
    inside = (col >= 0) & (col < n)
    col = np.clip(col, 0, n - 1)
    near, far = np.minimum(row, col), np.maximum(row, col)
    sign = 1.0 - 2.0 * ((far - near) % 2)
    value = sign * ratio ** (far - near).astype(np.float64) * lead(near) * trail(far, n) / denom(n)
    return np.where(inside, value, 0.0)


def line_table(n, start, size):
    row = start + np.arange(size)[:, None]
    col = start + np.arange(size)[None, :]
    entry = functools.partial(inverse_entry, row, n=n)
    first = entry(col - 1) - entry(col + 1)
    second = entry(col - 2) - entry(col + 2)
    return 7.0 / 9.0 * first + 1.0 / 36.0 * second


def split_table(table):
    high = table.astype(ml_dtypes.bfloat16)
    low = (table - high.astype(np.float64)).astype(ml_dtypes.bfloat16)
    return high, low


def edge_weights(n, start, size):
    last = start + size - 1
    j = start + np.arange(size)

    def forward(k):
        return np.where(k >= 0, (-ratio) ** (last - k).astype(np.float64) * lead(k), 0.0)

    def backward(k):
        return np.where(k <= n - 1, (-ratio) ** (k - start).astype(np.float64) * trail(k, n), 0.0)

    def weights(c):
        return 7.0 / 9.0 * (c(j - 1) - c(j + 1)) + 1.0 / 36.0 * (c(j - 2) - c(j + 2))

    return weights(forward), weights(backward)


def edge_columns(n, start, size):
    i = start + np.arange(size)
    left = (-ratio) ** (i - start + 1.0) * trail(i, n) / denom(n)
    right = (-ratio) ** (start + size - i).astype(np.float64) * lead(i) / denom(n)
    return left, right


def message_weights(n, start, size):
    count, block = n // size, start // size
    right, left = edge_weights(n, start, size)
    return np.stack([right if block < count - k else left for k in range(1, count)])


def message_shares(n, start, size):
    count, block = n // size, start // size
    decay = (-ratio) ** size
    left = [decay ** (k - 1) if block >= k else 0.0 for k in range(1, count)]
    right = [decay ** (count - k - 1) if block < k else 0.0 for k in range(1, count)]
    corner = [-1.0 / 12.0 if block > 0 else 0.0, 1.0 / 12.0 if block < count - 1 else 0.0]
    return np.array(left), np.array(right), np.array(corner)


def message_columns(n, start, size):
    left, right = edge_columns(n, start, size)
    share_left, share_right, corner = message_shares(n, start, size)
    corners = np.zeros((size, 2))
    corners[0, 0], corners[-1, 1] = corner
    return np.concatenate([np.outer(left, share_left) + np.outer(right, share_right), corners], axis=1)


def sweep_scalars(n, start, size):
    i = start + np.arange(size)
    after = start + size
    own_left = [0.0, 0.0]
    own_right = [0.0, 0.0]
    if start > 0:
        own_left = [7.0 / 9.0 * lead(start - 1) - ratio / 36.0 * lead(start - 2), lead(start - 1) / 36.0]
    if after < n:
        own_right = [
            -7.0 / 9.0 * trail(after, n) + ratio / 36.0 * trail(after + 1, n),
            -trail(after, n) / 36.0,
        ]
    rows = [lead(i), trail(i, n), lead(i) / denom(n), trail(i, n) / denom(n)]
    share_left, share_right, corner = message_shares(n, start, size)
    return np.concatenate(rows + [np.array(own_left + own_right), corner, share_left, share_right])


def per_block(make, n, count):
    size = n // count
    return np.stack([make(n, block * size, size) for block in range(count)])


def largest_divisor(size, most):
    return max(d for d in range(1, most + 1) if size % d == 0)


def message_forms(count):
    return [k in (1, count - 1) for k in range(1, count)]


def edge_kernel(info, y_weights, z_weights, *refs, y_count, z_count):
    step, steps = pl.program_id(0), pl.num_programs(0)
    y_refs, z_refs, outs = refs[:y_count], refs[y_count : y_count + z_count], refs[y_count + z_count :]
    chunk, yb, _ = (y_refs + z_refs)[0].shape[1:]
    ways = y_weights.shape[1] // 2 if y_refs else 0
    y_outs, z_outs = outs[:ways], outs[ways:]
    for field, ref in enumerate(y_refs):
        for z in range(chunk):
            sums = jnp.dot(y_weights[0], ref[0, z], preferred_element_type=f32)
            sums = sums[:ways] + sums[ways:]
            for k, out in enumerate(y_outs):
                out[field, 0, z, :] = sums[k]
                if out.shape[1] == 2:
                    edge = jnp.where(info[0] < ways - k, ref[0, z, yb - 1 :, :], ref[0, z, 0:1, :])
                    out[field, 1, z : z + 1, :] = edge.astype(f32)
    if not z_refs:
        return

    zb = z_weights.shape[1] // len(z_outs)
    for field, ref in enumerate(z_refs):
        for k, out in enumerate(z_outs):
            total = None
            for z in range(chunk):
                term = ref[0, z].astype(f32) * z_weights[info[1], k * zb + step * chunk + z]
                total = term if total is None else total + term

            @pl.when(step == 0)
            def _():
                out[field, 0] = total
                if out.shape[1] == 2:
                    out[field, 1] = ref[0, 0].astype(f32)

            @pl.when(step > 0)
            def _():
                out[field, 0] += total

            if out.shape[1] == 2:

                @pl.when((step == steps - 1) & (info[1] < len(z_outs) - k))
                def _():
                    out[field, 1] = ref[0, chunk - 1].astype(f32)


def edge_messages(info, velocity, y_weights, z_weights, y_fields, z_fields):
    _, zb, yb, nx = velocity.shape
    y_forms = message_forms(y_weights.shape[0]) if y_fields else []
    z_forms = message_forms(z_weights.shape[0]) if z_fields else []
    chunk = 8 if zb % 8 == 0 else zb
    fields = y_fields + z_fields
    in_y, in_z = len(y_fields), len(z_fields)
    piece = lambda f: pl.BlockSpec((1, chunk, yb, nx), lambda i, info: (f, i, 0, 0))
    y_spec = lambda near: pl.BlockSpec((in_y, 1 + near, chunk, nx), lambda i, info: (0, 0, i, 0))
    z_spec = lambda near: pl.BlockSpec((in_z, 1 + near, yb, nx), lambda i, info: (0, 0, 0, 0))
    outs = pl.pallas_call(
        functools.partial(edge_kernel, y_count=in_y, z_count=in_z),
        grid_spec=pltpu.PrefetchScalarGridSpec(
            num_scalar_prefetch=1,
            grid=(zb // chunk,),
            in_specs=[
                pl.BlockSpec((1,) + y_weights.shape[1:], lambda i, info: (info[0], 0, 0)),
                pl.BlockSpec(memory_space=pltpu.SMEM),
                *[piece(f) for f in fields],
            ],
            out_specs=[y_spec(near) for near in y_forms] + [z_spec(near) for near in z_forms],
        ),
        out_shape=[jax.ShapeDtypeStruct((in_y, 1 + near, zb, nx), f32) for near in y_forms]
        + [jax.ShapeDtypeStruct((in_z, 1 + near, yb, nx), f32) for near in z_forms],
        compiler_params=pltpu.CompilerParams(vmem_limit_bytes=VMEM_LIMIT),
        cost_estimate=light,
        name="edge_messages",
    )(info, y_weights, z_weights, *[velocity] * len(fields))
    return outs[: len(y_forms)], outs[len(y_forms) :]


def exchange(messages, axis):
    count = lax.axis_size(axis)
    out = []
    for k, message in enumerate(messages, 1):
        pairs = [(i, (i + k) % count) for i in range(count)]
        out.append(lax.ppermute(message, axis, pairs))
    return out


def slope_along_x(ref, tables, metric):
    chunk, yb, nx = ref.shape[1:]
    field = ref[0].reshape(chunk * yb, nx)
    high, low = tables
    slope = jnp.dot(field, high[...], preferred_element_type=f32)
    slope = slope + jnp.dot(field, low[...], preferred_element_type=f32)
    return (slope * metric[...]).reshape(chunk, yb, nx)


def slope_along_y(ref, z, table, columns, messages, metric):
    rows = table.shape[1] // 2
    both = jnp.dot(table[0], ref[0, z], preferred_element_type=f32)
    slope = both[:rows] + both[rows:]
    for k, message in enumerate(messages):
        slope = slope + columns[0, :, k : k + 1] * message[0, z : z + 1, :]
    last = len(messages)
    slope = slope + columns[0, :, last : last + 1] * messages[0][1, z : z + 1, :]
    slope = slope + columns[0, :, last + 1 : last + 2] * messages[-1][1, z : z + 1, :]
    return slope * metric[...]


def slopes_along_z(info, ref, scalars, messages, metric, out):
    _, zb, yb, nx = ref.shape
    rows, lanes = 16, 128
    across = nx // lanes
    block = info[1]
    last = len(messages)

    def tile(t, carry):
        ys = pl.ds(pl.multiple_of((t // across) * rows, rows), rows)
        xs = pl.ds(pl.multiple_of((t % across) * lanes, lanes), lanes)
        f = [ref[0, z, ys, xs].astype(f32) for z in range(zb)]
        scalar = lambda k: scalars[block, k]

        def rhs(z):
            total = None
            for step, weight in ((1, 7.0 / 9.0), (2, 1.0 / 36.0)):
                if z + step < zb and z - step >= 0:
                    term = (f[z + step] - f[z - step]) * weight
                elif z + step < zb:
                    term = f[z + step] * weight
                else:
                    term = f[z - step] * -weight
                total = term if total is None else total + term
            return total

        own = 4 * zb
        run = f[0] * scalar(own) + f[1] * scalar(own + 1)
        for k, message in enumerate(messages):
            run = run + message[0, 0, ys, xs] * scalar(own + 6 + k)
        forward = []
        for z in range(zb):
            run = run * -ratio + rhs(z) * scalar(z)
            forward.append(run)
        run = f[zb - 1] * scalar(own + 2) + f[zb - 2] * scalar(own + 3)
        for k, message in enumerate(messages):
            run = run + message[0, 0, ys, xs] * scalar(own + 6 + last + k)
        for z in reversed(range(zb)):
            run = run * -ratio
            slope = forward[z] * scalar(3 * zb + z) + run * scalar(2 * zb + z)
            run = run + rhs(z) * scalar(zb + z)
            if z == 0:
                slope = slope + messages[0][0, 1, ys, xs] * scalar(own + 4)
            if z == zb - 1:
                slope = slope + messages[-1][0, 1, ys, xs] * scalar(own + 5)
            out[z, ys, xs] = slope * metric[block * zb + z]
        return carry

    lax.fori_loop(0, (yb // rows) * across, tile, 0)


def hand_out(info, spin, outs):
    parts, _, rows, lanes = outs[0].shape
    if len(outs) == 1 and parts == 1:
        outs[0][0] = spin[...]
        return
    for q, out in enumerate(outs):
        xs = pl.ds(pl.multiple_of(info[2 + parts + q] * lanes, lanes), lanes)
        for part in range(parts):
            ys = pl.ds(pl.multiple_of(info[2 + part] * rows, rows), rows)
            out[part] = spin[:, ys, xs]


def spin_z_kernel(info, ways, v_ref, high, low, metric_x, u_ref, table, columns, *rest):
    messages, (metric_y, *outs, spin) = rest[: ways[0]], rest[ways[0] :]
    slope_vx = slope_along_x(v_ref, (high, low), metric_x).astype(bf16)
    for z in range(u_ref.shape[1]):
        slope_uy = slope_along_y(u_ref, z, table, columns, messages, metric_y)
        spin[z] = (slope_vx[z].astype(f32) - slope_uy).astype(bf16)
    hand_out(info, spin, outs)


def spin_y_kernel(info, ways, w_ref, high, low, metric_x, u_ref, scalars, *rest):
    messages, (metric_z, *outs, spin, slopes) = rest[: ways[1]], rest[ways[1] :]
    step = pl.program_id(0)
    chunk = w_ref.shape[1]

    @pl.when(step == 0)
    def _():
        slopes_along_z(info, u_ref, scalars, messages, metric_z, slopes)

    slope_wx = slope_along_x(w_ref, (high, low), metric_x).astype(bf16)
    for z in range(chunk):
        spin[z] = (slopes[step * chunk + z] - slope_wx[z].astype(f32)).astype(bf16)
    hand_out(info, spin, outs)


def spin_x_kernel(info, ways, w_ref, table, columns, *rest):
    y_messages, (metric_y, v_ref, scalars, *rest) = rest[: ways[0]], rest[ways[0] :]
    messages, (metric_z, *outs, spin, slopes) = rest[: ways[1]], rest[ways[1] :]
    step = pl.program_id(0)
    chunk = w_ref.shape[1]

    @pl.when(step == 0)
    def _():
        slopes_along_z(info, v_ref, scalars, messages, metric_z, slopes)

    for z in range(chunk):
        slope_wy = slope_along_y(w_ref, z, table, columns, y_messages, metric_y).astype(bf16)
        spin[z] = (slope_wy.astype(f32) - slopes[step * chunk + z]).astype(bf16)
    hand_out(info, spin, outs)


def spin_call(kernel, info, velocity, groups, splits, flops, ways, name, cut=1):
    _, zb, yb, nx = velocity.shape
    row_parts, col_parts = splits
    rows = yb // cut
    chunk = largest_divisor(zb, 4 if cut == 1 else 8)
    specs, args, scratch = [], [], [pltpu.VMEM((chunk, rows, nx), bf16)]
    at_row = lambda info: info[info.shape[0] - 1] if cut > 1 else 0
    whole = lambda a: pl.BlockSpec(a.shape, lambda i, info: (0,) * a.ndim)
    mine = lambda a: pl.BlockSpec(
        (1,) + a.shape[1:], lambda i, info: (info[0] * cut + at_row(info),) + (0,) * (a.ndim - 1)
    )
    smem = pl.BlockSpec(memory_space=pltpu.SMEM)

    def add(spec, arg):
        specs.append(spec)
        args.append(arg)

    for kind, field, *more in groups:
        if kind == "z":
            scalars, place, messages, metric = more
            add(pl.BlockSpec((1, zb, yb, nx), lambda i, info, field=field: (field, 0, 0, 0)), velocity)
            add(smem, scalars)
            for message in messages:
                add(
                    pl.BlockSpec(
                        (1,) + message.shape[1:], lambda i, info, place=place: (place, 0, 0, 0)
                    ),
                    message,
                )
            add(smem, metric)
            scratch.append(pltpu.VMEM((zb, yb, nx), f32))
            continue
        if kind == "x":
            add(
                pl.BlockSpec(
                    (1, chunk, rows, nx), lambda i, info, field=field: (field, i, at_row(info), 0)
                ),
                velocity,
            )
            (high, low), metric = more
            add(whole(high), high)
            add(whole(low), low)
            add(whole(metric), metric)
        else:
            table, columns, place, messages, metric = more
            table = table.reshape(table.shape[0], 2, cut, rows, yb).swapaxes(1, 2)
            table = jnp.asarray(table.reshape(-1, 2 * rows, yb))
            columns = jnp.asarray(columns.reshape(-1, rows, columns.shape[2]), f32)
            add(pl.BlockSpec((1, chunk, yb, nx), lambda i, info, field=field: (field, i, 0, 0)), velocity)
            add(mine(table), table)
            add(mine(columns), columns)
            for message in messages:
                parts = message.shape[1]
                add(
                    pl.BlockSpec(
                        (None, parts, None, chunk, nx),
                        lambda i, info, place=place: (place, 0, i, 0, 0),
                    ),
                    message.reshape(2, parts, zb // chunk, chunk, nx),
                )
            add(pl.BlockSpec((rows, 1), lambda i, info: (info[0] * cut + at_row(info), 0)), metric)

    block = (rows // row_parts, nx // col_parts)
    out_spec = pl.BlockSpec((row_parts, None, chunk) + block, lambda i, info: (0, 0, i, 0, 0))
    return pl.pallas_call(
        lambda info, *refs: kernel(info, ways, *refs),
        grid_spec=pltpu.PrefetchScalarGridSpec(
            num_scalar_prefetch=1,
            grid=(zb // chunk,),
            in_specs=specs,
            out_specs=[out_spec] * col_parts,
            scratch_shapes=scratch,
        ),
        out_shape=[jax.ShapeDtypeStruct((row_parts, 1, zb) + block, bf16)] * col_parts,
        compiler_params=pltpu.CompilerParams(vmem_limit_bytes=VMEM_LIMIT),
        cost_estimate=light,
        name=name,
    )(info, *args)


def sketch_kernel(info, weights, *rest):
    count = weights.shape[0]
    fields = rest[:count]
    out = rest[-1]
    values = [field[...].astype(f32) for field in fields]
    for k in range(out.shape[0]):
        total = values[0] * weights[info[1], k]
        for r in range(1, count):
            total = total + values[r] * weights[info[1 + r], k]
        out[k] = total


def sketch_part(info, sketch_matrix, fields, total, component, shape):
    held, zb, rows, lanes = fields[0].shape
    rank = sketch_matrix.shape[1]
    chunk = largest_divisor(zb, 4)
    steps = zb // chunk
    piece = pl.BlockSpec((held, chunk, rows, lanes), lambda i, info: (0, i, 0, 0))
    specs = [pl.BlockSpec(memory_space=pltpu.SMEM)] + [piece] * len(fields)
    args = [sketch_matrix, *fields]
    aliases = {}
    if total is not None:
        specs.append(pl.BlockSpec(memory_space=pl.ANY))
        args.append(total)
        aliases = {len(args): 0}
    return pl.pallas_call(
        sketch_kernel,
        grid_spec=pltpu.PrefetchScalarGridSpec(
            num_scalar_prefetch=1,
            grid=(steps,),
            in_specs=specs,
            out_specs=pl.BlockSpec(
                (rank, held, chunk, rows, lanes),
                lambda i, info: (0, component // held, info[0] * steps + i, 0, 0),
            ),
        ),
        out_shape=jax.ShapeDtypeStruct(shape, f32),
        input_output_aliases=aliases,
        compiler_params=pltpu.CompilerParams(vmem_limit_bytes=VMEM_LIMIT),
        cost_estimate=light,
        name="sketch_part",
    )(info, *args)


def col_rank(c, count):
    return (c % 2) * (count // 2) + c // 2 if count % 2 == 0 else c


def col_of_rank(t, count):
    return (t % (count // 2)) * 2 + t // (count // 2) if count % 2 == 0 else t


def routes(snaps, cols, depth):
    out = []
    place = lambda s, y, z: (s * cols + y) * depth + z
    for shift in range(depth):
        for turn in range(cols):
            first, second = [], []
            for s in range(snaps):
                for p in range(cols):
                    for z in range(depth):
                        c = col_of_rank((p - turn - s) % cols, cols)
                        first.append((place(s, p, z), place(s, c, z)))
                        second.append((place(s, c, z), place(p, c, (z + shift) % depth)))
            out.append((first, second))
    return out


def after(x, *others):
    return lax.optimization_barrier((x, *others))[0]


def general_way(vorticity, sketch_matrix):
    lines = lax.all_to_all(vorticity, "py", split_axis=4, concat_axis=3, tiled=True)
    snap_count = lax.axis_size("snap")
    pz_count = lax.axis_size("pz")
    shape_now = lines.shape
    block_rows = shape_now[3] // (snap_count * pz_count)
    split_rows = lines.reshape(shape_now[:3] + (snap_count, pz_count, block_rows, shape_now[4]))
    reordered = jnp.swapaxes(split_rows, 3, 4).reshape(shape_now)
    lines = lax.all_to_all(reordered, "pz", split_axis=3, concat_axis=2, tiled=True)
    lines = lax.all_to_all(lines, "snap", split_axis=3, concat_axis=0, tiled=True)
    return jnp.einsum(
        "sk,sczyx->kczyx", sketch_matrix, lines.astype(f32), precision=lax.Precision.HIGHEST
    )


def on_device(velocity, metric_x, metric_y, metric_z, sketch_matrix):
    snaps, cols, depth = (lax.axis_size(name) for name in ("snap", "py", "pz"))
    s, p, z = (lax.axis_index(name) for name in ("snap", "py", "pz"))
    _, _, zb, yb, nx = velocity.shape
    ny, nz = yb * cols, zb * depth
    velocity = velocity[0]
    direct = snaps == cols

    tables_x = [jnp.asarray(t) for t in split_table(line_table(nx, 0, nx).T)]
    tables_y = per_block(line_table, ny, cols)
    tables_y = np.concatenate(split_table(tables_y), axis=1)
    columns_y = per_block(message_columns, ny, cols)
    weights_y = split_table(per_block(message_weights, ny, cols))
    weights_y = jnp.asarray(np.concatenate(weights_y, axis=1))
    weights_z = jnp.asarray(per_block(message_weights, nz, depth).reshape(depth, -1), f32)
    scalars_z = jnp.asarray(per_block(sweep_scalars, nz, depth), f32)
    metric_x = metric_x.reshape(1, nx)
    metric_y = metric_y.reshape(ny, 1)

    rows_to = [(z + shift) % depth for shift in range(depth)]
    cols_to = [col_of_rank((p - turn - s) % cols, cols) for turn in range(cols)]
    pack = lambda *items: jnp.stack(items).astype(jnp.int32)
    info = pack(p, z, *rows_to, *cols_to) if direct else pack(p, z)

    weights = (weights_y, weights_z)
    y_sums, _ = edge_messages(info, velocity, *weights, (0, 2), ())
    y_edges = exchange(y_sums, "py")
    _, z_sums = edge_messages(after(info, y_sums[0]), velocity, *weights, (), (0, 1))
    z_edges = exchange(z_sums, "pz")

    points = zb * yb * nx
    along_x = lambda field: ("x", field, tables_x, metric_x)
    along_y = lambda field, place: ("y", field, tables_y, columns_y, place, y_edges, metric_y)
    along_z = lambda field: ("z", field, scalars_z, field, z_edges, metric_z)
    splits = (depth, cols) if direct else (1, 1)
    call = functools.partial(spin_call, ways=(cols - 1, depth - 1))
    spin_z = []
    ready = z_sums[0]
    for shift in range(depth if direct else 1):
        here = pack(p, z, 0 * z, *cols_to, rows_to[shift]) if direct else info
        spin_z += call(
            spin_z_kernel,
            after(here, ready),
            velocity,
            [along_x(1), along_y(0, 0)],
            splits=(1, cols) if direct else (1, 1),
            flops=points * 4 * (nx + yb) // (depth if direct else 1),
            name="spin_z",
            cut=depth if direct else 1,
        )

    def spin_y(info):
        return call(
            spin_y_kernel, info, velocity, [along_x(2), along_z(0)],
            flops=points * (4 * nx + 20), name="spin_y", splits=splits,
        )

    def spin_x(info):
        return call(
            spin_x_kernel, info, velocity, [along_y(2, 1), along_z(1)],
            flops=points * (4 * yb + 20), name="spin_x", splits=splits,
        )

    if not direct:
        vorticity = jnp.concatenate([spin_x(info)[0][0], spin_y(info)[0][0], spin_z[0][0]])[None]
        return general_way(vorticity, sketch_matrix)

    all_routes = routes(snaps, cols, depth)
    arrived = {}

    def travel(name, route, hop, sent, *behind):
        if behind:
            sent = after(sent, *behind)
        arrived[name] = lax.ppermute(sent, ("snap", "py", "pz"), all_routes[route][hop])

    turns = range(cols)
    count = depth * cols
    for i in range(cols):
        travel(("z", i), i, 0, spin_z[i])
    for i in range(cols):
        travel(("z", "to", i), i, 1, arrived["z", i][0])
    for i in range(cols, count):
        travel(("z", i), i, 0, spin_z[i], arrived["z", i - 2])
    y_parts = spin_y(after(info, *[arrived["z", i] for i in range(count - 2)]))
    for i in range(cols, count):
        travel(("z", "to", i), i, 1, arrived["z", i][0], arrived["z", "to", i - cols], y_parts[0])
    for t in turns:
        before = arrived[("z", count - 2 + t) if t < 2 else ("y", t - 2)]
        travel(("y", t), t, 0, y_parts[t], before, arrived["z", "to", t])
    x_parts = spin_x(after(info, y_parts[0], arrived["z", "to", 0]))
    for t in turns:
        before = arrived[("y", cols - 2 + t) if t < 2 else ("x", t - 2)]
        travel(("x", t), t, 0, x_parts[t], before, arrived["z", "to", count - cols + t])

    shape = (sketch_matrix.shape[1], 3, nz, yb // depth, nx // cols)
    my_rank = col_rank(p, cols)

    def add_sketch(total, names, shift, component):
        whence = [(z - shift) % depth]
        whence += [(s - turn - my_rank) % snaps for turn in turns]
        fields = [arrived[name] for name in names]
        return sketch_part(pack(*whence), sketch_matrix, fields, total, component, shape)

    total = None
    for shift in range(depth):
        names = [("z", "to", shift * cols + t) for t in turns]
        total = add_sketch(total, names, shift, 2)
    ahead = [("z", "to", count - cols + t) for t in turns]
    plan = [("y", 0, 1)] + [("xy", shift, 0) for shift in range(1, depth)] + [("x", 0, 0)]
    for kind, shift, component in plan:
        names = [(kind, "to", shift, t) for t in turns]
        for t in turns:
            pieces = [arrived[one, t][shift] for one in kind]
            sent = jnp.concatenate(pieces) if len(pieces) > 1 else pieces[0]
            travel(names[t], shift * cols + t, 1, sent, arrived[ahead[t]])
        total = add_sketch(total, names, shift, component)
        ahead = names
    return total


def solution(mesh):
    placed = (P("snap", None, "pz", "py", None), P(), P(), P(), P())
    return jax.shard_map(
        on_device,
        mesh=mesh,
        in_specs=placed,
        out_specs=P(None, None, None, ("snap", "pz"), "py"),
        check_vma=False,
    )
```

```python
import functools

import jax
import jax.numpy as jnp
import ml_dtypes
import numpy as np
from jax import lax
from jax.experimental import pallas as pl
from jax.experimental.pallas import tpu as pltpu
from jax.sharding import PartitionSpec as P

ratio = (3.0 - 5.0**0.5) / 2.0
VMEM_LIMIT = 52 * 1024 * 1024
light = pl.CostEstimate(flops=1024, bytes_accessed=1024, transcendentals=0)
f32 = jnp.float32
bf16 = jnp.bfloat16


def lead(i):
    return 1.0 - ratio ** (2.0 * (np.asarray(i, np.float64) + 1.0))


def trail(i, n):
    return 1.0 - ratio ** (2.0 * (n - np.asarray(i, np.float64)))


def denom(n):
    return 5.0**0.5 / 3.0 * (1.0 - ratio ** (2.0 * (n + 1.0)))


def inverse_entry(row, col, n):
    inside = (col >= 0) & (col < n)
    col = np.clip(col, 0, n - 1)
    near, far = np.minimum(row, col), np.maximum(row, col)
    sign = 1.0 - 2.0 * ((far - near) % 2)
    value = sign * ratio ** (far - near).astype(np.float64) * lead(near) * trail(far, n) / denom(n)
    return np.where(inside, value, 0.0)


def line_table(n, start, size):
    row = start + np.arange(size)[:, None]
    col = start + np.arange(size)[None, :]
    entry = functools.partial(inverse_entry, row, n=n)
    first = entry(col - 1) - entry(col + 1)
    second = entry(col - 2) - entry(col + 2)
    return 7.0 / 9.0 * first + 1.0 / 36.0 * second


def split_table(table):
    high = table.astype(ml_dtypes.bfloat16)
    low = (table - high.astype(np.float64)).astype(ml_dtypes.bfloat16)
    return high, low


def edge_weights(n, start, size):
    last = start + size - 1
    j = start + np.arange(size)

    def forward(k):
        return np.where(k >= 0, (-ratio) ** (last - k).astype(np.float64) * lead(k), 0.0)

    def backward(k):
        return np.where(k <= n - 1, (-ratio) ** (k - start).astype(np.float64) * trail(k, n), 0.0)

    def weights(c):
        return 7.0 / 9.0 * (c(j - 1) - c(j + 1)) + 1.0 / 36.0 * (c(j - 2) - c(j + 2))

    return weights(forward), weights(backward)


def edge_columns(n, start, size):
    i = start + np.arange(size)
    left = (-ratio) ** (i - start + 1.0) * trail(i, n) / denom(n)
    right = (-ratio) ** (start + size - i).astype(np.float64) * lead(i) / denom(n)
    return left, right


def message_weights(n, start, size):
    count, block = n // size, start // size
    right, left = edge_weights(n, start, size)
    return np.stack([right if block < count - k else left for k in range(1, count)])


def message_shares(n, start, size):
    count, block = n // size, start // size
    decay = (-ratio) ** size
    left = [decay ** (k - 1) if block >= k else 0.0 for k in range(1, count)]
    right = [decay ** (count - k - 1) if block < k else 0.0 for k in range(1, count)]
    corner = [-1.0 / 12.0 if block > 0 else 0.0, 1.0 / 12.0 if block < count - 1 else 0.0]
    return np.array(left), np.array(right), np.array(corner)


def message_columns(n, start, size):
    left, right = edge_columns(n, start, size)
    share_left, share_right, corner = message_shares(n, start, size)
    corners = np.zeros((size, 2))
    corners[0, 0], corners[-1, 1] = corner
    return np.concatenate([np.outer(left, share_left) + np.outer(right, share_right), corners], axis=1)


def sweep_scalars(n, start, size):
    i = start + np.arange(size)
    after = start + size
    own_left = [0.0, 0.0]
    own_right = [0.0, 0.0]
    if start > 0:
        own_left = [7.0 / 9.0 * lead(start - 1) - ratio / 36.0 * lead(start - 2), lead(start - 1) / 36.0]
    if after < n:
        own_right = [
            -7.0 / 9.0 * trail(after, n) + ratio / 36.0 * trail(after + 1, n),
            -trail(after, n) / 36.0,
        ]
    rows = [lead(i) / 36.0, trail(i, n) / 36.0, lead(i) / denom(n), trail(i, n) / denom(n)]
    share_left, share_right, corner = message_shares(n, start, size)
    return np.concatenate(rows + [np.array(own_left + own_right), corner, share_left, share_right])


def per_block(make, n, count):
    size = n // count
    return np.stack([make(n, block * size, size) for block in range(count)])


def largest_divisor(size, most):
    return max(d for d in range(1, most + 1) if size % d == 0)


def message_forms(count):
    return [k in (1, count - 1) for k in range(1, count)]


def edge_kernel(info, y_weights, z_weights, *refs, y_count, z_count):
    step, steps = pl.program_id(0), pl.num_programs(0)
    y_refs, z_refs, outs = refs[:y_count], refs[y_count : y_count + z_count], refs[y_count + z_count :]
    chunk, yb, _ = (y_refs + z_refs)[0].shape[1:]
    ways = y_weights.shape[1] // 2 if y_refs else 0
    y_outs, z_outs = outs[:ways], outs[ways:]
    for field, ref in enumerate(y_refs):
        for z in range(chunk):
            sums = jnp.dot(y_weights[0], ref[0, z], preferred_element_type=f32)
            sums = sums[:ways] + sums[ways:]
            for k, out in enumerate(y_outs):
                out[field, 0, z, :] = sums[k]
                if out.shape[1] == 2:
                    edge = jnp.where(info[0] < ways - k, ref[0, z, yb - 1 :, :], ref[0, z, 0:1, :])
                    out[field, 1, z : z + 1, :] = edge.astype(f32)
    if not z_refs:
        return

    zb = z_weights.shape[1] // len(z_outs)
    for field, ref in enumerate(z_refs):
        for k, out in enumerate(z_outs):
            total = None
            for z in range(chunk):
                term = ref[0, z].astype(f32) * z_weights[info[1], k * zb + step * chunk + z]
                total = term if total is None else total + term

            @pl.when(step == 0)
            def _():
                out[field, 0] = total
                if out.shape[1] == 2:
                    out[field, 1] = ref[0, 0].astype(f32)

            @pl.when(step > 0)
            def _():
                out[field, 0] += total

            if out.shape[1] == 2:

                @pl.when((step == steps - 1) & (info[1] < len(z_outs) - k))
                def _():
                    out[field, 1] = ref[0, chunk - 1].astype(f32)


def edge_messages(info, velocity, y_weights, z_weights, y_fields, z_fields):
    _, zb, yb, nx = velocity.shape
    y_forms = message_forms(y_weights.shape[0]) if y_fields else []
    z_forms = message_forms(z_weights.shape[0]) if z_fields else []
    chunk = 8 if zb % 8 == 0 else zb
    fields = y_fields + z_fields
    in_y, in_z = len(y_fields), len(z_fields)
    piece = lambda f: pl.BlockSpec((1, chunk, yb, nx), lambda i, info: (f, i, 0, 0))
    y_spec = lambda near: pl.BlockSpec((in_y, 1 + near, chunk, nx), lambda i, info: (0, 0, i, 0))
    z_spec = lambda near: pl.BlockSpec((in_z, 1 + near, yb, nx), lambda i, info: (0, 0, 0, 0))
    outs = pl.pallas_call(
        functools.partial(edge_kernel, y_count=in_y, z_count=in_z),
        grid_spec=pltpu.PrefetchScalarGridSpec(
            num_scalar_prefetch=1,
            grid=(zb // chunk,),
            in_specs=[
                pl.BlockSpec((1,) + y_weights.shape[1:], lambda i, info: (info[0], 0, 0)),
                pl.BlockSpec(memory_space=pltpu.SMEM),
                *[piece(f) for f in fields],
            ],
            out_specs=[y_spec(near) for near in y_forms] + [z_spec(near) for near in z_forms],
        ),
        out_shape=[jax.ShapeDtypeStruct((in_y, 1 + near, zb, nx), f32) for near in y_forms]
        + [jax.ShapeDtypeStruct((in_z, 1 + near, yb, nx), f32) for near in z_forms],
        compiler_params=pltpu.CompilerParams(vmem_limit_bytes=VMEM_LIMIT),
        cost_estimate=light,
        name="edge_messages",
    )(info, y_weights, z_weights, *[velocity] * len(fields))
    return outs[: len(y_forms)], outs[len(y_forms) :]


def exchange(messages, axis):
    count = lax.axis_size(axis)
    out = []
    for k, message in enumerate(messages, 1):
        pairs = [(i, (i + k) % count) for i in range(count)]
        out.append(lax.ppermute(message, axis, pairs))
    return out


def slope_along_x(ref, tables, metric):
    chunk, yb, nx = ref.shape[1:]
    field = ref[0].reshape(chunk * yb, nx)
    high, low = tables
    slope = jnp.dot(field, high[...], preferred_element_type=f32)
    slope = slope + jnp.dot(field, low[...], preferred_element_type=f32)
    return (slope * metric[...]).reshape(chunk, yb, nx)


def slope_along_y(ref, z, table, columns, messages, metric):
    rows = table.shape[1] // 2
    both = jnp.dot(table[0], ref[0, z], preferred_element_type=f32)
    slope = both[:rows] + both[rows:]
    for k, message in enumerate(messages):
        slope = slope + columns[0, :, k : k + 1] * message[0, z : z + 1, :]
    last = len(messages)
    slope = slope + columns[0, :, last : last + 1] * messages[0][1, z : z + 1, :]
    slope = slope + columns[0, :, last + 1 : last + 2] * messages[-1][1, z : z + 1, :]
    return slope * metric[...]


def slopes_along_z(info, ref, scalars, messages, metric, out):
    _, zb, yb, nx = ref.shape
    rows, lanes = 16, 128
    across = nx // lanes
    block = info[1]
    last = len(messages)

    def tile(t, carry):
        ys = pl.ds(pl.multiple_of((t // across) * rows, rows), rows)
        xs = pl.ds(pl.multiple_of((t % across) * lanes, lanes), lanes)
        f = [ref[0, z, ys, xs].astype(f32) for z in range(zb)]
        scalar = lambda k: scalars[block, k]

        def rhs(z):
            near, far = [
                f[z + step] - f[z - step]
                if z + step < zb and z - step >= 0
                else (f[z + step] if z + step < zb else -f[z - step])
                for step in (1, 2)
            ]
            return near * 28.0 + far

        own = 4 * zb
        run = f[0] * scalar(own) + f[1] * scalar(own + 1)
        for k, message in enumerate(messages):
            run = run + message[0, 0, ys, xs] * scalar(own + 6 + k)
        forward = []
        sides = [rhs(z) for z in range(zb)]
        for z in range(zb):
            run = run * -ratio + sides[z] * scalar(z)
            forward.append(run)
        run = f[zb - 1] * scalar(own + 2) + f[zb - 2] * scalar(own + 3)
        for k, message in enumerate(messages):
            run = run + message[0, 0, ys, xs] * scalar(own + 6 + last + k)
        for z in reversed(range(zb)):
            run = run * -ratio
            scale = metric[block * zb + z]
            slope = forward[z] * (scalar(3 * zb + z) * scale) + run * (scalar(2 * zb + z) * scale)
            run = run + sides[z] * scalar(zb + z)
            if z == 0:
                slope = slope + messages[0][0, 1, ys, xs] * (scalar(own + 4) * scale)
            if z == zb - 1:
                slope = slope + messages[-1][0, 1, ys, xs] * (scalar(own + 5) * scale)
            out[z, ys, xs] = slope
        return carry

    lax.fori_loop(0, (yb // rows) * across, tile, 0)


def hand_out(info, spin, outs):
    parts, _, rows, lanes = outs[0].shape
    if len(outs) == 1 and parts == 1:
        outs[0][0] = spin[...]
        return
    for q, out in enumerate(outs):
        xs = pl.ds(pl.multiple_of(info[2 + parts + q] * lanes, lanes), lanes)
        for part in range(parts):
            ys = pl.ds(pl.multiple_of(info[2 + part] * rows, rows), rows)
            out[part] = spin[:, ys, xs]


def spin_z_kernel(info, ways, v_ref, high, low, metric_x, u_ref, table, columns, *rest):
    messages, (metric_y, *outs, spin) = rest[: ways[0]], rest[ways[0] :]
    slope_vx = slope_along_x(v_ref, (high, low), metric_x).astype(bf16)
    for z in range(u_ref.shape[1]):
        slope_uy = slope_along_y(u_ref, z, table, columns, messages, metric_y)
        spin[z] = (slope_vx[z].astype(f32) - slope_uy).astype(bf16)
    hand_out(info, spin, outs)


def spin_y_kernel(info, ways, w_ref, high, low, metric_x, u_ref, scalars, *rest):
    messages, (metric_z, *outs, spin, slopes) = rest[: ways[1]], rest[ways[1] :]
    step = pl.program_id(0)
    chunk = w_ref.shape[1]

    @pl.when(step == 0)
    def _():
        slopes_along_z(info, u_ref, scalars, messages, metric_z, slopes)

    slope_wx = slope_along_x(w_ref, (high, low), metric_x).astype(bf16)
    for z in range(chunk):
        spin[z] = (slopes[step * chunk + z] - slope_wx[z].astype(f32)).astype(bf16)
    hand_out(info, spin, outs)


def spin_x_kernel(info, ways, w_ref, table, columns, *rest):
    y_messages, (metric_y, v_ref, scalars, *rest) = rest[: ways[0]], rest[ways[0] :]
    messages, (metric_z, *outs, spin, slopes) = rest[: ways[1]], rest[ways[1] :]
    step = pl.program_id(0)
    chunk = w_ref.shape[1]

    @pl.when(step == 0)
    def _():
        slopes_along_z(info, v_ref, scalars, messages, metric_z, slopes)

    for z in range(chunk):
        slope_wy = slope_along_y(w_ref, z, table, columns, y_messages, metric_y).astype(bf16)
        spin[z] = (slope_wy.astype(f32) - slopes[step * chunk + z]).astype(bf16)
    hand_out(info, spin, outs)


def spin_call(kernel, info, velocity, groups, splits, flops, ways, name, cut=1):
    _, zb, yb, nx = velocity.shape
    row_parts, col_parts = splits
    rows = yb // cut
    chunk = largest_divisor(zb, 4 if cut == 1 else 8)
    specs, args, scratch = [], [], [pltpu.VMEM((chunk, rows, nx), bf16)]
    at_row = lambda info: info[info.shape[0] - 1] if cut > 1 else 0
    whole = lambda a: pl.BlockSpec(a.shape, lambda i, info: (0,) * a.ndim)
    mine = lambda a: pl.BlockSpec(
        (1,) + a.shape[1:], lambda i, info: (info[0] * cut + at_row(info),) + (0,) * (a.ndim - 1)
    )
    smem = pl.BlockSpec(memory_space=pltpu.SMEM)

    def add(spec, arg):
        specs.append(spec)
        args.append(arg)

    for kind, field, *more in groups:
        if kind == "z":
            scalars, place, messages, metric = more
            add(pl.BlockSpec((1, zb, yb, nx), lambda i, info, field=field: (field, 0, 0, 0)), velocity)
            add(smem, scalars)
            for message in messages:
                add(
                    pl.BlockSpec(
                        (1,) + message.shape[1:], lambda i, info, place=place: (place, 0, 0, 0)
                    ),
                    message,
                )
            add(smem, metric)
            scratch.append(pltpu.VMEM((zb, yb, nx), f32))
            continue
        if kind == "x":
            add(
                pl.BlockSpec(
                    (1, chunk, rows, nx), lambda i, info, field=field: (field, i, at_row(info), 0)
                ),
                velocity,
            )
            (high, low), metric = more
            add(whole(high), high)
            add(whole(low), low)
            add(whole(metric), metric)
        else:
            table, columns, place, messages, metric = more
            table = table.reshape(table.shape[0], 2, cut, rows, yb).swapaxes(1, 2)
            table = jnp.asarray(table.reshape(-1, 2 * rows, yb))
            columns = jnp.asarray(columns.reshape(-1, rows, columns.shape[2]), f32)
            add(pl.BlockSpec((1, chunk, yb, nx), lambda i, info, field=field: (field, i, 0, 0)), velocity)
            add(mine(table), table)
            add(mine(columns), columns)
            for message in messages:
                parts = message.shape[1]
                add(
                    pl.BlockSpec(
                        (None, parts, None, chunk, nx),
                        lambda i, info, place=place: (place, 0, i, 0, 0),
                    ),
                    message.reshape(2, parts, zb // chunk, chunk, nx),
                )
            add(pl.BlockSpec((rows, 1), lambda i, info: (info[0] * cut + at_row(info), 0)), metric)

    block = (rows // row_parts, nx // col_parts)
    out_spec = pl.BlockSpec((row_parts, None, chunk) + block, lambda i, info: (0, 0, i, 0, 0))
    return pl.pallas_call(
        lambda info, *refs: kernel(info, ways, *refs),
        grid_spec=pltpu.PrefetchScalarGridSpec(
            num_scalar_prefetch=1,
            grid=(zb // chunk,),
            in_specs=specs,
            out_specs=[out_spec] * col_parts,
            scratch_shapes=scratch,
        ),
        out_shape=[jax.ShapeDtypeStruct((row_parts, 1, zb) + block, bf16)] * col_parts,
        compiler_params=pltpu.CompilerParams(vmem_limit_bytes=VMEM_LIMIT),
        cost_estimate=light,
        name=name,
    )(info, *args)


def sketch_kernel(info, weights, *rest):
    count = weights.shape[0]
    fields = rest[:count]
    out = rest[-1]
    values = [field[...].astype(f32) for field in fields]
    for k in range(out.shape[0]):
        total = values[0] * weights[info[1], k]
        for r in range(1, count):
            total = total + values[r] * weights[info[1 + r], k]
        out[k] = total


def sketch_part(info, sketch_matrix, fields, total, component, shape):
    held, zb, rows, lanes = fields[0].shape
    rank = sketch_matrix.shape[1]
    chunk = largest_divisor(zb, 4)
    steps = zb // chunk
    piece = pl.BlockSpec((held, chunk, rows, lanes), lambda i, info: (0, i, 0, 0))
    specs = [pl.BlockSpec(memory_space=pltpu.SMEM)] + [piece] * len(fields)
    args = [sketch_matrix, *fields]
    aliases = {}
    if total is not None:
        specs.append(pl.BlockSpec(memory_space=pl.ANY))
        args.append(total)
        aliases = {len(args): 0}
    return pl.pallas_call(
        sketch_kernel,
        grid_spec=pltpu.PrefetchScalarGridSpec(
            num_scalar_prefetch=1,
            grid=(steps,),
            in_specs=specs,
            out_specs=pl.BlockSpec(
                (rank, held, chunk, rows, lanes),
                lambda i, info: (0, component // held, info[0] * steps + i, 0, 0),
            ),
        ),
        out_shape=jax.ShapeDtypeStruct(shape, f32),
        input_output_aliases=aliases,
        compiler_params=pltpu.CompilerParams(vmem_limit_bytes=VMEM_LIMIT),
        cost_estimate=light,
        name="sketch_part",
    )(info, *args)


def col_rank(c, count):
    return (c % 2) * (count // 2) + c // 2 if count % 2 == 0 else c


def col_of_rank(t, count):
    return (t % (count // 2)) * 2 + t // (count // 2) if count % 2 == 0 else t


def routes(snaps, cols, depth):
    out = []
    place = lambda s, y, z: (s * cols + y) * depth + z
    for shift in range(depth):
        for turn in range(cols):
            first, second = [], []
            for s in range(snaps):
                for p in range(cols):
                    for z in range(depth):
                        c = col_of_rank((p - turn - s) % cols, cols)
                        first.append((place(s, p, z), place(s, c, z)))
                        second.append((place(s, c, z), place(p, c, (z + shift) % depth)))
            out.append((first, second))
    return out


def after(x, *others):
    return lax.optimization_barrier((x, *others))[0]


def general_way(vorticity, sketch_matrix):
    lines = lax.all_to_all(vorticity, "py", split_axis=4, concat_axis=3, tiled=True)
    snap_count = lax.axis_size("snap")
    pz_count = lax.axis_size("pz")
    shape_now = lines.shape
    block_rows = shape_now[3] // (snap_count * pz_count)
    split_rows = lines.reshape(shape_now[:3] + (snap_count, pz_count, block_rows, shape_now[4]))
    reordered = jnp.swapaxes(split_rows, 3, 4).reshape(shape_now)
    lines = lax.all_to_all(reordered, "pz", split_axis=3, concat_axis=2, tiled=True)
    lines = lax.all_to_all(lines, "snap", split_axis=3, concat_axis=0, tiled=True)
    return jnp.einsum(
        "sk,sczyx->kczyx", sketch_matrix, lines.astype(f32), precision=lax.Precision.HIGHEST
    )


def on_device(velocity, metric_x, metric_y, metric_z, sketch_matrix):
    snaps, cols, depth = (lax.axis_size(name) for name in ("snap", "py", "pz"))
    s, p, z = (lax.axis_index(name) for name in ("snap", "py", "pz"))
    _, _, zb, yb, nx = velocity.shape
    ny, nz = yb * cols, zb * depth
    velocity = velocity[0]
    direct = snaps == cols

    tables_x = [jnp.asarray(t) for t in split_table(line_table(nx, 0, nx).T)]
    tables_y = per_block(line_table, ny, cols)
    tables_y = np.concatenate(split_table(tables_y), axis=1)
    columns_y = per_block(message_columns, ny, cols)
    weights_y = split_table(per_block(message_weights, ny, cols))
    weights_y = jnp.asarray(np.concatenate(weights_y, axis=1))
    weights_z = jnp.asarray(per_block(message_weights, nz, depth).reshape(depth, -1), f32)
    scalars_z = jnp.asarray(per_block(sweep_scalars, nz, depth), f32)
    metric_x = metric_x.reshape(1, nx)
    metric_y = metric_y.reshape(ny, 1)

    rows_to = [(z + shift) % depth for shift in range(depth)]
    cols_to = [col_of_rank((p - turn - s) % cols, cols) for turn in range(cols)]
    pack = lambda *items: jnp.stack(items).astype(jnp.int32)
    info = pack(p, z, *rows_to, *cols_to) if direct else pack(p, z)

    weights = (weights_y, weights_z)
    y_sums, _ = edge_messages(info, velocity, *weights, (0, 2), ())
    y_edges = exchange(y_sums, "py")
    _, z_sums = edge_messages(after(info, y_sums[0]), velocity, *weights, (), (0, 1))
    z_edges = exchange(z_sums, "pz")

    points = zb * yb * nx
    along_x = lambda field: ("x", field, tables_x, metric_x)
    along_y = lambda field, place: ("y", field, tables_y, columns_y, place, y_edges, metric_y)
    along_z = lambda field: ("z", field, scalars_z, field, z_edges, metric_z)
    splits = (depth, cols) if direct else (1, 1)
    call = functools.partial(spin_call, ways=(cols - 1, depth - 1))
    spin_z = []
    ready = z_sums[0]
    for shift in range(depth if direct else 1):
        here = pack(p, z, 0 * z, *cols_to, rows_to[shift]) if direct else info
        spin_z += call(
            spin_z_kernel,
            after(here, ready),
            velocity,
            [along_x(1), along_y(0, 0)],
            splits=(1, cols) if direct else (1, 1),
            flops=points * 4 * (nx + yb) // (depth if direct else 1),
            name="spin_z",
            cut=depth if direct else 1,
        )

    def spin_y(info):
        return call(
            spin_y_kernel, info, velocity, [along_x(2), along_z(0)],
            flops=points * (4 * nx + 20), name="spin_y", splits=splits,
        )

    def spin_x(info):
        return call(
            spin_x_kernel, info, velocity, [along_y(2, 1), along_z(1)],
            flops=points * (4 * yb + 20), name="spin_x", splits=splits,
        )

    if not direct:
        vorticity = jnp.concatenate([spin_x(info)[0][0], spin_y(info)[0][0], spin_z[0][0]])[None]
        return general_way(vorticity, sketch_matrix)

    all_routes = routes(snaps, cols, depth)
    arrived = {}

    def travel(name, route, hop, sent, *behind):
        if behind:
            sent = after(sent, *behind)
        arrived[name] = lax.ppermute(sent, ("snap", "py", "pz"), all_routes[route][hop])

    turns = range(cols)
    count = depth * cols
    for i in range(cols):
        travel(("z", i), i, 0, spin_z[i])
    for i in range(cols):
        travel(("z", "to", i), i, 1, arrived["z", i][0])
    for i in range(cols, count):
        travel(("z", i), i, 0, spin_z[i], arrived["z", i - 2], *z_edges[: i // (cols + 2)])
    y_parts = spin_y(after(info, *[arrived["z", i] for i in range(count)]))
    x_parts = spin_x(after(info, y_parts[0]))
    kernels_over = [x_parts[0]] + [arrived["z", "to", i] for i in range(cols)]
    for i in range(cols, count):
        travel(("z", "to", i), i, 1, arrived["z", i][0], *kernels_over)
    first = [(kind, t, made[t]) for kind, made in (("y", y_parts), ("x", x_parts)) for t in turns]

    def send_first(place, *behind):
        kind, t, sent = first[place]
        if place > 1:
            behind += (arrived[first[place - 2][:2]],)
        travel((kind, t), t, 0, sent, *behind)

    for place in range(2 * cols):
        passed = cols + min(place - 2, cols - 1)
        if place > 0:
            send_first(place, *([arrived["z", "to", passed]] if place > 1 else kernels_over))
        else:
            send_first(place)

    shape = (sketch_matrix.shape[1], 3, nz, yb // depth, nx // cols)
    my_rank = col_rank(p, cols)

    def add_sketch(total, names, shift, component):
        whence = [(z - shift) % depth]
        whence += [(s - turn - my_rank) % snaps for turn in turns]
        fields = [arrived[name] for name in names]
        return sketch_part(pack(*whence), sketch_matrix, fields, total, component, shape)

    total = None
    for shift in range(depth):
        names = [("z", "to", shift * cols + t) for t in turns]
        total = add_sketch(total, names, shift, 2)
    ahead = [("z", "to", count - cols + t) for t in turns]
    plan = [("y", 0, 1)] + [("xy", shift, 0) for shift in range(1, depth)] + [("x", 0, 0)]
    for kind, shift, component in plan:
        names = [(kind, "to", shift, t) for t in turns]
        for t in turns:
            pieces = [arrived[one, t][shift] for one in kind]
            sent = jnp.concatenate(pieces) if len(pieces) > 1 else pieces[0]
            travel(names[t], shift * cols + t, 1, sent, arrived[ahead[t]])
        total = add_sketch(total, names, shift, component)
        ahead = names
    return total


def solution(mesh):
    placed = (P("snap", None, "pz", "py", None), P(), P(), P(), P())
    return jax.shard_map(
        on_device,
        mesh=mesh,
        in_specs=placed,
        out_specs=P(None, None, None, ("snap", "pz"), "py"),
        check_vma=False,
    )
```

```python
import functools

import jax
import jax.numpy as jnp
import ml_dtypes
import numpy as np
from jax import lax
from jax.experimental import pallas as pl
from jax.experimental.pallas import tpu as pltpu
from jax.sharding import PartitionSpec as P

ratio = (3.0 - 5.0**0.5) / 2.0
VMEM_LIMIT = 52 * 1024 * 1024
light = pl.CostEstimate(flops=1024, bytes_accessed=1024, transcendentals=0)
f32 = jnp.float32
bf16 = jnp.bfloat16


def lead(i):
    return 1.0 - ratio ** (2.0 * (np.asarray(i, np.float64) + 1.0))


def trail(i, n):
    return 1.0 - ratio ** (2.0 * (n - np.asarray(i, np.float64)))


def denom(n):
    return 5.0**0.5 / 3.0 * (1.0 - ratio ** (2.0 * (n + 1.0)))


def inverse_entry(row, col, n):
    inside = (col >= 0) & (col < n)
    col = np.clip(col, 0, n - 1)
    near, far = np.minimum(row, col), np.maximum(row, col)
    sign = 1.0 - 2.0 * ((far - near) % 2)
    value = sign * ratio ** (far - near).astype(np.float64) * lead(near) * trail(far, n) / denom(n)
    return np.where(inside, value, 0.0)


def line_table(n, start, size):
    row = start + np.arange(size)[:, None]
    col = start + np.arange(size)[None, :]
    entry = functools.partial(inverse_entry, row, n=n)
    first = entry(col - 1) - entry(col + 1)
    second = entry(col - 2) - entry(col + 2)
    return 7.0 / 9.0 * first + 1.0 / 36.0 * second


def split_table(table):
    high = table.astype(ml_dtypes.bfloat16)
    low = (table - high.astype(np.float64)).astype(ml_dtypes.bfloat16)
    return high, low


def edge_weights(n, start, size):
    last = start + size - 1
    j = start + np.arange(size)

    def forward(k):
        return np.where(k >= 0, (-ratio) ** (last - k).astype(np.float64) * lead(k), 0.0)

    def backward(k):
        return np.where(k <= n - 1, (-ratio) ** (k - start).astype(np.float64) * trail(k, n), 0.0)

    def weights(c):
        return 7.0 / 9.0 * (c(j - 1) - c(j + 1)) + 1.0 / 36.0 * (c(j - 2) - c(j + 2))

    return weights(forward), weights(backward)


def edge_columns(n, start, size):
    i = start + np.arange(size)
    left = (-ratio) ** (i - start + 1.0) * trail(i, n) / denom(n)
    right = (-ratio) ** (start + size - i).astype(np.float64) * lead(i) / denom(n)
    return left, right


def message_weights(n, start, size):
    count, block = n // size, start // size
    right, left = edge_weights(n, start, size)
    return np.stack([right if block < count - k else left for k in range(1, count)])


def message_shares(n, start, size):
    count, block = n // size, start // size
    decay = (-ratio) ** size
    left = [decay ** (k - 1) if block >= k else 0.0 for k in range(1, count)]
    right = [decay ** (count - k - 1) if block < k else 0.0 for k in range(1, count)]
    corner = [-1.0 / 12.0 if block > 0 else 0.0, 1.0 / 12.0 if block < count - 1 else 0.0]
    return np.array(left), np.array(right), np.array(corner)


def message_columns(n, start, size):
    left, right = edge_columns(n, start, size)
    share_left, share_right, corner = message_shares(n, start, size)
    corners = np.zeros((size, 2))
    corners[0, 0], corners[-1, 1] = corner
    return np.concatenate([np.outer(left, share_left) + np.outer(right, share_right), corners], axis=1)


def sweep_scalars(n, start, size):
    i = start + np.arange(size)
    after = start + size
    own_left = [0.0, 0.0]
    own_right = [0.0, 0.0]
    if start > 0:
        own_left = [7.0 / 9.0 * lead(start - 1) - ratio / 36.0 * lead(start - 2), lead(start - 1) / 36.0]
    if after < n:
        own_right = [
            -7.0 / 9.0 * trail(after, n) + ratio / 36.0 * trail(after + 1, n),
            -trail(after, n) / 36.0,
        ]
    rows = [lead(i) / 36.0, trail(i, n) / 36.0, lead(i) / denom(n), trail(i, n) / denom(n)]
    share_left, share_right, corner = message_shares(n, start, size)
    return np.concatenate(rows + [np.array(own_left + own_right), corner, share_left, share_right])


def per_block(make, n, count):
    size = n // count
    return np.stack([make(n, block * size, size) for block in range(count)])


def largest_divisor(size, most):
    return max(d for d in range(1, most + 1) if size % d == 0)


def message_forms(count):
    return [k in (1, count - 1) for k in range(1, count)]


def edge_kernel(info, y_weights, z_weights, *refs, y_count, z_count):
    step, steps = pl.program_id(0), pl.num_programs(0)
    y_refs, z_refs, outs = refs[:y_count], refs[y_count : y_count + z_count], refs[y_count + z_count :]
    chunk, yb, _ = (y_refs + z_refs)[0].shape[1:]
    ways = y_weights.shape[1] // 2 if y_refs else 0
    y_outs, z_outs = outs[:ways], outs[ways:]
    for field, ref in enumerate(y_refs):
        for z in range(chunk):
            sums = jnp.dot(y_weights[0], ref[0, z], preferred_element_type=f32)
            sums = sums[:ways] + sums[ways:]
            for k, out in enumerate(y_outs):
                out[field, 0, z, :] = sums[k]
                if out.shape[1] == 2:
                    edge = jnp.where(info[0] < ways - k, ref[0, z, yb - 1 :, :], ref[0, z, 0:1, :])
                    out[field, 1, z : z + 1, :] = edge.astype(f32)
    if not z_refs:
        return

    zb = z_weights.shape[1] // len(z_outs)
    for field, ref in enumerate(z_refs):
        for k, out in enumerate(z_outs):
            total = None
            for z in range(chunk):
                term = ref[0, z].astype(f32) * z_weights[info[1], k * zb + step * chunk + z]
                total = term if total is None else total + term

            @pl.when(step == 0)
            def _():
                out[field, 0] = total
                if out.shape[1] == 2:
                    out[field, 1] = ref[0, 0].astype(f32)

            @pl.when(step > 0)
            def _():
                out[field, 0] += total

            if out.shape[1] == 2:

                @pl.when((step == steps - 1) & (info[1] < len(z_outs) - k))
                def _():
                    out[field, 1] = ref[0, chunk - 1].astype(f32)


def edge_messages(info, velocity, y_weights, z_weights, y_fields, z_fields):
    _, zb, yb, nx = velocity.shape
    y_forms = message_forms(y_weights.shape[0]) if y_fields else []
    z_forms = message_forms(z_weights.shape[0]) if z_fields else []
    chunk = 8 if zb % 8 == 0 else zb
    fields = y_fields + z_fields
    in_y, in_z = len(y_fields), len(z_fields)
    piece = lambda f: pl.BlockSpec((1, chunk, yb, nx), lambda i, info: (f, i, 0, 0))
    y_spec = lambda near: pl.BlockSpec((in_y, 1 + near, chunk, nx), lambda i, info: (0, 0, i, 0))
    z_spec = lambda near: pl.BlockSpec((in_z, 1 + near, yb, nx), lambda i, info: (0, 0, 0, 0))
    outs = pl.pallas_call(
        functools.partial(edge_kernel, y_count=in_y, z_count=in_z),
        grid_spec=pltpu.PrefetchScalarGridSpec(
            num_scalar_prefetch=1,
            grid=(zb // chunk,),
            in_specs=[
                pl.BlockSpec((1,) + y_weights.shape[1:], lambda i, info: (info[0], 0, 0)),
                pl.BlockSpec(memory_space=pltpu.SMEM),
                *[piece(f) for f in fields],
            ],
            out_specs=[y_spec(near) for near in y_forms] + [z_spec(near) for near in z_forms],
        ),
        out_shape=[jax.ShapeDtypeStruct((in_y, 1 + near, zb, nx), f32) for near in y_forms]
        + [jax.ShapeDtypeStruct((in_z, 1 + near, yb, nx), f32) for near in z_forms],
        compiler_params=pltpu.CompilerParams(vmem_limit_bytes=VMEM_LIMIT),
        cost_estimate=light,
        name="edge_messages",
    )(info, y_weights, z_weights, *[velocity] * len(fields))
    return outs[: len(y_forms)], outs[len(y_forms) :]


def exchange(messages, axis):
    count = lax.axis_size(axis)
    out = []
    for k, message in enumerate(messages, 1):
        pairs = [(i, (i + k) % count) for i in range(count)]
        out.append(lax.ppermute(message, axis, pairs))
    return out


def slope_along_x(ref, tables, metric):
    chunk, yb, nx = ref.shape[1:]
    field = ref[0].reshape(chunk * yb, nx)
    high, low = tables
    slope = jnp.dot(field, high[...], preferred_element_type=f32)
    slope = slope + jnp.dot(field, low[...], preferred_element_type=f32)
    return (slope * metric[...]).reshape(chunk, yb, nx)


def slope_along_y(ref, z, table, columns, messages, metric):
    rows = table.shape[1] // 2
    both = jnp.dot(table[0], ref[0, z], preferred_element_type=f32)
    slope = both[:rows] + both[rows:]
    for k, message in enumerate(messages):
        slope = slope + columns[0, :, k : k + 1] * message[0, z : z + 1, :]
    last = len(messages)
    slope = slope + columns[0, :, last : last + 1] * messages[0][1, z : z + 1, :]
    slope = slope + columns[0, :, last + 1 : last + 2] * messages[-1][1, z : z + 1, :]
    return slope * metric[...]


def slopes_along_z(info, ref, scalars, messages, metric, out):
    _, zb, yb, nx = ref.shape
    rows, lanes = 16, 128
    across = nx // lanes
    block = info[1]
    last = len(messages)

    def tile(t, carry):
        ys = pl.ds(pl.multiple_of((t // across) * rows, rows), rows)
        xs = pl.ds(pl.multiple_of((t % across) * lanes, lanes), lanes)
        f = [ref[0, z, ys, xs].astype(f32) for z in range(zb)]
        scalar = lambda k: scalars[block, k]

        def rhs(z):
            near, far = [
                f[z + step] - f[z - step]
                if z + step < zb and z - step >= 0
                else (f[z + step] if z + step < zb else -f[z - step])
                for step in (1, 2)
            ]
            return near * 28.0 + far

        own = 4 * zb
        run = f[0] * scalar(own) + f[1] * scalar(own + 1)
        for k, message in enumerate(messages):
            run = run + message[0, 0, ys, xs] * scalar(own + 6 + k)
        forward = []
        sides = [rhs(z) for z in range(zb)]
        for z in range(zb):
            run = run * -ratio + sides[z] * scalar(z)
            forward.append(run)
        run = f[zb - 1] * scalar(own + 2) + f[zb - 2] * scalar(own + 3)
        for k, message in enumerate(messages):
            run = run + message[0, 0, ys, xs] * scalar(own + 6 + last + k)
        for z in reversed(range(zb)):
            run = run * -ratio
            scale = metric[block * zb + z]
            slope = forward[z] * (scalar(3 * zb + z) * scale) + run * (scalar(2 * zb + z) * scale)
            run = run + sides[z] * scalar(zb + z)
            if z == 0:
                slope = slope + messages[0][0, 1, ys, xs] * (scalar(own + 4) * scale)
            if z == zb - 1:
                slope = slope + messages[-1][0, 1, ys, xs] * (scalar(own + 5) * scale)
            out[z, ys, xs] = slope
        return carry

    lax.fori_loop(0, (yb // rows) * across, tile, 0)


def hand_out(info, spin, outs):
    parts, _, rows, lanes = outs[0].shape
    if len(outs) == 1 and parts == 1:
        outs[0][0] = spin[...]
        return
    for q, out in enumerate(outs):
        xs = pl.ds(pl.multiple_of(info[2 + parts + q] * lanes, lanes), lanes)
        for part in range(parts):
            ys = pl.ds(pl.multiple_of(info[2 + part] * rows, rows), rows)
            out[part] = spin[:, ys, xs]


def spin_z_kernel(info, ways, v_ref, high, low, metric_x, u_ref, table, columns, *rest):
    messages, (metric_y, *outs, spin) = rest[: ways[0]], rest[ways[0] :]
    slope_vx = slope_along_x(v_ref, (high, low), metric_x).astype(bf16)
    for z in range(u_ref.shape[1]):
        slope_uy = slope_along_y(u_ref, z, table, columns, messages, metric_y)
        spin[z] = (slope_vx[z].astype(f32) - slope_uy).astype(bf16)
    hand_out(info, spin, outs)


def spin_y_kernel(info, ways, w_ref, high, low, metric_x, u_ref, scalars, *rest):
    messages, (metric_z, *outs, spin, slopes) = rest[: ways[1]], rest[ways[1] :]
    step = pl.program_id(0)
    chunk = w_ref.shape[1]

    @pl.when(step == 0)
    def _():
        slopes_along_z(info, u_ref, scalars, messages, metric_z, slopes)

    slope_wx = slope_along_x(w_ref, (high, low), metric_x).astype(bf16)
    for z in range(chunk):
        spin[z] = (slopes[step * chunk + z] - slope_wx[z].astype(f32)).astype(bf16)
    hand_out(info, spin, outs)


def spin_x_kernel(info, ways, w_ref, table, columns, *rest):
    y_messages, (metric_y, v_ref, scalars, *rest) = rest[: ways[0]], rest[ways[0] :]
    messages, (metric_z, *outs, spin, slopes) = rest[: ways[1]], rest[ways[1] :]
    step = pl.program_id(0)
    chunk = w_ref.shape[1]

    @pl.when(step == 0)
    def _():
        slopes_along_z(info, v_ref, scalars, messages, metric_z, slopes)

    for z in range(chunk):
        slope_wy = slope_along_y(w_ref, z, table, columns, y_messages, metric_y).astype(bf16)
        spin[z] = (slope_wy.astype(f32) - slopes[step * chunk + z]).astype(bf16)
    hand_out(info, spin, outs)


def spin_call(kernel, info, velocity, groups, splits, flops, ways, name, cut=1):
    _, zb, yb, nx = velocity.shape
    row_parts, col_parts = splits
    rows = yb // cut
    chunk = largest_divisor(zb, 4 if cut == 1 else 8)
    specs, args, scratch = [], [], [pltpu.VMEM((chunk, rows, nx), bf16)]
    at_row = lambda info: info[info.shape[0] - 1] if cut > 1 else 0
    whole = lambda a: pl.BlockSpec(a.shape, lambda i, info: (0,) * a.ndim)
    mine = lambda a: pl.BlockSpec(
        (1,) + a.shape[1:], lambda i, info: (info[0] * cut + at_row(info),) + (0,) * (a.ndim - 1)
    )
    smem = pl.BlockSpec(memory_space=pltpu.SMEM)

    def add(spec, arg):
        specs.append(spec)
        args.append(arg)

    for kind, field, *more in groups:
        if kind == "z":
            scalars, place, messages, metric = more
            add(pl.BlockSpec((1, zb, yb, nx), lambda i, info, field=field: (field, 0, 0, 0)), velocity)
            add(smem, scalars)
            for message in messages:
                add(
                    pl.BlockSpec(
                        (1,) + message.shape[1:], lambda i, info, place=place: (place, 0, 0, 0)
                    ),
                    message,
                )
            add(smem, metric)
            scratch.append(pltpu.VMEM((zb, yb, nx), f32))
            continue
        if kind == "x":
            add(
                pl.BlockSpec(
                    (1, chunk, rows, nx), lambda i, info, field=field: (field, i, at_row(info), 0)
                ),
                velocity,
            )
            (high, low), metric = more
            add(whole(high), high)
            add(whole(low), low)
            add(whole(metric), metric)
        else:
            table, columns, place, messages, metric = more
            table = table.reshape(table.shape[0], 2, cut, rows, yb).swapaxes(1, 2)
            table = jnp.asarray(table.reshape(-1, 2 * rows, yb))
            columns = jnp.asarray(columns.reshape(-1, rows, columns.shape[2]), f32)
            add(pl.BlockSpec((1, chunk, yb, nx), lambda i, info, field=field: (field, i, 0, 0)), velocity)
            add(mine(table), table)
            add(mine(columns), columns)
            for message in messages:
                parts = message.shape[1]
                add(
                    pl.BlockSpec(
                        (None, parts, None, chunk, nx),
                        lambda i, info, place=place: (place, 0, i, 0, 0),
                    ),
                    message.reshape(2, parts, zb // chunk, chunk, nx),
                )
            add(pl.BlockSpec((rows, 1), lambda i, info: (info[0] * cut + at_row(info), 0)), metric)

    block = (rows // row_parts, nx // col_parts)
    out_spec = pl.BlockSpec((row_parts, None, chunk) + block, lambda i, info: (0, 0, i, 0, 0))
    return pl.pallas_call(
        lambda info, *refs: kernel(info, ways, *refs),
        grid_spec=pltpu.PrefetchScalarGridSpec(
            num_scalar_prefetch=1,
            grid=(zb // chunk,),
            in_specs=specs,
            out_specs=[out_spec] * col_parts,
            scratch_shapes=scratch,
        ),
        out_shape=[jax.ShapeDtypeStruct((row_parts, 1, zb) + block, bf16)] * col_parts,
        compiler_params=pltpu.CompilerParams(vmem_limit_bytes=VMEM_LIMIT),
        cost_estimate=light,
        name=name,
    )(info, *args)


def sketch_kernel(info, weights, *rest):
    count = weights.shape[0]
    fields = rest[:count]
    out = rest[-1]
    values = [field[...].astype(f32) for field in fields]
    for k in range(out.shape[0]):
        total = values[0] * weights[info[1], k]
        for r in range(1, count):
            total = total + values[r] * weights[info[1 + r], k]
        out[k] = total


def sketch_part(info, sketch_matrix, fields, total, component, shape):
    held, zb, rows, lanes = fields[0].shape
    rank = sketch_matrix.shape[1]
    chunk = largest_divisor(zb, 4)
    steps = zb // chunk
    piece = pl.BlockSpec((held, chunk, rows, lanes), lambda i, info: (0, i, 0, 0))
    specs = [pl.BlockSpec(memory_space=pltpu.SMEM)] + [piece] * len(fields)
    args = [sketch_matrix, *fields]
    aliases = {}
    if total is not None:
        specs.append(pl.BlockSpec(memory_space=pl.ANY))
        args.append(total)
        aliases = {len(args): 0}
    return pl.pallas_call(
        sketch_kernel,
        grid_spec=pltpu.PrefetchScalarGridSpec(
            num_scalar_prefetch=1,
            grid=(steps,),
            in_specs=specs,
            out_specs=pl.BlockSpec(
                (rank, held, chunk, rows, lanes),
                lambda i, info: (0, component // held, info[0] * steps + i, 0, 0),
            ),
        ),
        out_shape=jax.ShapeDtypeStruct(shape, f32),
        input_output_aliases=aliases,
        compiler_params=pltpu.CompilerParams(vmem_limit_bytes=VMEM_LIMIT),
        cost_estimate=light,
        name="sketch_part",
    )(info, *args)


def col_rank(c, count):
    return (c % 2) * (count // 2) + c // 2 if count % 2 == 0 else c


def col_of_rank(t, count):
    return (t % (count // 2)) * 2 + t // (count // 2) if count % 2 == 0 else t


def routes(snaps, cols, depth):
    out = []
    place = lambda s, y, z: (s * cols + y) * depth + z
    for shift in range(depth):
        for turn in range(cols):
            first, second = [], []
            for s in range(snaps):
                for p in range(cols):
                    for z in range(depth):
                        c = col_of_rank((p - turn - s) % cols, cols)
                        first.append((place(s, p, z), place(s, c, z)))
                        second.append((place(s, c, z), place(p, c, (z + shift) % depth)))
            out.append((first, second))
    return out


def after(x, *others):
    return lax.optimization_barrier((x, *others))[0]


def general_way(vorticity, sketch_matrix):
    lines = lax.all_to_all(vorticity, "py", split_axis=4, concat_axis=3, tiled=True)
    snap_count = lax.axis_size("snap")
    pz_count = lax.axis_size("pz")
    shape_now = lines.shape
    block_rows = shape_now[3] // (snap_count * pz_count)
    split_rows = lines.reshape(shape_now[:3] + (snap_count, pz_count, block_rows, shape_now[4]))
    reordered = jnp.swapaxes(split_rows, 3, 4).reshape(shape_now)
    lines = lax.all_to_all(reordered, "pz", split_axis=3, concat_axis=2, tiled=True)
    lines = lax.all_to_all(lines, "snap", split_axis=3, concat_axis=0, tiled=True)
    return jnp.einsum(
        "sk,sczyx->kczyx", sketch_matrix, lines.astype(f32), precision=lax.Precision.HIGHEST
    )


def on_device(velocity, metric_x, metric_y, metric_z, sketch_matrix):
    snaps, cols, depth = (lax.axis_size(name) for name in ("snap", "py", "pz"))
    s, p, z = (lax.axis_index(name) for name in ("snap", "py", "pz"))
    _, _, zb, yb, nx = velocity.shape
    ny, nz = yb * cols, zb * depth
    velocity = velocity[0]
    direct = snaps == cols

    tables_x = [jnp.asarray(t) for t in split_table(line_table(nx, 0, nx).T)]
    tables_y = per_block(line_table, ny, cols)
    tables_y = np.concatenate(split_table(tables_y), axis=1)
    columns_y = per_block(message_columns, ny, cols)
    weights_y = split_table(per_block(message_weights, ny, cols))
    weights_y = jnp.asarray(np.concatenate(weights_y, axis=1))
    weights_z = jnp.asarray(per_block(message_weights, nz, depth).reshape(depth, -1), f32)
    scalars_z = jnp.asarray(per_block(sweep_scalars, nz, depth), f32)
    metric_x = metric_x.reshape(1, nx)
    metric_y = metric_y.reshape(ny, 1)

    rows_to = [(z + shift) % depth for shift in range(depth)]
    cols_to = [col_of_rank((p - turn - s) % cols, cols) for turn in range(cols)]
    pack = lambda *items: jnp.stack(items).astype(jnp.int32)
    info = pack(p, z, *rows_to, *cols_to) if direct else pack(p, z)

    weights = (weights_y, weights_z)
    y_sums, _ = edge_messages(info, velocity, *weights, (0, 2), ())
    y_edges = exchange(y_sums, "py")
    _, z_sums = edge_messages(after(info, y_sums[0]), velocity, *weights, (), (0, 1))
    z_edges = exchange(z_sums, "pz")

    points = zb * yb * nx
    along_x = lambda field: ("x", field, tables_x, metric_x)
    along_y = lambda field, place: ("y", field, tables_y, columns_y, place, y_edges, metric_y)
    along_z = lambda field: ("z", field, scalars_z, field, z_edges, metric_z)
    splits = (depth, cols) if direct else (1, 1)
    call = functools.partial(spin_call, ways=(cols - 1, depth - 1))
    spin_z = []
    ready = z_sums[0]
    for shift in range(depth if direct else 1):
        here = pack(p, z, 0 * z, *cols_to, rows_to[shift]) if direct else info
        spin_z += call(
            spin_z_kernel,
            after(here, ready),
            velocity,
            [along_x(1), along_y(0, 0)],
            splits=(1, cols) if direct else (1, 1),
            flops=points * 4 * (nx + yb) // (depth if direct else 1),
            name="spin_z",
            cut=depth if direct else 1,
        )

    def spin_y(info):
        return call(
            spin_y_kernel, info, velocity, [along_x(2), along_z(0)],
            flops=points * (4 * nx + 20), name="spin_y", splits=splits,
        )

    def spin_x(info):
        return call(
            spin_x_kernel, info, velocity, [along_y(2, 1), along_z(1)],
            flops=points * (4 * yb + 20), name="spin_x", splits=splits,
        )

    if not direct:
        vorticity = jnp.concatenate([spin_x(info)[0][0], spin_y(info)[0][0], spin_z[0][0]])[None]
        return general_way(vorticity, sketch_matrix)

    all_routes = routes(snaps, cols, depth)
    arrived = {}

    def travel(name, route, hop, sent, *behind):
        if behind:
            sent = after(sent, *behind)
        arrived[name] = lax.ppermute(sent, ("snap", "py", "pz"), all_routes[route][hop])

    turns = range(cols)
    count = depth * cols
    for i in range(count):
        travel(("z", i), i, 0, spin_z[i], *[arrived["z", j] for j in range(i - cols, i - cols + 1) if j >= 0])
    y_parts = spin_y(after(info, *[arrived["z", i] for i in range(count)]))
    x_parts = spin_x(info)
    for i in range(count):
        behind = [arrived["z", cols + i] if i < cols else arrived["z", "to", i - cols]]
        if i == cols:
            behind.append(y_parts[0])
        if i == cols + 1:
            behind.append(x_parts[0])
        travel(("z", "to", i), i, 1, arrived["z", i][0], *behind)
    for t in turns:
        travel(("y", t), t, 0, y_parts[t], arrived["z", "to", t])
    for t in turns:
        travel(("x", t), t, 0, x_parts[t], arrived["y", t], arrived["z", "to", count - cols + t])

    shape = (sketch_matrix.shape[1], 3, nz, yb // depth, nx // cols)
    my_rank = col_rank(p, cols)

    def add_sketch(total, names, shift, component):
        whence = [(z - shift) % depth]
        whence += [(s - turn - my_rank) % snaps for turn in turns]
        fields = [arrived[name] for name in names]
        return sketch_part(pack(*whence), sketch_matrix, fields, total, component, shape)

    total = None
    for shift in range(depth):
        names = [("z", "to", shift * cols + t) for t in turns]
        total = add_sketch(total, names, shift, 2)
    ahead = [("z", "to", count - cols + t) for t in turns]
    plan = [("y", 0, 1)] + [("xy", shift, 0) for shift in range(1, depth)] + [("x", 0, 0)]
    for kind, shift, component in plan:
        names = [(kind, "to", shift, t) for t in turns]
        for t in turns:
            pieces = [arrived[one, t][shift] for one in kind]
            sent = jnp.concatenate(pieces) if len(pieces) > 1 else pieces[0]
            travel(names[t], shift * cols + t, 1, sent, arrived[ahead[t]])
        total = add_sketch(total, names, shift, component)
        ahead = names
    return total


def solution(mesh):
    placed = (P("snap", None, "pz", "py", None), P(), P(), P(), P())
    return jax.shard_map(
        on_device,
        mesh=mesh,
        in_specs=placed,
        out_specs=P(None, None, None, ("snap", "pz"), "py"),
        check_vma=False,
    )
```

```python
import functools

import jax
import jax.numpy as jnp
import ml_dtypes
import numpy as np
from jax import lax
from jax.experimental import pallas as pl
from jax.experimental.pallas import tpu as pltpu
from jax.sharding import PartitionSpec as P

ratio = (3.0 - 5.0**0.5) / 2.0
VMEM_LIMIT = 52 * 1024 * 1024
light = pl.CostEstimate(flops=1024, bytes_accessed=1024, transcendentals=0)
f32 = jnp.float32
bf16 = jnp.bfloat16


def lead(i):
    return 1.0 - ratio ** (2.0 * (np.asarray(i, np.float64) + 1.0))


def trail(i, n):
    return 1.0 - ratio ** (2.0 * (n - np.asarray(i, np.float64)))


def denom(n):
    return 5.0**0.5 / 3.0 * (1.0 - ratio ** (2.0 * (n + 1.0)))


def inverse_entry(row, col, n):
    inside = (col >= 0) & (col < n)
    col = np.clip(col, 0, n - 1)
    near, far = np.minimum(row, col), np.maximum(row, col)
    sign = 1.0 - 2.0 * ((far - near) % 2)
    value = sign * ratio ** (far - near).astype(np.float64) * lead(near) * trail(far, n) / denom(n)
    return np.where(inside, value, 0.0)


def line_table(n, start, size):
    row = start + np.arange(size)[:, None]
    col = start + np.arange(size)[None, :]
    entry = functools.partial(inverse_entry, row, n=n)
    first = entry(col - 1) - entry(col + 1)
    second = entry(col - 2) - entry(col + 2)
    return 7.0 / 9.0 * first + 1.0 / 36.0 * second


def split_table(table):
    high = table.astype(ml_dtypes.bfloat16)
    low = (table - high.astype(np.float64)).astype(ml_dtypes.bfloat16)
    return high, low


def edge_weights(n, start, size):
    last = start + size - 1
    j = start + np.arange(size)

    def forward(k):
        return np.where(k >= 0, (-ratio) ** (last - k).astype(np.float64) * lead(k), 0.0)

    def backward(k):
        return np.where(k <= n - 1, (-ratio) ** (k - start).astype(np.float64) * trail(k, n), 0.0)

    def weights(c):
        return 7.0 / 9.0 * (c(j - 1) - c(j + 1)) + 1.0 / 36.0 * (c(j - 2) - c(j + 2))

    return weights(forward), weights(backward)


def edge_columns(n, start, size):
    i = start + np.arange(size)
    left = (-ratio) ** (i - start + 1.0) * trail(i, n) / denom(n)
    right = (-ratio) ** (start + size - i).astype(np.float64) * lead(i) / denom(n)
    return left, right


def message_weights(n, start, size):
    count, block = n // size, start // size
    right, left = edge_weights(n, start, size)
    return np.stack([right if block < count - k else left for k in range(1, count)])


def message_shares(n, start, size):
    count, block = n // size, start // size
    decay = (-ratio) ** size
    left = [decay ** (k - 1) if block >= k else 0.0 for k in range(1, count)]
    right = [decay ** (count - k - 1) if block < k else 0.0 for k in range(1, count)]
    corner = [-1.0 / 12.0 if block > 0 else 0.0, 1.0 / 12.0 if block < count - 1 else 0.0]
    return np.array(left), np.array(right), np.array(corner)


def message_columns(n, start, size):
    left, right = edge_columns(n, start, size)
    share_left, share_right, corner = message_shares(n, start, size)
    corners = np.zeros((size, 2))
    corners[0, 0], corners[-1, 1] = corner
    return np.concatenate([np.outer(left, share_left) + np.outer(right, share_right), corners], axis=1)


def sweep_scalars(n, start, size):
    i = start + np.arange(size)
    after = start + size
    own_left = [0.0, 0.0]
    own_right = [0.0, 0.0]
    if start > 0:
        own_left = [7.0 / 9.0 * lead(start - 1) - ratio / 36.0 * lead(start - 2), lead(start - 1) / 36.0]
    if after < n:
        own_right = [
            -7.0 / 9.0 * trail(after, n) + ratio / 36.0 * trail(after + 1, n),
            -trail(after, n) / 36.0,
        ]
    rows = [lead(i) / 36.0, trail(i, n) / 36.0, lead(i) / denom(n), trail(i, n) / denom(n)]
    share_left, share_right, corner = message_shares(n, start, size)
    return np.concatenate(rows + [np.array(own_left + own_right), corner, share_left, share_right])


def per_block(make, n, count):
    size = n // count
    return np.stack([make(n, block * size, size) for block in range(count)])


def largest_divisor(size, most):
    return max(d for d in range(1, most + 1) if size % d == 0)


def message_forms(count):
    return [k in (1, count - 1) for k in range(1, count)]


def edge_kernel(info, y_weights, z_weights, *refs, y_count, z_count):
    step, steps = pl.program_id(0), pl.num_programs(0)
    y_refs, z_refs, outs = refs[:y_count], refs[y_count : y_count + z_count], refs[y_count + z_count :]
    chunk, yb, _ = (y_refs + z_refs)[0].shape[1:]
    ways = y_weights.shape[1] // 2 if y_refs else 0
    y_outs, z_outs = outs[:ways], outs[ways:]
    for field, ref in enumerate(y_refs):
        for z in range(chunk):
            sums = jnp.dot(y_weights[0], ref[0, z], preferred_element_type=f32)
            sums = sums[:ways] + sums[ways:]
            for k, out in enumerate(y_outs):
                out[field, 0, z, :] = sums[k]
                if out.shape[1] == 2:
                    edge = jnp.where(info[0] < ways - k, ref[0, z, yb - 1 :, :], ref[0, z, 0:1, :])
                    out[field, 1, z : z + 1, :] = edge.astype(f32)
    if not z_refs:
        return

    zb = z_weights.shape[1] // len(z_outs)
    for field, ref in enumerate(z_refs):
        for k, out in enumerate(z_outs):
            total = None
            for z in range(chunk):
                term = ref[0, z].astype(f32) * z_weights[info[1], k * zb + step * chunk + z]
                total = term if total is None else total + term

            @pl.when(step == 0)
            def _():
                out[field, 0] = total
                if out.shape[1] == 2:
                    out[field, 1] = ref[0, 0].astype(f32)

            @pl.when(step > 0)
            def _():
                out[field, 0] += total

            if out.shape[1] == 2:

                @pl.when((step == steps - 1) & (info[1] < len(z_outs) - k))
                def _():
                    out[field, 1] = ref[0, chunk - 1].astype(f32)


def edge_messages(info, velocity, y_weights, z_weights, y_fields, z_fields):
    _, zb, yb, nx = velocity.shape
    y_forms = message_forms(y_weights.shape[0]) if y_fields else []
    z_forms = message_forms(z_weights.shape[0]) if z_fields else []
    chunk = 8 if zb % 8 == 0 else zb
    fields = y_fields + z_fields
    in_y, in_z = len(y_fields), len(z_fields)
    piece = lambda f: pl.BlockSpec((1, chunk, yb, nx), lambda i, info: (f, i, 0, 0))
    y_spec = lambda near: pl.BlockSpec((in_y, 1 + near, chunk, nx), lambda i, info: (0, 0, i, 0))
    z_spec = lambda near: pl.BlockSpec((in_z, 1 + near, yb, nx), lambda i, info: (0, 0, 0, 0))
    outs = pl.pallas_call(
        functools.partial(edge_kernel, y_count=in_y, z_count=in_z),
        grid_spec=pltpu.PrefetchScalarGridSpec(
            num_scalar_prefetch=1,
            grid=(zb // chunk,),
            in_specs=[
                pl.BlockSpec((1,) + y_weights.shape[1:], lambda i, info: (info[0], 0, 0)),
                pl.BlockSpec(memory_space=pltpu.SMEM),
                *[piece(f) for f in fields],
            ],
            out_specs=[y_spec(near) for near in y_forms] + [z_spec(near) for near in z_forms],
        ),
        out_shape=[jax.ShapeDtypeStruct((in_y, 1 + near, zb, nx), f32) for near in y_forms]
        + [jax.ShapeDtypeStruct((in_z, 1 + near, yb, nx), f32) for near in z_forms],
        compiler_params=pltpu.CompilerParams(vmem_limit_bytes=VMEM_LIMIT),
        cost_estimate=light,
        name="edge_messages",
    )(info, y_weights, z_weights, *[velocity] * len(fields))
    return outs[: len(y_forms)], outs[len(y_forms) :]


def exchange(messages, axis):
    count = lax.axis_size(axis)
    out = []
    for k, message in enumerate(messages, 1):
        pairs = [(i, (i + k) % count) for i in range(count)]
        out.append(lax.ppermute(message, axis, pairs))
    return out


def slope_along_x(ref, tables, metric):
    chunk, yb, nx = ref.shape[1:]
    field = ref[0].reshape(chunk * yb, nx)
    high, low = tables
    slope = jnp.dot(field, high[...], preferred_element_type=f32)
    slope = slope + jnp.dot(field, low[...], preferred_element_type=f32)
    return (slope * metric[...]).reshape(chunk, yb, nx)


def slope_along_y(ref, z, table, columns, messages, metric):
    rows = table.shape[1] // 2
    both = jnp.dot(table[0], ref[0, z], preferred_element_type=f32)
    slope = both[:rows] + both[rows:]
    for k, message in enumerate(messages):
        slope = slope + columns[0, :, k : k + 1] * message[0, z : z + 1, :]
    last = len(messages)
    slope = slope + columns[0, :, last : last + 1] * messages[0][1, z : z + 1, :]
    slope = slope + columns[0, :, last + 1 : last + 2] * messages[-1][1, z : z + 1, :]
    return slope * metric[...]


def slopes_along_z(info, ref, scalars, messages, metric, out):
    _, zb, yb, nx = ref.shape
    rows, lanes = 16, 128
    across = nx // lanes
    block = info[1]
    last = len(messages)

    def tile(t, carry):
        ys = pl.ds(pl.multiple_of((t // across) * rows, rows), rows)
        xs = pl.ds(pl.multiple_of((t % across) * lanes, lanes), lanes)
        f = [ref[0, z, ys, xs].astype(f32) for z in range(zb)]
        scalar = lambda k: scalars[block, k]

        def rhs(z):
            near, far = [
                f[z + step] - f[z - step]
                if z + step < zb and z - step >= 0
                else (f[z + step] if z + step < zb else -f[z - step])
                for step in (1, 2)
            ]
            return near * 28.0 + far

        own = 4 * zb
        run = f[0] * scalar(own) + f[1] * scalar(own + 1)
        for k, message in enumerate(messages):
            run = run + message[0, 0, ys, xs] * scalar(own + 6 + k)
        forward = []
        sides = [rhs(z) for z in range(zb)]
        for z in range(zb):
            run = run * -ratio + sides[z] * scalar(z)
            forward.append(run)
        run = f[zb - 1] * scalar(own + 2) + f[zb - 2] * scalar(own + 3)
        for k, message in enumerate(messages):
            run = run + message[0, 0, ys, xs] * scalar(own + 6 + last + k)
        for z in reversed(range(zb)):
            run = run * -ratio
            scale = metric[block * zb + z]
            slope = forward[z] * (scalar(3 * zb + z) * scale) + run * (scalar(2 * zb + z) * scale)
            run = run + sides[z] * scalar(zb + z)
            if z == 0:
                slope = slope + messages[0][0, 1, ys, xs] * (scalar(own + 4) * scale)
            if z == zb - 1:
                slope = slope + messages[-1][0, 1, ys, xs] * (scalar(own + 5) * scale)
            out[z, ys, xs] = slope
        return carry

    lax.fori_loop(0, (yb // rows) * across, tile, 0)


def hand_out(info, spin, outs):
    parts, _, rows, lanes = outs[0].shape
    if len(outs) == 1 and parts == 1:
        outs[0][0] = spin[...]
        return
    for q, out in enumerate(outs):
        xs = pl.ds(pl.multiple_of(info[2 + parts + q] * lanes, lanes), lanes)
        for part in range(parts):
            ys = pl.ds(pl.multiple_of(info[2 + part] * rows, rows), rows)
            out[part] = spin[:, ys, xs]


def spin_z_kernel(info, ways, v_ref, high, low, metric_x, u_ref, table, columns, *rest):
    messages, (metric_y, *outs, spin) = rest[: ways[0]], rest[ways[0] :]
    slope_vx = slope_along_x(v_ref, (high, low), metric_x).astype(bf16)
    for z in range(u_ref.shape[1]):
        slope_uy = slope_along_y(u_ref, z, table, columns, messages, metric_y)
        spin[z] = (slope_vx[z].astype(f32) - slope_uy).astype(bf16)
    hand_out(info, spin, outs)


def spin_y_kernel(info, ways, w_ref, high, low, metric_x, u_ref, scalars, *rest):
    messages, (metric_z, *outs, spin, slopes) = rest[: ways[1]], rest[ways[1] :]
    step = pl.program_id(0)
    chunk = w_ref.shape[1]

    @pl.when(step == 0)
    def _():
        slopes_along_z(info, u_ref, scalars, messages, metric_z, slopes)

    slope_wx = slope_along_x(w_ref, (high, low), metric_x).astype(bf16)
    for z in range(chunk):
        spin[z] = (slopes[step * chunk + z] - slope_wx[z].astype(f32)).astype(bf16)
    hand_out(info, spin, outs)


def spin_x_kernel(info, ways, w_ref, table, columns, *rest):
    y_messages, (metric_y, v_ref, scalars, *rest) = rest[: ways[0]], rest[ways[0] :]
    messages, (metric_z, *rest, spin, slopes) = rest[: ways[1]], rest[ways[1] :]
    outs = rest[len(rest) // 2 :]
    step = pl.program_id(0)
    chunk = w_ref.shape[1]

    @pl.when(step == 0)
    def _():
        slopes_along_z(info, v_ref, scalars, messages, metric_z, slopes)

    for z in range(chunk):
        slope_wy = slope_along_y(w_ref, z, table, columns, y_messages, metric_y).astype(bf16)
        spin[z] = (slope_wy.astype(f32) - slopes[step * chunk + z]).astype(bf16)
    hand_out(info, spin, outs)


def spin_call(kernel, info, velocity, groups, splits, flops, ways, name, slot=(0, 1), into=(), cut=1):
    _, zb, yb, nx = velocity.shape
    row_parts, col_parts = splits
    rows = yb // cut
    chunk = largest_divisor(zb, 4 if cut == 1 else 8)
    specs, args, scratch = [], [], [pltpu.VMEM((chunk, rows, nx), bf16)]
    at_row = lambda info: info[info.shape[0] - 1] if cut > 1 else 0
    whole = lambda a: pl.BlockSpec(a.shape, lambda i, info: (0,) * a.ndim)
    mine = lambda a: pl.BlockSpec(
        (1,) + a.shape[1:], lambda i, info: (info[0] * cut + at_row(info),) + (0,) * (a.ndim - 1)
    )
    smem = pl.BlockSpec(memory_space=pltpu.SMEM)

    def add(spec, arg):
        specs.append(spec)
        args.append(arg)

    for kind, field, *more in groups:
        if kind == "z":
            scalars, place, messages, metric = more
            add(pl.BlockSpec((1, zb, yb, nx), lambda i, info, field=field: (field, 0, 0, 0)), velocity)
            add(smem, scalars)
            for message in messages:
                add(
                    pl.BlockSpec(
                        (1,) + message.shape[1:], lambda i, info, place=place: (place, 0, 0, 0)
                    ),
                    message,
                )
            add(smem, metric)
            scratch.append(pltpu.VMEM((zb, yb, nx), f32))
            continue
        if kind == "x":
            add(
                pl.BlockSpec(
                    (1, chunk, rows, nx), lambda i, info, field=field: (field, i, at_row(info), 0)
                ),
                velocity,
            )
            (high, low), metric = more
            add(whole(high), high)
            add(whole(low), low)
            add(whole(metric), metric)
        else:
            table, columns, place, messages, metric = more
            table = table.reshape(table.shape[0], 2, cut, rows, yb).swapaxes(1, 2)
            table = jnp.asarray(table.reshape(-1, 2 * rows, yb))
            columns = jnp.asarray(columns.reshape(-1, rows, columns.shape[2]), f32)
            add(pl.BlockSpec((1, chunk, yb, nx), lambda i, info, field=field: (field, i, 0, 0)), velocity)
            add(mine(table), table)
            add(mine(columns), columns)
            for message in messages:
                parts = message.shape[1]
                add(
                    pl.BlockSpec(
                        (None, parts, None, chunk, nx),
                        lambda i, info, place=place: (place, 0, i, 0, 0),
                    ),
                    message.reshape(2, parts, zb // chunk, chunk, nx),
                )
            add(pl.BlockSpec((rows, 1), lambda i, info: (info[0] * cut + at_row(info), 0)), metric)

    block = (rows // row_parts, nx // col_parts)
    at, held = slot
    aliases = {}
    for q, buffer in enumerate(into):
        add(pl.BlockSpec(memory_space=pl.ANY), buffer)
        aliases[len(args)] = q
    out_spec = pl.BlockSpec((row_parts, None, chunk) + block, lambda i, info: (0, at, i, 0, 0))
    return pl.pallas_call(
        lambda info, *refs: kernel(info, ways, *refs),
        grid_spec=pltpu.PrefetchScalarGridSpec(
            num_scalar_prefetch=1,
            grid=(zb // chunk,),
            in_specs=specs,
            out_specs=[out_spec] * col_parts,
            scratch_shapes=scratch,
        ),
        out_shape=[jax.ShapeDtypeStruct((row_parts, held, zb) + block, bf16)] * col_parts,
        input_output_aliases=aliases,
        compiler_params=pltpu.CompilerParams(vmem_limit_bytes=VMEM_LIMIT),
        cost_estimate=light,
        name=name,
    )(info, *args)


def sketch_kernel(info, weights, *rest):
    count = weights.shape[0]
    fields = rest[:count]
    out = rest[-1]
    values = [field[...].astype(f32) for field in fields]
    for k in range(out.shape[0]):
        total = values[0] * weights[info[1], k]
        for r in range(1, count):
            total = total + values[r] * weights[info[1 + r], k]
        out[k] = total


def sketch_part(info, sketch_matrix, fields, total, component, shape):
    held, zb, rows, lanes = fields[0].shape
    rank = sketch_matrix.shape[1]
    chunk = largest_divisor(zb, 4)
    steps = zb // chunk
    piece = pl.BlockSpec((held, chunk, rows, lanes), lambda i, info: (0, i, 0, 0))
    specs = [pl.BlockSpec(memory_space=pltpu.SMEM)] + [piece] * len(fields)
    args = [sketch_matrix, *fields]
    aliases = {}
    if total is not None:
        specs.append(pl.BlockSpec(memory_space=pl.ANY))
        args.append(total)
        aliases = {len(args): 0}
    return pl.pallas_call(
        sketch_kernel,
        grid_spec=pltpu.PrefetchScalarGridSpec(
            num_scalar_prefetch=1,
            grid=(steps,),
            in_specs=specs,
            out_specs=pl.BlockSpec(
                (rank, held, chunk, rows, lanes),
                lambda i, info: (0, component // held, info[0] * steps + i, 0, 0),
            ),
        ),
        out_shape=jax.ShapeDtypeStruct(shape, f32),
        input_output_aliases=aliases,
        compiler_params=pltpu.CompilerParams(vmem_limit_bytes=VMEM_LIMIT),
        cost_estimate=light,
        name="sketch_part",
    )(info, *args)


def col_rank(c, count):
    return (c % 2) * (count // 2) + c // 2 if count % 2 == 0 else c


def col_of_rank(t, count):
    return (t % (count // 2)) * 2 + t // (count // 2) if count % 2 == 0 else t


def routes(snaps, cols, depth):
    out = []
    place = lambda s, y, z: (s * cols + y) * depth + z
    for shift in range(depth):
        for turn in range(cols):
            first, second = [], []
            for s in range(snaps):
                for p in range(cols):
                    for z in range(depth):
                        c = col_of_rank((p - turn - s) % cols, cols)
                        first.append((place(s, p, z), place(s, c, z)))
                        second.append((place(s, c, z), place(p, c, (z + shift) % depth)))
            out.append((first, second))
    return out


def after(x, *others):
    return lax.optimization_barrier((x, *others))[0]


def general_way(vorticity, sketch_matrix):
    lines = lax.all_to_all(vorticity, "py", split_axis=4, concat_axis=3, tiled=True)
    snap_count = lax.axis_size("snap")
    pz_count = lax.axis_size("pz")
    shape_now = lines.shape
    block_rows = shape_now[3] // (snap_count * pz_count)
    split_rows = lines.reshape(shape_now[:3] + (snap_count, pz_count, block_rows, shape_now[4]))
    reordered = jnp.swapaxes(split_rows, 3, 4).reshape(shape_now)
    lines = lax.all_to_all(reordered, "pz", split_axis=3, concat_axis=2, tiled=True)
    lines = lax.all_to_all(lines, "snap", split_axis=3, concat_axis=0, tiled=True)
    return jnp.einsum(
        "sk,sczyx->kczyx", sketch_matrix, lines.astype(f32), precision=lax.Precision.HIGHEST
    )


def on_device(velocity, metric_x, metric_y, metric_z, sketch_matrix):
    snaps, cols, depth = (lax.axis_size(name) for name in ("snap", "py", "pz"))
    s, p, z = (lax.axis_index(name) for name in ("snap", "py", "pz"))
    _, _, zb, yb, nx = velocity.shape
    ny, nz = yb * cols, zb * depth
    velocity = velocity[0]
    direct = snaps == cols

    tables_x = [jnp.asarray(t) for t in split_table(line_table(nx, 0, nx).T)]
    tables_y = per_block(line_table, ny, cols)
    tables_y = np.concatenate(split_table(tables_y), axis=1)
    columns_y = per_block(message_columns, ny, cols)
    weights_y = split_table(per_block(message_weights, ny, cols))
    weights_y = jnp.asarray(np.concatenate(weights_y, axis=1))
    weights_z = jnp.asarray(per_block(message_weights, nz, depth).reshape(depth, -1), f32)
    scalars_z = jnp.asarray(per_block(sweep_scalars, nz, depth), f32)
    metric_x = metric_x.reshape(1, nx)
    metric_y = metric_y.reshape(ny, 1)

    rows_to = [(z + shift) % depth for shift in range(depth)]
    cols_to = [col_of_rank((p - turn - s) % cols, cols) for turn in range(cols)]
    pack = lambda *items: jnp.stack(items).astype(jnp.int32)
    info = pack(p, z, *rows_to, *cols_to) if direct else pack(p, z)

    weights = (weights_y, weights_z)
    y_sums, _ = edge_messages(info, velocity, *weights, (0, 2), ())
    y_edges = exchange(y_sums, "py")
    _, z_sums = edge_messages(after(info, y_sums[0]), velocity, *weights, (), (0, 1))
    z_edges = exchange(z_sums, "pz")

    points = zb * yb * nx
    along_x = lambda field: ("x", field, tables_x, metric_x)
    along_y = lambda field, place: ("y", field, tables_y, columns_y, place, y_edges, metric_y)
    along_z = lambda field: ("z", field, scalars_z, field, z_edges, metric_z)
    splits = (depth, cols) if direct else (1, 1)
    call = functools.partial(spin_call, ways=(cols - 1, depth - 1))
    spin_z = []
    ready = z_sums[0]
    for shift in range(depth if direct else 1):
        here = pack(p, z, 0 * z, *cols_to, rows_to[shift]) if direct else info
        spin_z += call(
            spin_z_kernel,
            after(here, ready),
            velocity,
            [along_x(1), along_y(0, 0)],
            splits=(1, cols) if direct else (1, 1),
            flops=points * 4 * (nx + yb) // (depth if direct else 1),
            name="spin_z",
            cut=depth if direct else 1,
        )
    def with_spin_y(info):
        return call(
            spin_y_kernel, info, velocity, [along_x(2), along_z(0)],
            flops=points * (4 * nx + 20), name="spin_y", slot=(1, 2), splits=splits,
        )

    def with_spin_x(pair, info):
        return call(
            spin_x_kernel, info, velocity, [along_y(2, 1), along_z(1)],
            flops=points * (4 * yb + 20), name="spin_x", slot=(0, 2), into=pair, splits=splits,
        )

    if not direct:
        pair = with_spin_x(with_spin_y(info), info)
        vorticity = jnp.concatenate([pair[0][0], spin_z[0][0]])[None]
        return general_way(vorticity, sketch_matrix)

    all_routes = routes(snaps, cols, depth)
    everywhere = ("snap", "py", "pz")
    count = len(all_routes)
    arrived = {}

    def travel(hop, i, sent, *behind):
        behind = [arrived[b] if isinstance(b, tuple) else b for b in behind]
        if behind:
            sent = after(sent, *behind)
        arrived[hop, i] = lax.ppermute(sent, everywhere, all_routes[i % count][hop])

    line = [(0, i) for i in range(count)] + [(1, i) for i in range(cols)]
    spin_y_at = len(line)
    line += [(1, i) for i in range(cols, count)]
    spin_x_at = spin_y_at + 1
    line += [(0, count + turn) for turn in range(cols)]
    line += [(1, i) for i in range(count, 2 * count)]
    pair = None
    for at, (hop, i) in enumerate(line):
        behind = [line[at - 4]] if at >= 4 else []
        if at == spin_y_at:
            pair = with_spin_y(after(info, *[arrived[0, i] for i in range(count)]))
            behind.append(pair[0])
        if at == spin_x_at:
            pair = with_spin_x(pair, info)
            behind.append(pair[0])
        if hop == 0:
            sent = spin_z[i] if i < count else pair[i - count]
        elif i < count:
            sent = arrived[0, i][0]
        else:
            sent = arrived[0, count + i % cols][(i - count) // cols]
        travel(hop, i, sent, *behind)

    shape = (sketch_matrix.shape[1], 3, nz, yb // depth, nx // cols)
    my_rank = col_rank(p, cols)
    total = None
    for place, component in enumerate((2, 0)):
        for shift in range(depth):
            whence = [(z - shift) % depth]
            whence += [(s - turn - my_rank) % snaps for turn in range(cols)]
            begin = place * count + shift * cols
            total = sketch_part(
                jnp.stack(whence).astype(jnp.int32),
                sketch_matrix,
                [arrived[1, i] for i in range(begin, begin + cols)],
                total,
                component,
                shape,
            )
    return total


def solution(mesh):
    placed = (P("snap", None, "pz", "py", None), P(), P(), P(), P())
    return jax.shard_map(
        on_device,
        mesh=mesh,
        in_specs=placed,
        out_specs=P(None, None, None, ("snap", "pz"), "py"),
        check_vma=False,
    )
```

```python
import functools

import jax
import jax.numpy as jnp
import ml_dtypes
import numpy as np
from jax import lax
from jax.experimental import pallas as pl
from jax.experimental.pallas import tpu as pltpu
from jax.sharding import PartitionSpec as P

ratio = (3.0 - 5.0**0.5) / 2.0
VMEM_LIMIT = 52 * 1024 * 1024
light = pl.CostEstimate(flops=1024, bytes_accessed=1024, transcendentals=0)
f32 = jnp.float32
bf16 = jnp.bfloat16


def lead(i):
    return 1.0 - ratio ** (2.0 * (np.asarray(i, np.float64) + 1.0))


def trail(i, n):
    return 1.0 - ratio ** (2.0 * (n - np.asarray(i, np.float64)))


def denom(n):
    return 5.0**0.5 / 3.0 * (1.0 - ratio ** (2.0 * (n + 1.0)))


def inverse_entry(row, col, n):
    inside = (col >= 0) & (col < n)
    col = np.clip(col, 0, n - 1)
    near, far = np.minimum(row, col), np.maximum(row, col)
    sign = 1.0 - 2.0 * ((far - near) % 2)
    value = sign * ratio ** (far - near).astype(np.float64) * lead(near) * trail(far, n) / denom(n)
    return np.where(inside, value, 0.0)


def line_table(n, start, size):
    row = start + np.arange(size)[:, None]
    col = start + np.arange(size)[None, :]
    entry = functools.partial(inverse_entry, row, n=n)
    first = entry(col - 1) - entry(col + 1)
    second = entry(col - 2) - entry(col + 2)
    return 7.0 / 9.0 * first + 1.0 / 36.0 * second


def split_table(table):
    high = table.astype(ml_dtypes.bfloat16)
    low = (table - high.astype(np.float64)).astype(ml_dtypes.bfloat16)
    return high, low


def edge_weights(n, start, size):
    last = start + size - 1
    j = start + np.arange(size)

    def forward(k):
        return np.where(k >= 0, (-ratio) ** (last - k).astype(np.float64) * lead(k), 0.0)

    def backward(k):
        return np.where(k <= n - 1, (-ratio) ** (k - start).astype(np.float64) * trail(k, n), 0.0)

    def weights(c):
        return 7.0 / 9.0 * (c(j - 1) - c(j + 1)) + 1.0 / 36.0 * (c(j - 2) - c(j + 2))

    return weights(forward), weights(backward)


def edge_columns(n, start, size):
    i = start + np.arange(size)
    left = (-ratio) ** (i - start + 1.0) * trail(i, n) / denom(n)
    right = (-ratio) ** (start + size - i).astype(np.float64) * lead(i) / denom(n)
    return left, right


def message_weights(n, start, size):
    count, block = n // size, start // size
    right, left = edge_weights(n, start, size)
    return np.stack([right if block < count - k else left for k in range(1, count)])


def message_shares(n, start, size):
    count, block = n // size, start // size
    decay = (-ratio) ** size
    left = [decay ** (k - 1) if block >= k else 0.0 for k in range(1, count)]
    right = [decay ** (count - k - 1) if block < k else 0.0 for k in range(1, count)]
    corner = [-1.0 / 12.0 if block > 0 else 0.0, 1.0 / 12.0 if block < count - 1 else 0.0]
    return np.array(left), np.array(right), np.array(corner)


def message_columns(n, start, size):
    left, right = edge_columns(n, start, size)
    share_left, share_right, corner = message_shares(n, start, size)
    corners = np.zeros((size, 2))
    corners[0, 0], corners[-1, 1] = corner
    return np.concatenate([np.outer(left, share_left) + np.outer(right, share_right), corners], axis=1)


def sweep_scalars(n, start, size):
    i = start + np.arange(size)
    after = start + size
    own_left = [0.0, 0.0]
    own_right = [0.0, 0.0]
    if start > 0:
        own_left = [7.0 / 9.0 * lead(start - 1) - ratio / 36.0 * lead(start - 2), lead(start - 1) / 36.0]
    if after < n:
        own_right = [
            -7.0 / 9.0 * trail(after, n) + ratio / 36.0 * trail(after + 1, n),
            -trail(after, n) / 36.0,
        ]
    rows = [lead(i) / 36.0, trail(i, n) / 36.0, lead(i) / denom(n), trail(i, n) / denom(n)]
    share_left, share_right, corner = message_shares(n, start, size)
    return np.concatenate(rows + [np.array(own_left + own_right), corner, share_left, share_right])


def per_block(make, n, count):
    size = n // count
    return np.stack([make(n, block * size, size) for block in range(count)])


def largest_divisor(size, most):
    return max(d for d in range(1, most + 1) if size % d == 0)


def message_forms(count):
    return [k in (1, count - 1) for k in range(1, count)]


def edge_kernel(info, y_weights, z_weights, *refs, y_count, z_count):
    step, steps = pl.program_id(0), pl.num_programs(0)
    y_refs, z_refs, outs = refs[:y_count], refs[y_count : y_count + z_count], refs[y_count + z_count :]
    chunk, yb, _ = (y_refs + z_refs)[0].shape[1:]
    ways = y_weights.shape[1] // 2 if y_refs else 0
    y_outs, z_outs = outs[:ways], outs[ways:]
    for field, ref in enumerate(y_refs):
        for z in range(chunk):
            sums = jnp.dot(y_weights[0], ref[0, z], preferred_element_type=f32)
            sums = sums[:ways] + sums[ways:]
            for k, out in enumerate(y_outs):
                out[field, 0, z, :] = sums[k]
                if out.shape[1] == 2:
                    edge = jnp.where(info[0] < ways - k, ref[0, z, yb - 1 :, :], ref[0, z, 0:1, :])
                    out[field, 1, z : z + 1, :] = edge.astype(f32)
    if not z_refs:
        return

    zb = z_weights.shape[1] // len(z_outs)
    for field, ref in enumerate(z_refs):
        for k, out in enumerate(z_outs):
            total = None
            for z in range(chunk):
                term = ref[0, z].astype(f32) * z_weights[info[1], k * zb + step * chunk + z]
                total = term if total is None else total + term

            @pl.when(step == 0)
            def _():
                out[field, 0] = total
                if out.shape[1] == 2:
                    out[field, 1] = ref[0, 0].astype(f32)

            @pl.when(step > 0)
            def _():
                out[field, 0] += total

            if out.shape[1] == 2:

                @pl.when((step == steps - 1) & (info[1] < len(z_outs) - k))
                def _():
                    out[field, 1] = ref[0, chunk - 1].astype(f32)


def edge_messages(info, velocity, y_weights, z_weights, y_fields, z_fields):
    _, zb, yb, nx = velocity.shape
    y_forms = message_forms(y_weights.shape[0]) if y_fields else []
    z_forms = message_forms(z_weights.shape[0]) if z_fields else []
    chunk = 8 if zb % 8 == 0 else zb
    fields = y_fields + z_fields
    in_y, in_z = len(y_fields), len(z_fields)
    piece = lambda f: pl.BlockSpec((1, chunk, yb, nx), lambda i, info: (f, i, 0, 0))
    y_spec = lambda near: pl.BlockSpec((in_y, 1 + near, chunk, nx), lambda i, info: (0, 0, i, 0))
    z_spec = lambda near: pl.BlockSpec((in_z, 1 + near, yb, nx), lambda i, info: (0, 0, 0, 0))
    outs = pl.pallas_call(
        functools.partial(edge_kernel, y_count=in_y, z_count=in_z),
        grid_spec=pltpu.PrefetchScalarGridSpec(
            num_scalar_prefetch=1,
            grid=(zb // chunk,),
            in_specs=[
                pl.BlockSpec((1,) + y_weights.shape[1:], lambda i, info: (info[0], 0, 0)),
                pl.BlockSpec(memory_space=pltpu.SMEM),
                *[piece(f) for f in fields],
            ],
            out_specs=[y_spec(near) for near in y_forms] + [z_spec(near) for near in z_forms],
        ),
        out_shape=[jax.ShapeDtypeStruct((in_y, 1 + near, zb, nx), f32) for near in y_forms]
        + [jax.ShapeDtypeStruct((in_z, 1 + near, yb, nx), f32) for near in z_forms],
        compiler_params=pltpu.CompilerParams(vmem_limit_bytes=VMEM_LIMIT),
        cost_estimate=light,
        name="edge_messages",
    )(info, y_weights, z_weights, *[velocity] * len(fields))
    return outs[: len(y_forms)], outs[len(y_forms) :]


def exchange(messages, axis):
    count = lax.axis_size(axis)
    out = []
    for k, message in enumerate(messages, 1):
        pairs = [(i, (i + k) % count) for i in range(count)]
        out.append(lax.ppermute(message, axis, pairs))
    return out


def slope_along_x(ref, tables, metric):
    chunk, yb, nx = ref.shape[1:]
    field = ref[0].reshape(chunk * yb, nx)
    high, low = tables
    slope = jnp.dot(field, high[...], preferred_element_type=f32)
    slope = slope + jnp.dot(field, low[...], preferred_element_type=f32)
    return (slope * metric[...]).reshape(chunk, yb, nx)


def slope_along_y(ref, z, table, columns, messages, metric):
    rows = table.shape[1] // 2
    both = jnp.dot(table[0], ref[0, z], preferred_element_type=f32)
    slope = both[:rows] + both[rows:]
    for k, message in enumerate(messages):
        slope = slope + columns[0, :, k : k + 1] * message[0, z : z + 1, :]
    last = len(messages)
    slope = slope + columns[0, :, last : last + 1] * messages[0][1, z : z + 1, :]
    slope = slope + columns[0, :, last + 1 : last + 2] * messages[-1][1, z : z + 1, :]
    return slope * metric[...]


def slopes_along_z(info, ref, scalars, messages, metric, out):
    _, zb, yb, nx = ref.shape
    rows, lanes = 16, 128
    across = nx // lanes
    block = info[1]
    last = len(messages)

    def tile(t, carry):
        ys = pl.ds(pl.multiple_of((t // across) * rows, rows), rows)
        xs = pl.ds(pl.multiple_of((t % across) * lanes, lanes), lanes)
        f = [ref[0, z, ys, xs].astype(f32) for z in range(zb)]
        scalar = lambda k: scalars[block, k]

        def rhs(z):
            near, far = [
                f[z + step] - f[z - step]
                if z + step < zb and z - step >= 0
                else (f[z + step] if z + step < zb else -f[z - step])
                for step in (1, 2)
            ]
            return near * 28.0 + far

        own = 4 * zb
        run = f[0] * scalar(own) + f[1] * scalar(own + 1)
        for k, message in enumerate(messages):
            run = run + message[0, 0, ys, xs] * scalar(own + 6 + k)
        forward = []
        sides = [rhs(z) for z in range(zb)]
        for z in range(zb):
            run = run * -ratio + sides[z] * scalar(z)
            forward.append(run)
        run = f[zb - 1] * scalar(own + 2) + f[zb - 2] * scalar(own + 3)
        for k, message in enumerate(messages):
            run = run + message[0, 0, ys, xs] * scalar(own + 6 + last + k)
        for z in reversed(range(zb)):
            run = run * -ratio
            scale = metric[block * zb + z]
            slope = forward[z] * (scalar(3 * zb + z) * scale) + run * (scalar(2 * zb + z) * scale)
            run = run + sides[z] * scalar(zb + z)
            if z == 0:
                slope = slope + messages[0][0, 1, ys, xs] * (scalar(own + 4) * scale)
            if z == zb - 1:
                slope = slope + messages[-1][0, 1, ys, xs] * (scalar(own + 5) * scale)
            out[z, ys, xs] = slope
        return carry

    lax.fori_loop(0, (yb // rows) * across, tile, 0)


def hand_out(info, spin, outs):
    parts, _, rows, lanes = outs[0].shape
    if len(outs) == 1 and parts == 1:
        outs[0][0] = spin[...]
        return
    for q, out in enumerate(outs):
        xs = pl.ds(pl.multiple_of(info[2 + parts + q] * lanes, lanes), lanes)
        for part in range(parts):
            ys = pl.ds(pl.multiple_of(info[2 + part] * rows, rows), rows)
            out[part] = spin[:, ys, xs]


def spin_z_kernel(info, ways, v_ref, high, low, metric_x, u_ref, table, columns, *rest):
    messages, (metric_y, *outs, spin) = rest[: ways[0]], rest[ways[0] :]
    slope_vx = slope_along_x(v_ref, (high, low), metric_x).astype(bf16)
    for z in range(u_ref.shape[1]):
        slope_uy = slope_along_y(u_ref, z, table, columns, messages, metric_y)
        spin[z] = (slope_vx[z].astype(f32) - slope_uy).astype(bf16)
    hand_out(info, spin, outs)


def spin_y_kernel(info, ways, w_ref, high, low, metric_x, u_ref, scalars, *rest):
    messages, (metric_z, *outs, spin, slopes) = rest[: ways[1]], rest[ways[1] :]
    step = pl.program_id(0)
    chunk = w_ref.shape[1]

    @pl.when(step == 0)
    def _():
        slopes_along_z(info, u_ref, scalars, messages, metric_z, slopes)

    slope_wx = slope_along_x(w_ref, (high, low), metric_x).astype(bf16)
    for z in range(chunk):
        spin[z] = (slopes[step * chunk + z] - slope_wx[z].astype(f32)).astype(bf16)
    hand_out(info, spin, outs)


def spin_x_kernel(info, ways, w_ref, table, columns, *rest):
    y_messages, (metric_y, v_ref, scalars, *rest) = rest[: ways[0]], rest[ways[0] :]
    messages, (metric_z, *rest, spin, slopes) = rest[: ways[1]], rest[ways[1] :]
    outs = rest[len(rest) // 2 :]
    step = pl.program_id(0)
    chunk = w_ref.shape[1]

    @pl.when(step == 0)
    def _():
        slopes_along_z(info, v_ref, scalars, messages, metric_z, slopes)

    for z in range(chunk):
        slope_wy = slope_along_y(w_ref, z, table, columns, y_messages, metric_y).astype(bf16)
        spin[z] = (slope_wy.astype(f32) - slopes[step * chunk + z]).astype(bf16)
    hand_out(info, spin, outs)


def spin_call(kernel, info, velocity, groups, splits, flops, ways, name, slot=(0, 1), into=(), cut=1):
    _, zb, yb, nx = velocity.shape
    row_parts, col_parts = splits
    rows = yb // cut
    chunk = largest_divisor(zb, 4 if cut == 1 else 8)
    specs, args, scratch = [], [], [pltpu.VMEM((chunk, rows, nx), bf16)]
    at_row = lambda info: info[info.shape[0] - 1] if cut > 1 else 0
    whole = lambda a: pl.BlockSpec(a.shape, lambda i, info: (0,) * a.ndim)
    mine = lambda a: pl.BlockSpec(
        (1,) + a.shape[1:], lambda i, info: (info[0] * cut + at_row(info),) + (0,) * (a.ndim - 1)
    )
    smem = pl.BlockSpec(memory_space=pltpu.SMEM)

    def add(spec, arg):
        specs.append(spec)
        args.append(arg)

    for kind, field, *more in groups:
        if kind == "z":
            scalars, place, messages, metric = more
            add(pl.BlockSpec((1, zb, yb, nx), lambda i, info, field=field: (field, 0, 0, 0)), velocity)
            add(smem, scalars)
            for message in messages:
                add(
                    pl.BlockSpec(
                        (1,) + message.shape[1:], lambda i, info, place=place: (place, 0, 0, 0)
                    ),
                    message,
                )
            add(smem, metric)
            scratch.append(pltpu.VMEM((zb, yb, nx), f32))
            continue
        if kind == "x":
            add(
                pl.BlockSpec(
                    (1, chunk, rows, nx), lambda i, info, field=field: (field, i, at_row(info), 0)
                ),
                velocity,
            )
            (high, low), metric = more
            add(whole(high), high)
            add(whole(low), low)
            add(whole(metric), metric)
        else:
            table, columns, place, messages, metric = more
            table = table.reshape(table.shape[0], 2, cut, rows, yb).swapaxes(1, 2)
            table = jnp.asarray(table.reshape(-1, 2 * rows, yb))
            columns = jnp.asarray(columns.reshape(-1, rows, columns.shape[2]), f32)
            add(pl.BlockSpec((1, chunk, yb, nx), lambda i, info, field=field: (field, i, 0, 0)), velocity)
            add(mine(table), table)
            add(mine(columns), columns)
            for message in messages:
                parts = message.shape[1]
                add(
                    pl.BlockSpec(
                        (None, parts, None, chunk, nx),
                        lambda i, info, place=place: (place, 0, i, 0, 0),
                    ),
                    message.reshape(2, parts, zb // chunk, chunk, nx),
                )
            add(pl.BlockSpec((rows, 1), lambda i, info: (info[0] * cut + at_row(info), 0)), metric)

    block = (rows // row_parts, nx // col_parts)
    at, held = slot
    aliases = {}
    for q, buffer in enumerate(into):
        add(pl.BlockSpec(memory_space=pl.ANY), buffer)
        aliases[len(args)] = q
    out_spec = pl.BlockSpec((row_parts, None, chunk) + block, lambda i, info: (0, at, i, 0, 0))
    return pl.pallas_call(
        lambda info, *refs: kernel(info, ways, *refs),
        grid_spec=pltpu.PrefetchScalarGridSpec(
            num_scalar_prefetch=1,
            grid=(zb // chunk,),
            in_specs=specs,
            out_specs=[out_spec] * col_parts,
            scratch_shapes=scratch,
        ),
        out_shape=[jax.ShapeDtypeStruct((row_parts, held, zb) + block, bf16)] * col_parts,
        input_output_aliases=aliases,
        compiler_params=pltpu.CompilerParams(vmem_limit_bytes=VMEM_LIMIT),
        cost_estimate=light,
        name=name,
    )(info, *args)


def sketch_kernel(info, weights, *rest):
    count = weights.shape[0]
    fields = rest[:count]
    out = rest[-1]
    values = [field[...].astype(f32) for field in fields]
    for k in range(out.shape[0]):
        total = values[0] * weights[info[1], k]
        for r in range(1, count):
            total = total + values[r] * weights[info[1 + r], k]
        out[k] = total


def sketch_part(info, sketch_matrix, fields, total, component, shape):
    held, zb, rows, lanes = fields[0].shape
    rank = sketch_matrix.shape[1]
    chunk = largest_divisor(zb, 4)
    steps = zb // chunk
    piece = pl.BlockSpec((held, chunk, rows, lanes), lambda i, info: (0, i, 0, 0))
    specs = [pl.BlockSpec(memory_space=pltpu.SMEM)] + [piece] * len(fields)
    args = [sketch_matrix, *fields]
    aliases = {}
    if total is not None:
        specs.append(pl.BlockSpec(memory_space=pl.ANY))
        args.append(total)
        aliases = {len(args): 0}
    return pl.pallas_call(
        sketch_kernel,
        grid_spec=pltpu.PrefetchScalarGridSpec(
            num_scalar_prefetch=1,
            grid=(steps,),
            in_specs=specs,
            out_specs=pl.BlockSpec(
                (rank, held, chunk, rows, lanes),
                lambda i, info: (0, component // held, info[0] * steps + i, 0, 0),
            ),
        ),
        out_shape=jax.ShapeDtypeStruct(shape, f32),
        input_output_aliases=aliases,
        compiler_params=pltpu.CompilerParams(vmem_limit_bytes=VMEM_LIMIT),
        cost_estimate=light,
        name="sketch_part",
    )(info, *args)


def col_rank(c, count):
    return (c % 2) * (count // 2) + c // 2 if count % 2 == 0 else c


def col_of_rank(t, count):
    return (t % (count // 2)) * 2 + t // (count // 2) if count % 2 == 0 else t


def routes(snaps, cols, depth):
    out = []
    place = lambda s, y, z: (s * cols + y) * depth + z
    for shift in range(depth):
        for turn in range(cols):
            first, second = [], []
            for s in range(snaps):
                for p in range(cols):
                    for z in range(depth):
                        c = col_of_rank((p - turn - s) % cols, cols)
                        first.append((place(s, p, z), place(s, c, z)))
                        second.append((place(s, c, z), place(p, c, (z + shift) % depth)))
            out.append((first, second))
    return out


def after(x, *others):
    return lax.optimization_barrier((x, *others))[0]


def general_way(vorticity, sketch_matrix):
    lines = lax.all_to_all(vorticity, "py", split_axis=4, concat_axis=3, tiled=True)
    snap_count = lax.axis_size("snap")
    pz_count = lax.axis_size("pz")
    shape_now = lines.shape
    block_rows = shape_now[3] // (snap_count * pz_count)
    split_rows = lines.reshape(shape_now[:3] + (snap_count, pz_count, block_rows, shape_now[4]))
    reordered = jnp.swapaxes(split_rows, 3, 4).reshape(shape_now)
    lines = lax.all_to_all(reordered, "pz", split_axis=3, concat_axis=2, tiled=True)
    lines = lax.all_to_all(lines, "snap", split_axis=3, concat_axis=0, tiled=True)
    return jnp.einsum(
        "sk,sczyx->kczyx", sketch_matrix, lines.astype(f32), precision=lax.Precision.HIGHEST
    )


def on_device(velocity, metric_x, metric_y, metric_z, sketch_matrix):
    snaps, cols, depth = (lax.axis_size(name) for name in ("snap", "py", "pz"))
    s, p, z = (lax.axis_index(name) for name in ("snap", "py", "pz"))
    _, _, zb, yb, nx = velocity.shape
    ny, nz = yb * cols, zb * depth
    velocity = velocity[0]
    direct = snaps == cols

    tables_x = [jnp.asarray(t) for t in split_table(line_table(nx, 0, nx).T)]
    tables_y = per_block(line_table, ny, cols)
    tables_y = np.concatenate(split_table(tables_y), axis=1)
    columns_y = per_block(message_columns, ny, cols)
    weights_y = split_table(per_block(message_weights, ny, cols))
    weights_y = jnp.asarray(np.concatenate(weights_y, axis=1))
    weights_z = jnp.asarray(per_block(message_weights, nz, depth).reshape(depth, -1), f32)
    scalars_z = jnp.asarray(per_block(sweep_scalars, nz, depth), f32)
    metric_x = metric_x.reshape(1, nx)
    metric_y = metric_y.reshape(ny, 1)

    rows_to = [(z + shift) % depth for shift in range(depth)]
    cols_to = [col_of_rank((p - turn - s) % cols, cols) for turn in range(cols)]
    pack = lambda *items: jnp.stack(items).astype(jnp.int32)
    info = pack(p, z, *rows_to, *cols_to) if direct else pack(p, z)

    weights = (weights_y, weights_z)
    y_sums, _ = edge_messages(info, velocity, *weights, (0, 2), ())
    y_edges = exchange(y_sums, "py")
    _, z_sums = edge_messages(after(info, y_sums[0]), velocity, *weights, (), (0, 1))
    z_edges = exchange(z_sums, "pz")

    points = zb * yb * nx
    along_x = lambda field: ("x", field, tables_x, metric_x)
    along_y = lambda field, place: ("y", field, tables_y, columns_y, place, y_edges, metric_y)
    along_z = lambda field: ("z", field, scalars_z, field, z_edges, metric_z)
    splits = (depth, cols) if direct else (1, 1)
    call = functools.partial(spin_call, ways=(cols - 1, depth - 1))
    spin_z = []
    ready = z_sums[0]
    for shift in range(depth if direct else 1):
        here = pack(p, z, 0 * z, *cols_to, rows_to[shift]) if direct else info
        spin_z += call(
            spin_z_kernel,
            after(here, ready),
            velocity,
            [along_x(1), along_y(0, 0)],
            splits=(1, cols) if direct else (1, 1),
            flops=points * 4 * (nx + yb) // (depth if direct else 1),
            name="spin_z",
            cut=depth if direct else 1,
        )
    def with_spin_y(info):
        return call(
            spin_y_kernel, info, velocity, [along_x(2), along_z(0)],
            flops=points * (4 * nx + 20), name="spin_y", slot=(1, 2), splits=splits,
        )

    def with_spin_x(pair, info):
        return call(
            spin_x_kernel, info, velocity, [along_y(2, 1), along_z(1)],
            flops=points * (4 * yb + 20), name="spin_x", slot=(0, 2), into=pair, splits=splits,
        )

    if not direct:
        pair = with_spin_x(with_spin_y(info), info)
        vorticity = jnp.concatenate([pair[0][0], spin_z[0][0]])[None]
        return general_way(vorticity, sketch_matrix)

    all_routes = routes(snaps, cols, depth)
    everywhere = ("snap", "py", "pz")
    count = len(all_routes)
    arrived = {}

    def travel(hop, i, sent, *behind):
        behind = [arrived[b] if isinstance(b, tuple) else b for b in behind]
        if behind:
            sent = after(sent, *behind)
        arrived[hop, i] = lax.ppermute(sent, everywhere, all_routes[i % count][hop])

    line = [(0, i) for i in range(cols)]
    for i in range(cols):
        line += [(1, i), (0, cols + i)]
    line += [(0, i) for i in range(2 * cols, count)]
    spin_y_at = len(line)
    line += [(1, i) for i in range(cols, count)]
    spin_x_at = spin_y_at + 1
    line += [(0, count + turn) for turn in range(cols)]
    line += [(1, i) for i in range(count, 2 * count)]
    pair = None
    for at, (hop, i) in enumerate(line):
        behind = [line[at - 4]] if at >= 4 else []
        if at == spin_y_at:
            pair = with_spin_y(after(info, *[arrived[0, i] for i in range(count)]))
            behind.append(pair[0])
        if at == spin_x_at:
            pair = with_spin_x(pair, info)
            behind.append(pair[0])
        if hop == 0:
            sent = spin_z[i] if i < count else pair[i - count]
        elif i < count:
            sent = arrived[0, i][0]
        else:
            sent = arrived[0, count + i % cols][(i - count) // cols]
        travel(hop, i, sent, *behind)

    shape = (sketch_matrix.shape[1], 3, nz, yb // depth, nx // cols)
    my_rank = col_rank(p, cols)
    total = None
    for place, component in enumerate((2, 0)):
        for shift in range(depth):
            whence = [(z - shift) % depth]
            whence += [(s - turn - my_rank) % snaps for turn in range(cols)]
            begin = place * count + shift * cols
            total = sketch_part(
                jnp.stack(whence).astype(jnp.int32),
                sketch_matrix,
                [arrived[1, i] for i in range(begin, begin + cols)],
                total,
                component,
                shape,
            )
    return total


def solution(mesh):
    placed = (P("snap", None, "pz", "py", None), P(), P(), P(), P())
    return jax.shard_map(
        on_device,
        mesh=mesh,
        in_specs=placed,
        out_specs=P(None, None, None, ("snap", "pz"), "py"),
        check_vma=False,
    )
```
